32 devices in a mesh: gx: 4 (over y, core), gy: 8 (over z, x).
Axes of the slice: x: 2, y: 2, z: 4, core: 2. Of those that a mesh axis runs over, the one named last changes fastest.
Arguments:
- first_lame: float32 [256, 4096], P('gx', 'gy'), may hold values from 1 to 10
- shear_modulus: float32 [256, 4096], P('gx', 'gy'), may hold values from 1 to 10
- applied_load: float32 [2, 256, 4096], P(None, 'gx', 'gy'), may hold values from -12 to 12
- plastic_owner: int32 [16384, 1], P(('gx', 'gy')), may hold values from 0 to 31; in each aligned block of 512 rows (0 to 511, 512 to 1023, ...) at most 32 rows name the same one
- plastic_cell: int32 [16384], P(('gx', 'gy')), may hold values from 0 to 32767
- plastic_code: int32 [16384], P(('gx', 'gy')), may hold values from 0 to 3
Outputs:
- displacement: float32 [2, 256, 4096], P(None, 'gx', 'gy')
The draws below stay inside these ranges and needn't reach their ends.
Inputs may be any that keep to these rules, and one draw needn't show every extreme that they name: `plastic_owner`: owners are numbered row-major over (gx, gy). In each aligned block of 512 entries (the list of one device) no owner is named more than 32 times, a bound that some block reaches. `plastic_cell`: Row-major position within the owner's 64 x 512 block; a cell may be listed several times. `plastic_code`: code 0 marks a padding entry. An entry's owner, cell and code may travel together as one number, ((owner * 64 * 512) + cell) * 4 + code.
All inputs are finite; a program needn't handle non-finite values.
Results may differ from the reference program's by a relative error of at most 0.00011.
Values sent between devices are 32-bit elements; how exact they have to be, the bound alone decides.
No kernel may reach another device: no remote copies, remote signals or barrier semaphores. Data moves between devices by JAX's collectives and lax.ppermute only.
A program may use at most 128 MiB of HBM per device.

```python
import math
import jax
import jax.numpy as jnp
import numpy as np
from jax import lax

CX = 64
CY = 512
BLK = 512
CAP = 32
LEVELS = 3
SWEEPS = 2
COARSE_SWEEPS = 6
NX = 256
NY = 4096
N_GY = 8
DEVICES = 32


def set_ends(drawn, stream_key, low, top_value):
    shape = drawn.shape
    spot = [jax.random.randint(jax.random.fold_in(stream_key, axis), (), 0, shape[axis]) for axis in range(len(shape))]
    drawn = drawn.at[tuple(spot)].set(low)
    longest = shape.index(max(shape))
    spot[longest] = (spot[longest] + 1) % shape[longest]
    return drawn.at[tuple(spot)].set(top_value)


def steps_of(key, shape, shards, low, top_value):
    def one(position, shards_of):
        steps = jax.random.uniform(jax.random.fold_in(jax.random.fold_in(key, 6), position), (shards_of,), jnp.float32, low / len(shards), top_value / len(shards))
        return jnp.repeat(jnp.exp(steps), shape[position] // shards_of).reshape((-1,) + (1,) * (len(shape) - position - 1))

    gain = one(*shards[0])
    for cut in shards[1:]:
        gain = gain * one(*cut)
    return gain


def assign_block(rng, own, number, rows, amount, top, most, skew):
    ranking = jax.random.permutation(rng, amount)
    heavy_load, common = portions_of(amount, rows * top, most, skew, True), portions_of(amount, rows * top, most, skew, False)
    places = jnp.arange(amount)

    def named(sizes, offset_by):
        used = int((sizes > 0).sum())
        fixed = max(1, used // 4)
        shifted = fixed + (places - fixed + offset_by * (used - fixed)) % max(1, amount - fixed)
        return jnp.zeros((amount,), jnp.int32).at[ranking[jnp.where(places < fixed, places, shifted)]].set(jnp.asarray(sizes, jnp.int32))

    sizes = jnp.where(number % 4 == 0, named(heavy_load, number // 4), named(common, number - number // 4 - 1))
    mixed = jax.random.permutation(jax.random.fold_in(own, 3), amount)
    giver, sink = mixed[0:amount // 2 * 2:2], mixed[1:amount // 2 * 2:2]
    margin = jnp.minimum(sizes[giver] - 1, most - sizes[sink]) // 2
    margin = jnp.where((giver == ranking[0]) | (sink == ranking[0]) | (sizes[sink] == 0), 0, jnp.maximum(margin, 0))
    shifted = jax.random.randint(jax.random.fold_in(own, 4), (amount // 2,), 0, 1 << 20) % (margin + 1)
    sizes = sizes.at[giver].add(-shifted).at[sink].add(shifted)
    labels = jnp.searchsorted(jnp.cumsum(sizes), jnp.arange(rows * top), side="right").astype(jnp.int32)
    table = labels.reshape(top, rows).T
    table = table[jax.random.permutation(jax.random.fold_in(own, 1), rows)]
    offset_by = jax.random.randint(jax.random.fold_in(own, 2), (rows, 1), 0, top)
    return jnp.take_along_axis(table, (jnp.arange(top)[None, :] + offset_by) % top, axis=1)


def portions_of(amount, total, reach, lean, full):
    portions = [(1 << 20) // math.isqrt(standing ** lean) + 1 for standing in range(1, amount + 1)]
    largest = reach if full else min(reach, max(-(-total // amount), total * portions[0] // sum(portions)))
    least = 1 if total - largest >= amount - 1 else 0
    given, surplus = [largest] + [least] * (amount - 1), total - largest - least * (amount - 1)
    while surplus > 0:
        candidates = [i for i in range(1, amount) if given[i] < largest] or [i for i in range(1, amount) if given[i] < reach]
        mass, budget = sum([portions[i] for i in candidates]), surplus
        for i in candidates:
            extra = min(reach - given[i], max(1, budget * portions[i] // mass), surplus)
            given[i] = given[i] + extra
            surplus = surplus - extra
    return np.array(given)


def gaussian(rng, extent, width, most, cuts=(), dtype=jnp.bfloat16):
    gain = steps_of(rng, extent, cuts, -0.22, 0.18) if cuts else 1.0
    drawn = jax.random.normal(rng, extent, jnp.float32) * width * gain
    return jnp.minimum(jnp.maximum(drawn, -most), most).astype(dtype)


def setup_inputs(seed: int = 0) -> dict:
    seeds = jax.random.split(jax.random.key(seed), 7)
    first_lame = jnp.clip(jnp.exp(math.log(10.0) - 2.3025851 * jax.random.uniform(seeds[0], (NX, NY), jnp.float32) ** steps_of(seeds[0], (NX, NY), ((0, 4), (1, 8)), -0.2, 0.2)), 1.0, 10.0)
    shear_modulus = jnp.clip(jnp.exp(math.log(10.0) - 2.3025851 * jax.random.uniform(seeds[1], (NX, NY), jnp.float32) ** steps_of(seeds[1], (NX, NY), ((0, 4), (1, 8)), -0.2, 0.2)), 1.0, 10.0)
    applied_load = gaussian(seeds[2], (2, NX, NY), 2.0, 12.0, ((1, 4), (2, 8)), jnp.float32)
    plastic_owner_keys = jax.random.split(jax.random.fold_in(seeds[3], 1), (DEVICES * BLK) // BLK)
    plastic_owner_turns = jax.random.permutation(jax.random.fold_in(seeds[3], 3), (DEVICES * BLK) // BLK)
    plastic_owner = jax.vmap(lambda own, number: assign_block(jax.random.fold_in(seeds[3], 2), own, number, BLK, DEVICES, 1, CAP, 2))(plastic_owner_keys, plastic_owner_turns).reshape((DEVICES * BLK, 1))
    plastic_cell = set_ends(jax.random.randint(seeds[4], (DEVICES * BLK,), 0, CX * CY), jax.random.fold_in(seeds[4], 1), 0, (CX * CY) - 1).astype(jnp.int32)
    plastic_code = set_ends(jax.random.randint(seeds[5], (DEVICES * BLK,), 0, 4), jax.random.fold_in(seeds[5], 1), 0, 3).astype(jnp.int32)
    return {"first_lame": first_lame, "shear_modulus": shear_modulus, "applied_load": applied_load, "plastic_owner": plastic_owner, "plastic_cell": plastic_cell, "plastic_code": plastic_code}


DAMPING = 0.5
YIELD_DROP = 0.6
HIGHEST = lax.Precision.HIGHEST
ELEMENT_NODES = ((0, 0), (1, 0), (0, 1), (1, 1))

def element_tables():
    gauss_points = (0.5 - 0.5 / math.sqrt(3.0), 0.5 + 0.5 / math.sqrt(3.0))
    scale_rows = np.array([2.0, 2.0, 1.0])
    volumetric = np.zeros((8, 8))
    deviatoric = np.zeros((8, 8))
    for coord_row in gauss_points:
        for coord_col in gauss_points:
            strain = np.zeros((3, 8))
            for corner, (row_step, col_step) in enumerate(ELEMENT_NODES):
                shape_row = coord_row if row_step else 1.0 - coord_row
                shape_col = coord_col if col_step else 1.0 - coord_col
                slope_row = (1.0 if row_step else -1.0) * shape_col
                slope_col = (1.0 if col_step else -1.0) * shape_row
                strain[0, 2 * corner] = slope_row
                strain[1, 2 * corner + 1] = slope_col
                strain[2, 2 * corner] = slope_col
                strain[2, 2 * corner + 1] = slope_row
            trace_row = strain[0] + strain[1]
            volumetric = volumetric + 0.25 * np.outer(trace_row, trace_row)
            deviatoric = deviatoric + 0.25 * np.dot(strain.T, scale_rows[:, None] * strain)
    first_map = np.zeros((64, 8))
    second_map = np.zeros((64, 256))
    for sub_row in (0, 1):
        for sub_col in (0, 1):
            interp = np.zeros((8, 8))
            for corner, (row_step, col_step) in enumerate(ELEMENT_NODES):
                place_row = 0.5 * (sub_row + row_step)
                place_col = 0.5 * (sub_col + col_step)
                for source_corner, (src_row, src_col) in enumerate(ELEMENT_NODES):
                    weight = (place_row if src_row else 1.0 - place_row) * (place_col if src_col else 1.0 - place_col)
                    interp[2 * corner, 2 * source_corner] = weight
                    interp[2 * corner + 1, 2 * source_corner + 1] = weight
            subcell = sub_row * 2 + sub_col
            first_map[:, 2 * subcell] = np.dot(interp.T, np.dot(volumetric, interp)).reshape(64)
            first_map[:, 2 * subcell + 1] = np.dot(interp.T, np.dot(deviatoric, interp)).reshape(64)
            paired = np.outer(interp.T, interp.T).reshape(8, 8, 8, 8).transpose(0, 2, 1, 3)
            second_map[:, 64 * subcell:64 * subcell + 64] = paired.reshape(64, 64)
    return (jnp.asarray(volumetric, jnp.float32), jnp.asarray(deviatoric, jnp.float32), jnp.asarray(first_map, jnp.float32), jnp.asarray(second_map, jnp.float32))

def element_dofs(extended):
    row_count = extended.shape[1] - 1
    column_count = extended.shape[2] - 1
    return jnp.stack([extended[component, row_step:row_step + row_count, col_step:col_step + column_count] for row_step, col_step in ELEMENT_NODES for component in (0, 1)])

def element_scatter(values):
    padded = None
    for corner, (row_step, col_step) in enumerate(ELEMENT_NODES):
        placed = jnp.pad(values[2 * corner:2 * corner + 2], ((0, 0), (row_step, 1 - row_step), (col_step, 1 - col_step)))
        padded = placed if padded is None else padded + placed
    return padded

def extend(field):
    return jnp.pad(field, ((0, 0), (0, 1), (0, 1)))

def assemble(padded):
    return padded[:, :-1, :-1]

def fine_apply(field, first_eff, shear_eff, tables):
    row_count, column_count = first_eff.shape
    degrees = element_dofs(extend(field)).reshape(8, row_count * column_count)
    values = first_eff.reshape(1, -1) * jnp.dot(tables[0], degrees, precision=HIGHEST) + shear_eff.reshape(1, -1) * jnp.dot(tables[1], degrees, precision=HIGHEST)
    return assemble(element_scatter(values.reshape(8, row_count, column_count)))

def matrix_apply(field, element_matrix):
    row_count, column_count = (element_matrix.shape[1], element_matrix.shape[2])
    degrees = element_dofs(extend(field))
    values = lax.optimization_barrier(jnp.sum(element_matrix.reshape(8, 8, row_count, column_count) * degrees[None], axis=1))
    return assemble(element_scatter(values))

def matrix_diagonal(element_matrix):
    return assemble(element_scatter(element_matrix[0::9]))

def first_coarse(first_eff, shear_eff, first_map):
    row_count, column_count = first_eff.shape
    half_rows, half_cols = (row_count // 2, column_count // 2)

    def by_subcell(values):
        return values.reshape(half_rows, 2, half_cols, 2).transpose(1, 3, 0, 2).reshape(4, half_rows * half_cols)
    coefficients = jnp.stack([by_subcell(first_eff), by_subcell(shear_eff)], axis=1).reshape(8, half_rows * half_cols)
    return jnp.dot(first_map, coefficients, precision=HIGHEST).reshape(64, half_rows, half_cols)

def next_coarse(element_matrix, second_map):
    row_count, column_count = (element_matrix.shape[1], element_matrix.shape[2])
    half_rows, half_cols = (row_count // 2, column_count // 2)
    sub_blocks = element_matrix.reshape(64, half_rows, 2, half_cols, 2).transpose(2, 4, 0, 1, 3).reshape(256, half_rows * half_cols)
    return jnp.dot(second_map, sub_blocks, precision=HIGHEST).reshape(64, half_rows, half_cols)

def restrict_terms(residual):
    component_count, row_count, column_count = residual.shape
    paired = residual.reshape(component_count, row_count // 2, 2, column_count)
    even_part, odd_part = (paired[:, :, 0], paired[:, :, 1])
    row_terms = jnp.pad(even_part + 0.5 * odd_part, ((0, 0), (0, 1), (0, 0))) + jnp.pad(0.5 * odd_part, ((0, 0), (1, 0), (0, 0)))
    paired = row_terms.reshape(component_count, row_count // 2 + 1, column_count // 2, 2)
    even_part, odd_part = (paired[..., 0], paired[..., 1])
    return jnp.pad(even_part + 0.5 * odd_part, ((0, 0), (0, 0), (0, 1))) + jnp.pad(0.5 * odd_part, ((0, 0), (0, 0), (1, 0)))

def prolong(extended):
    component_count, outer_rows, outer_cols = extended.shape
    half_rows, half_cols = (outer_rows - 1, outer_cols - 1)
    row_terms = jnp.stack([extended[:, :half_rows], 0.5 * (extended[:, :half_rows] + extended[:, 1:])], axis=2)
    row_terms = row_terms.reshape(component_count, 2 * half_rows, outer_cols)
    both_terms = jnp.stack([row_terms[:, :, :half_cols], 0.5 * (row_terms[:, :, :half_cols] + row_terms[:, :, 1:])], axis=3)
    return both_terms.reshape(component_count, 2 * half_rows, 2 * half_cols)

def relax(source, element_matrix):
    diagonal = matrix_diagonal(element_matrix)
    field = DAMPING * source / diagonal
    for sweep_index in range(COARSE_SWEEPS - 1):
        field = field + DAMPING * (source - matrix_apply(field, element_matrix)) / diagonal
    return field

def cycle(level, source, operators, matrices):
    if level == LEVELS:
        return relax(source, matrices[LEVELS - 1])
    apply_level, diagonal = operators[level]
    field = DAMPING * source / diagonal
    for sweep_index in range(SWEEPS - 1):
        field = field + DAMPING * (source - apply_level(field)) / diagonal
    residual = source - apply_level(field)
    coarse_source = assemble(restrict_terms(residual))
    correction = cycle(level + 1, coarse_source, operators, matrices)
    field = field + prolong(extend(correction))
    for sweep_index in range(SWEEPS):
        field = field + DAMPING * (source - apply_level(field)) / diagonal
    return field

def reference(first_lame, shear_modulus, applied_load, plastic_owner, plastic_cell, plastic_code):
    owner_list = plastic_owner[:, 0]
    row_index = (owner_list // N_GY * CX + plastic_cell // CY).astype(jnp.int32)
    col_index = (owner_list % N_GY * CY + plastic_cell % CY).astype(jnp.int32)
    code_total = jnp.zeros((NX, NY), jnp.int32).at[row_index, col_index].add(plastic_code)
    factor = jnp.power(YIELD_DROP, code_total.astype(jnp.float32))
    first_eff = first_lame * factor
    shear_eff = shear_modulus * factor
    tables = element_tables()
    fine_diagonal = assemble(element_scatter(first_eff[None] * jnp.diagonal(tables[0])[:, None, None] + shear_eff[None] * jnp.diagonal(tables[1])[:, None, None]))

    def fine_level(field):
        return fine_apply(field, first_eff, shear_eff, tables)
    matrices = [first_coarse(first_eff, shear_eff, tables[2])]
    for level in range(1, LEVELS):
        matrices.append(next_coarse(matrices[-1], tables[3]))
    operators = [(fine_level, fine_diagonal)]
    for level in range(1, LEVELS):
        element_matrix = matrices[level - 1]
        operators.append((lambda field, chosen=element_matrix: matrix_apply(field, chosen), matrix_diagonal(element_matrix)))
    return cycle(0, applied_load, operators, matrices)
```

```python
import functools
import math

import jax
import jax.numpy as jnp
import numpy as np
from jax import lax
from jax.experimental import pallas as pl
from jax.experimental.pallas import tpu as pltpu
from jax.sharding import PartitionSpec as P

LEVELS = 3
SWEEPS = 2
COARSE_SWEEPS = 6
YIELD_DROP = 0.6
GROUP = 1 << LEVELS
HALO_ROWS = 32
HALO_COLS = 128
LANES = 128
VMEM_LIMIT = 56 * 1024 * 1024
F32 = jnp.float32
BF16 = jnp.bfloat16

FIRST = ("11", "12", "33", "1r", "2r", "3r", "1c", "2c", "3c", "rr", "rc")
FULL = FIRST + ("cc",)
FIRST_AT = {name: FIRST.index(name) for name in FIRST} | {"22": 0, "cc": FIRST.index("rr")}
FULL_AT = {name: FULL.index(name) for name in FULL} | {"22": 0}


def passed_along(array, axis, by):
    devices = lax.axis_size(axis)
    pairs = [(i, i + by) for i in range(devices) if 0 <= i + by < devices]
    return lax.ppermute(array, axis, pairs)


def log2(number):
    power = number.bit_length() - 1
    assert 1 << power == number
    return power


def from_before(value, axis):
    return pltpu.roll(value, 1, axis)


def from_after(value, axis):
    return pltpu.roll(value, value.shape[axis] - 1, axis)


def plus(*terms):
    total = None
    for term in terms:
        if term is not None:
            total = term if total is None else total + term
    return total


def times(weight, term):
    return None if term is None else weight * term


def factor_kernel(place, words, factor, rows_of, cols_of, codes, counts, *, rows, cols, gy):
    word = words[...]
    cell_bits = log2(rows * cols)
    owner = word >> (cell_bits + 2)
    cell = (word >> 2) & (rows * cols - 1)
    row = (owner >> log2(gy)) * rows + (cell >> log2(cols)) - place[0] * rows + HALO_ROWS
    col = (owner & (gy - 1)) * cols + (cell & (cols - 1)) - place[1] * cols
    inside = (row >= 0) & (row < rows + 2 * HALO_ROWS) & (col >= -HALO_COLS) & (col < cols + HALO_COLS)
    at = jnp.where(col < 0, col + cols + HALO_COLS, jnp.where(col >= cols, col + HALO_COLS, col))
    half = (cols + 2 * HALO_COLS) // 2
    tall = rows + 2 * HALO_ROWS
    upper = at >= half
    rows_of[...] = jnp.where(inside, jnp.where(upper, row + tall, row), -1)
    cols_of[...] = jnp.where(upper, at - half, at)
    codes[...] = (word & 3).astype(F32)
    counts[...] = jnp.zeros_like(counts)
    length = words.shape[1]

    @pl.loop(0, words.shape[0])
    def _(i):
        line = pl.ds(i, 1)
        row_id = lax.broadcasted_iota(jnp.int32, (2 * tall, length), 0)
        col_id = lax.broadcasted_iota(jnp.int32, (half, length), 0)
        by_row = jnp.where(row_id == rows_of[line, :], codes[line, :], 0.0).astype(BF16)
        by_col = jnp.where(col_id == cols_of[line, :], 1.0, 0.0).astype(BF16)
        counts[...] += lax.dot_general(
            by_row, by_col, (((1,), (1,)), ((), ())), preferred_element_type=F32
        )

    per_half = half // LANES
    for tile in range(2 * per_half):
        side, lane = tile // per_half, tile % per_half
        count = counts[side * tall : (side + 1) * tall, lane * LANES : (lane + 1) * LANES]
        factor[tile] = jnp.exp(count * math.log(YIELD_DROP))


def yield_factor(place, words, rows, cols, gy):
    tall, wide = rows + 2 * HALO_ROWS, cols + 2 * HALO_COLS
    return pl.pallas_call(
        functools.partial(factor_kernel, rows=rows, cols=cols, gy=gy),
        out_shape=jax.ShapeDtypeStruct((wide // LANES, tall, LANES), F32),
        in_specs=[
            pl.BlockSpec(memory_space=pltpu.SMEM),
            pl.BlockSpec(memory_space=pltpu.VMEM),
        ],
        out_specs=pl.BlockSpec(memory_space=pltpu.VMEM),
        scratch_shapes=[
            pltpu.VMEM(words.shape, jnp.int32),
            pltpu.VMEM(words.shape, jnp.int32),
            pltpu.VMEM(words.shape, F32),
            pltpu.VMEM((2 * tall, wide // 2), F32),
        ],
        compiler_params=pltpu.CompilerParams(vmem_limit_bytes=VMEM_LIMIT),
        cost_estimate=pl.CostEstimate(flops=10**9, bytes_accessed=10**6, transcendentals=0),
        name="yield_factor",
    )(place, words)


class Level:
    def __init__(self, matrix, names_at, inverse, spill):
        self.matrix, self.names_at, self.inverse, self.spill = matrix, names_at, inverse, spill
        self.count = matrix.shape[1]

    def entry(self, name, m, k):
        at = self.names_at.get(name)
        return None if at is None else self.matrix[at, m, k]

    def stress(self, m, k, modes):
        names = "123rc"
        known = {}
        result = []
        for i in range(5):
            terms = []
            for j in range(5):
                name = names[min(i, j)] + names[max(i, j)]
                if name not in known:
                    known[name] = self.entry(name, m, k)
                if known[name] is not None:
                    terms.append(known[name] * modes[j])
            result.append(plus(*terms))
        return result

    def halves(self, component, m, k):
        if component == 0:
            names = ("11", "33", "rr", "13", "1r", "3r")
        else:
            names = ("22", "33", "cc", "23", "3c", "2c")
        first, second, third, cross, by_col, by_row = [self.entry(name, m, k) for name in names]
        base = first + second + third
        by_row, by_col, cross = 2.0 * by_row, 2.0 * by_col, times(2.0, cross)
        if cross is None:
            return base - by_row, base + by_row, by_col, by_col
        return base - by_row, base + by_row, by_col - cross, by_col + cross

    def components(self):
        return (0, 1)

    def make_inverse(self, row_ok, col_ok):
        count = self.count
        for component in self.components():
            kept = {}
            for k in range(count):
                parts = [self.halves(component, m, k) for m in range(count)]
                for m in range(count):
                    above = parts[m - 1] if m else parts[count - 1]
                    lower = [above[1], above[3]]
                    if m == 0:
                        lower = [from_before(value, 0) for value in lower]
                    even, odd = parts[m][0] + lower[0], parts[m][2] + lower[1]
                    kept[m, k] = (even - odd, even + odd)
            for k in range(count):
                for m in range(count):
                    left = kept[m, k - 1][1] if k else from_before(kept[m, count - 1][1], 1)
                    diagonal = kept[m, k][0] + left
                    value = jnp.where(diagonal > 0.0, 0.5 / diagonal, 0.0)
                    if m == 0:
                        value = value * row_ok
                    if k == 0:
                        value = value * col_ok
                    self.inverse[component, m, k] = value


class FineLevel(Level):
    def stress(self, m, k, modes):
        lame, shear, mixed = self.matrix[0, m, k], self.matrix[1, m, k], self.matrix[2, m, k]
        first, second, third, bend_row, bend_col = modes
        twice, mean = shear + shear, lame * (first + second)
        return [
            mean + twice * first,
            mean + twice * second,
            shear * third,
            mixed * bend_row,
            mixed * bend_col,
        ]

    def components(self):
        return (0,)

    def make_inverse(self, row_ok, col_ok):
        count = self.count

        @pl.loop(0, count)
        def _(k):
            parts = [self.matrix[2, m, k] for m in range(count)]
            for m in range(count):
                above = parts[m - 1] if m else from_before(parts[count - 1], 0)
                self.inverse[0, m, k] = parts[m] + above

        for m in range(count):
            left = from_before(self.inverse[0, m, count - 1], 1)
            for k in range(count):
                here = self.inverse[0, m, k]
                diagonal = 4.0 * (here + left)
                left = here
                value = jnp.where(diagonal > 0.0, 0.5 / diagonal, 0.0)
                if m == 0:
                    value = value * row_ok
                if k == 0:
                    value = value * col_ok
                self.inverse[0, m, k] = value


def inverse_of(level, component, m, k):
    return level.inverse[min(component, len(level.components()) - 1), m, k]


def close_columns(level, x):
    count = level.count
    for component in (0, 1):
        for m in range(count):
            x[component, m, count] = from_after(x[component, m, 0], 1)


def start(level, x, source):
    count = level.count

    def column(k):
        for component in (0, 1):
            for m in range(count):
                x[component, m, k] = source[component, m, k] * inverse_of(level, component, m, k)

    over_columns(count, column)
    close_columns(level, x)


def over_columns(count, column):
    if count > 2:
        pl.loop(0, count)(column)
    else:
        for k in range(count):
            column(k)


def apply(level, x, source, out, residual):
    count, spill = level.count, level.spill
    spill[...] = jnp.zeros_like(spill)

    def column(k):
        sums, steps = [], []
        for m in range(count):
            here = [x[component, m, k] for component in (0, 1)]
            after = [x[component, m, k + 1] for component in (0, 1)]
            sums.append([here[c] + after[c] for c in (0, 1)])
            steps.append([after[c] - here[c] for c in (0, 1)])
        sums.append([from_after(value, 0) for value in sums[0]])
        steps.append([from_after(value, 0) for value in steps[0]])
        own, passed = [], []
        for m in range(count):
            modes = (
                sums[m + 1][0] - sums[m][0],
                steps[m][1] + steps[m + 1][1],
                (steps[m][0] + steps[m + 1][0]) + (sums[m + 1][1] - sums[m][1]),
                steps[m + 1][0] - steps[m][0],
                steps[m + 1][1] - steps[m][1],
            )
            first, second, third, bend_row, bend_col = level.stress(m, k, modes)
            own.append((first, third - bend_row, third, second - bend_col))
            passed.append((first, third + bend_row, third, second + bend_col))
        for m in range(count):
            above = passed[m - 1] if m else [from_before(value, 0) for value in passed[count - 1]]
            for component in (0, 1):
                at = 2 * component
                even = above[at] - own[m][at]
                odd = above[at + 1] + own[m][at + 1]
                left = spill[component, m]
                spill[component, m] = even + odd
                rest = source[component, m, k] - ((even - odd) + left)
                if not residual:
                    rest = x[component, m, k] + inverse_of(level, component, m, k) * rest
                out[component, m, k] = rest

    over_columns(count, column)
    for component in (0, 1):
        for m in range(count):
            left = from_before(spill[component, m], 1)
            if not residual:
                left = left * inverse_of(level, component, m, 0)
            out[component, m, 0] = out[component, m, 0] - left
    if not residual:
        close_columns(level, out)


def restrict(residual, target, count):
    half = count // 2
    for component in (0, 1):
        for k in range(half):
            lines = []
            for m in range(count):
                odd = residual[component, m, 2 * k + 1]
                if k:
                    before = residual[component, m, 2 * k - 1]
                else:
                    before = from_before(residual[component, m, count - 1], 1)
                lines.append(residual[component, m, 2 * k] + 0.5 * (odd + before))
            for m in range(half):
                before = lines[2 * m - 1] if m else from_before(lines[count - 1], 0)
                target[component, m, k] = lines[2 * m] + 0.5 * (lines[2 * m + 1] + before)


def prolong(coarse, before, x, count):
    half = count // 2
    for component in (0, 1):
        planes = {(m, k): coarse(component, m, k) for m in range(half) for k in range(half)}
        for m in range(half):
            planes[m, half] = from_after(planes[m, 0], 1)
        for k in range(half + 1):
            planes[half, k] = from_after(planes[0, k], 0)
        for m in range(half):
            for k in range(half):
                a, b, c, d = planes[m, k], planes[m + 1, k], planes[m, k + 1], planes[m + 1, k + 1]
                x[component, 2 * m, 2 * k] = before[component, 2 * m, 2 * k] + a
                x[component, 2 * m + 1, 2 * k] = before[component, 2 * m + 1, 2 * k] + 0.5 * (a + b)
                x[component, 2 * m, 2 * k + 1] = before[component, 2 * m, 2 * k + 1] + 0.5 * (a + c)
                x[component, 2 * m + 1, 2 * k + 1] = before[component, 2 * m + 1, 2 * k + 1] + 0.25 * ((a + b) + (c + d))


def haar(level, names_at, m, k):
    def signed(name, row, col):
        if name not in names_at:
            return None
        value = {
            (a, b): level.matrix[names_at[name], 2 * m + a, 2 * k + b] for a in (0, 1) for b in (0, 1)
        }
        low = value[0, 1] - value[0, 0] if col else value[0, 1] + value[0, 0]
        high = value[1, 1] - value[1, 0] if col else value[1, 1] + value[1, 0]
        return high - low if row else high + low

    return signed


def coarsen_fine(fine, coarse):
    count = coarse.count

    def column(k):
        for m in range(count):
            signed = haar(fine, {"l": 0, "s": 1}, m, k)
            lame, shear = signed("l", 0, 0), signed("s", 0, 0)
            lame_row, shear_row = signed("l", 1, 0), signed("s", 1, 0)
            lame_col, shear_col = signed("l", 0, 1), signed("s", 0, 1)
            lame_both, shear_both = signed("l", 1, 1), signed("s", 1, 1)
            values = {
                "11": 0.25 * (lame + 2.0 * shear),
                "12": 0.25 * lame,
                "33": 0.25 * shear,
                "1r": 0.125 * (lame_col + 2.0 * shear_col),
                "2r": 0.125 * lame_col,
                "3r": 0.125 * shear_row,
                "1c": 0.125 * lame_row,
                "2c": 0.125 * (lame_row + 2.0 * shear_row),
                "3c": 0.125 * shear_col,
                "rr": (lame + 3.0 * shear) * (1.0 / 12.0),
                "rc": 0.0625 * (lame_both + shear_both),
            }
            for name, value in values.items():
                coarse.matrix[FIRST_AT[name], m, k] = value

    over_columns(count, column)


def coarsen(fine, write, count):
    for k in range(count):
        for m in range(count):
            signed = haar(fine, fine.names_at, m, k)

            def total(name):
                return signed(name, 0, 0)

            def by_row(name):
                return signed(name, 1, 0)

            def by_col(name):
                return signed(name, 0, 1)

            def by_both(name):
                return signed(name, 1, 1)

            values = {}
            for name in ("11", "12", "33"):
                values[name] = times(0.25, total(name))
            for i in "123":
                one, two, three = ["".join(sorted(i + j)) for j in "123"]
                values[i + "r"] = 0.125 * plus(by_col(one), by_row(three), total(i + "r"))
                values[i + "c"] = 0.125 * plus(by_row(two), by_col(three), total(i + "c"))
            values["rr"] = 0.0625 * plus(
                total("11"),
                total("33"),
                times(2.0, by_both("13")),
                2.0 * (by_col("1r") + by_row("3r")),
                total("rr"),
            )
            values["cc"] = 0.0625 * plus(
                total("22"),
                total("33"),
                times(2.0, by_both("23")),
                2.0 * (by_row("2c") + by_col("3c")),
                total("cc"),
            )
            values["rc"] = 0.0625 * plus(
                by_both("12"),
                total("13"),
                total("23"),
                by_both("33"),
                by_col("1c"),
                by_row("3c"),
                by_row("2r"),
                by_col("3r"),
                total("rc"),
            )
            for name in FULL:
                write(FULL_AT[name], m, k, values[name])


def edge_masks(place, shape, rows, cols, first_row, grid_rows, grid_cols):
    row = lax.broadcasted_iota(jnp.int32, shape, 0) * GROUP + (place[0] * rows + first_row)
    col = lax.broadcasted_iota(jnp.int32, shape, 1) * GROUP + (place[1] * cols - HALO_COLS)
    return (
        jnp.where(row < grid_rows, 1.0, 0.0).astype(F32),
        jnp.where(col < grid_cols, 1.0, 0.0).astype(F32),
    )


def three_parts(value):
    high = value.astype(BF16)
    rest = value - high.astype(F32)
    middle = rest.astype(BF16)
    low = (rest - middle.astype(F32)).astype(BF16)
    return high, middle, low


def down_kernel(
    place, first_lame, shear_modulus, applied_load, left, right, upper, lower, factor,
    matrix0, inverse0, source0, x0, matrix1, inverse1, source1, x1, matrix2, inverse2, source2, x2, coarsest,
    tiles, stacked, spread, other0, other1, other2, spill0, spill1, spill2, matrix3,
    *, rows, cols, gx, gy,
):
    tall, wide = rows + 2 * HALO_ROWS, cols + 2 * HALO_COLS
    side = tall // GROUP
    row_ok, col_ok = edge_masks(place, (side, LANES), rows, cols, -HALO_ROWS, gx * rows, gy * cols)

    for tile in range(wide // LANES):
        at = lax.broadcasted_iota(jnp.int32, (LANES, GROUP * LANES), 0) + tile * LANES
        if tile < cols // LANES:
            at = at + HALO_COLS
        elif tile == cols // LANES:
            at = at - cols
        target = (at & (GROUP - 1)) * LANES + (at >> LEVELS)
        lane = lax.broadcasted_iota(jnp.int32, (LANES, GROUP * LANES), 1)
        spread[tile * LANES : (tile + 1) * LANES, :] = jnp.where(lane == target, 1.0, 0.0).astype(BF16)

    own = (first_lame, shear_modulus, applied_load.at[0], applied_load.at[1])
    for field in range(4):
        for tile in range(wide // LANES):
            lanes = slice(tile * LANES, (tile + 1) * LANES)
            if tile < cols // LANES:
                middle = own[field][:, lanes]
            else:
                middle = (left if tile == cols // LANES else right)[field]
            parts = [
                (slice(0, HALO_ROWS), upper[field, :, lanes]),
                (slice(HALO_ROWS, HALO_ROWS + rows), middle),
                (slice(HALO_ROWS + rows, tall), lower[field, :, lanes]),
            ]
            for span, value in parts:
                if field < 2:
                    value = value * (0.25 * factor[tile, span, :])
                tiles[tile, span, :] = value
        for m in range(GROUP):
            for tile in range(wide // LANES):
                lanes = slice(tile * LANES, (tile + 1) * LANES)
                for part, value in enumerate(three_parts(tiles[tile, pl.ds(m, side, stride=GROUP), :])):
                    stacked[part * tall + m * side : part * tall + (m + 1) * side, lanes] = value
        for pair in range(GROUP // 2):
            lanes = slice(pair * 2 * LANES, (pair + 1) * 2 * LANES)
            product = jnp.dot(stacked[...], spread[:, lanes], preferred_element_type=F32)
            product = product[:tall] + product[tall : 2 * tall] + product[2 * tall :]
            for m in range(GROUP):
                for half in (0, 1):
                    plane = product[m * side : (m + 1) * side, half * LANES : (half + 1) * LANES]
                    if field < 2:
                        matrix0[field, m, 2 * pair + half] = plane
                    else:
                        source0[field - 2, m, 2 * pair + half] = plane

    def mix(k):
        for m in range(GROUP):
            matrix0[2, m, k] = matrix0[0, m, k] * (1.0 / 3.0) + matrix0[1, m, k]

    over_columns(GROUP, mix)

    level0 = FineLevel(matrix0, {}, inverse0, spill0)
    level1 = Level(matrix1, FIRST_AT, inverse1, spill1)
    level2 = Level(matrix2, FULL_AT, inverse2, spill2)

    coarsen_fine(level0, level1)

    def write2(at, m, k, value):
        matrix2[at, m, k] = value

    coarsen(level1, write2, level2.count)

    def write3(at, m, k, value):
        matrix3[at] = value

    coarsen(level2, write3, 1)
    for level in (level0, level1, level2):
        level.make_inverse(row_ok, col_ok)

    source3 = matrix3.at[pl.ds(len(FULL), 2)]
    chain = (
        (level0, source0, x0, other0, source1),
        (level1, source1, x1, other1, source2),
        (level2, source2, x2, other2, None),
    )
    for level, source, x, other, target in chain:
        start(level, other, source)
        apply(level, other, source, x, residual=False)
        apply(level, x, source, other, residual=True)
        if target is not None:
            restrict(other, target, level.count)
        else:
            restrict_last(other, source3)
    first = HALO_ROWS // GROUP
    for at in range(len(FULL) + 2):
        coarsest[at] = matrix3[at, first : first + rows // GROUP, :]


def restrict_last(residual, target):
    class Planes:
        def __setitem__(self, where, value):
            target[where[0]] = value

    restrict(residual, Planes(), 2)


def up_kernel(
    place, coarse, coarse_before, coarse_after,
    matrix0, inverse0, source0, x0_in, matrix1, inverse1, source1, x1_in, matrix2, inverse2, source2, x2_in,
    displacement,
    x0, other0, x1, other1, x2, other2, spill0, spill1, spill2, spill3, matrix3, inverse3, source3, x3, other3,
    stacked, gathered, tiles,
    *, rows, cols, gx, gy,
):
    block = rows // GROUP
    for at in range(len(FULL) + 2):
        for piece, part in enumerate((coarse_before, coarse, coarse_after)):
            if at < len(FULL):
                matrix3[at, 0, 0, piece * block : (piece + 1) * block, :] = part[at]
            else:
                source3[at - len(FULL), 0, 0, piece * block : (piece + 1) * block, :] = part[at]
    level3 = Level(matrix3, FULL_AT, inverse3, spill3)
    level3.make_inverse(*edge_masks(place, (3 * block, LANES), rows, cols, -rows, gx * rows, gy * cols))
    start(level3, x3, source3)
    now, then = x3, other3
    for _ in range(COARSE_SWEEPS - 1):
        apply(level3, now, source3, then, residual=False)
        now, then = then, now
    offset = block - HALO_ROWS // GROUP
    side = (rows + 2 * HALO_ROWS) // GROUP
    coarse_plane = functools.partial(cut_plane, now, offset, side)

    level0 = FineLevel(matrix0, {}, inverse0, spill0)
    level1 = Level(matrix1, FIRST_AT, inverse1, spill1)
    level2 = Level(matrix2, FULL_AT, inverse2, spill2)
    for level, source, before, x, other in (
        (level2, source2, x2_in, x2, other2),
        (level1, source1, x1_in, x1, other1),
        (level0, source0, x0_in, x0, other0),
    ):
        prolong(coarse_plane, before, x, level.count)
        close_columns(level, x)
        apply(level, x, source, other, residual=False)
        apply(level, other, source, x, residual=False)
        coarse_plane = functools.partial(whole_plane, x)

    for tile in range(cols // LANES):
        at = lax.broadcasted_iota(jnp.int32, (GROUP * LANES, LANES), 1) + tile * LANES + HALO_COLS
        target = (at & (GROUP - 1)) * LANES + (at >> LEVELS)
        line = lax.broadcasted_iota(jnp.int32, (GROUP * LANES, LANES), 0)
        gathered[:, tile * LANES : (tile + 1) * LANES] = jnp.where(line == target, 1.0, 0.0).astype(BF16)
    first = HALO_ROWS // GROUP
    for component in (0, 1):
        for pair in range(GROUP // 2):
            for k in range(GROUP):
                value = jnp.concatenate(
                    [x0[component, 2 * pair + h, k, first : first + block, :] for h in (0, 1)], axis=0
                )
                for part, piece in enumerate(three_parts(value)):
                    line = part * 2 * rows + component * rows + pair * 2 * block
                    stacked[line : line + 2 * block, k * LANES : (k + 1) * LANES] = piece
    product = jnp.dot(stacked[...], gathered[...], preferred_element_type=F32)
    product = product[: 2 * rows] + product[2 * rows : 4 * rows] + product[4 * rows :]
    for component in (0, 1):
        for tile in range(cols // LANES):
            lanes = slice(tile * LANES, (tile + 1) * LANES)
            for m in range(GROUP):
                line = component * rows + m * block
                tiles[component, tile, pl.ds(m, block, stride=GROUP), :] = product[line : line + block, lanes]
            displacement[component, :, lanes] = tiles[component, tile]


def cut_plane(x, offset, side, component, m, k):
    return x[component, 0, 0, offset : offset + side, :]


def whole_plane(x, component, m, k):
    return x[component, m, k]


def body(first_lame, shear_modulus, applied_load, plastic_owner, plastic_cell, plastic_code):
    rows, cols = first_lame.shape
    gx, gy = lax.axis_size("gx"), lax.axis_size("gy")
    devices = gx * gy
    place = jnp.stack([lax.axis_index("gx"), lax.axis_index("gy")]).astype(jnp.int32)

    word = (plastic_owner[:, 0] * (rows * cols) + plastic_cell) * 4 + plastic_code
    fields = [first_lame, shear_modulus, applied_load[0], applied_load[1]]
    first_cols = jnp.stack([field[:, :HALO_COLS] for field in fields])
    last_cols = jnp.stack([field[:, -HALO_COLS:] for field in fields])
    left = passed_along(last_cols, "gy", 1)
    right = passed_along(first_cols, "gy", -1)

    words = lax.all_to_all(
        jnp.broadcast_to(word[None], (devices, word.shape[0])), ("gx", "gy"), 0, 0, tiled=True
    )
    words, left, right = lax.optimization_barrier((words, left, right))

    def whole_rows(span):
        return jnp.concatenate(
            [jnp.stack([field[span] for field in fields]), left[:, span], right[:, span]], axis=2
        )

    upper = passed_along(whole_rows(slice(rows - HALO_ROWS, rows)), "gx", 1)
    lower = passed_along(whole_rows(slice(0, HALO_ROWS)), "gx", -1)
    factor = yield_factor(place, words, rows, cols, gy)

    tall, wide = rows + 2 * HALO_ROWS, cols + 2 * HALO_COLS
    side = tall // GROUP
    vmem, smem = pl.BlockSpec(memory_space=pltpu.VMEM), pl.BlockSpec(memory_space=pltpu.SMEM)

    def planes(fields, count, extra=0, lines=side):
        return (fields, count, count + extra, lines, LANES)

    state = []
    for count, entries, inverses in ((GROUP, 3, 1), (GROUP // 2, len(FIRST), 2), (GROUP // 4, len(FULL), 2)):
        state += [planes(entries, count), planes(inverses, count), planes(2, count), planes(2, count, 1)]
    held = len(FULL) + 2
    counts = (GROUP, GROUP // 2, GROUP // 4)
    *state, coarse = pl.pallas_call(
        functools.partial(down_kernel, rows=rows, cols=cols, gx=gx, gy=gy),
        out_shape=[jax.ShapeDtypeStruct(shape, F32) for shape in state]
        + [jax.ShapeDtypeStruct((held, rows // GROUP, LANES), F32)],
        in_specs=[smem] + [vmem] * 8,
        out_specs=[vmem] * (len(state) + 1),
        scratch_shapes=[
            pltpu.VMEM((wide // LANES, tall, LANES), F32),
            pltpu.VMEM((3 * tall, wide), BF16),
            pltpu.VMEM((wide, GROUP * LANES), BF16),
        ]
        + [pltpu.VMEM(planes(2, count, 1), F32) for count in counts]
        + [pltpu.VMEM((2, count, side, LANES), F32) for count in counts]
        + [pltpu.VMEM((held, side, LANES), F32)],
        compiler_params=pltpu.CompilerParams(vmem_limit_bytes=VMEM_LIMIT),
        name="descent",
    )(place, first_lame, shear_modulus, applied_load, left, right, upper, lower, factor)

    coarse_before = passed_along(coarse, "gx", 1)
    coarse_after = passed_along(coarse, "gx", -1)
    lines = 3 * (rows // GROUP)
    return pl.pallas_call(
        functools.partial(up_kernel, rows=rows, cols=cols, gx=gx, gy=gy),
        out_shape=jax.ShapeDtypeStruct((2, rows, cols), F32),
        in_specs=[smem] + [vmem] * (3 + len(state)),
        out_specs=vmem,
        scratch_shapes=[
            shape
            for count in counts
            for shape in (pltpu.VMEM(planes(2, count, 1), F32),) * 2
        ]
        + [pltpu.VMEM((2, count, side, LANES), F32) for count in counts]
        + [
            pltpu.VMEM((2, 1, lines, LANES), F32),
            pltpu.VMEM(planes(len(FULL), 1, 0, lines), F32),
            pltpu.VMEM(planes(2, 1, 0, lines), F32),
            pltpu.VMEM(planes(2, 1, 0, lines), F32),
            pltpu.VMEM(planes(2, 1, 1, lines), F32),
            pltpu.VMEM(planes(2, 1, 1, lines), F32),
            pltpu.VMEM((6 * rows, GROUP * LANES), BF16),
            pltpu.VMEM((GROUP * LANES, cols), BF16),
            pltpu.VMEM((2, cols // LANES, rows, LANES), F32),
        ],
        compiler_params=pltpu.CompilerParams(vmem_limit_bytes=VMEM_LIMIT),
        name="ascent",
    )(place, coarse, coarse_before, coarse_after, *state)


def solution(mesh):
    return jax.shard_map(
        body,
        mesh=mesh,
        in_specs=(
            P("gx", "gy"),
            P("gx", "gy"),
            P(None, "gx", "gy"),
            P(("gx", "gy"), None),
            P(("gx", "gy")),
            P(("gx", "gy")),
        ),
        out_specs=P(None, "gx", "gy"),
        check_vma=False,
    )
```

```python
import functools
import math

import jax
import jax.numpy as jnp
import numpy as np
from jax import lax
from jax.experimental import pallas as pl
from jax.experimental.pallas import tpu as pltpu
from jax.sharding import PartitionSpec as P

LEVELS = 3
SWEEPS = 2
COARSE_SWEEPS = 6
YIELD_DROP = 0.6
GROUP = 1 << LEVELS
HALO_ROWS = 32
HALO_COLS = 128
LANES = 128
VMEM_LIMIT = 30 * 1024 * 1024
F32 = jnp.float32
BF16 = jnp.bfloat16

FIRST = ("11", "12", "33", "1r", "2r", "3r", "1c", "2c", "3c", "rr", "rc")
FULL = FIRST + ("cc",)
FIRST_AT = {name: FIRST.index(name) for name in FIRST} | {"22": 0, "cc": FIRST.index("rr")}
FULL_AT = {name: FULL.index(name) for name in FULL} | {"22": 0}


def passed_along(array, axis, by):
    devices = lax.axis_size(axis)
    pairs = [(i, i + by) for i in range(devices) if 0 <= i + by < devices]
    return lax.ppermute(array, axis, pairs)


def log2(number):
    power = number.bit_length() - 1
    assert 1 << power == number
    return power


def from_before(value, axis):
    return pltpu.roll(value, 1, axis)


def from_after(value, axis):
    return pltpu.roll(value, value.shape[axis] - 1, axis)


def plus(*terms):
    total = None
    for term in terms:
        if term is not None:
            total = term if total is None else total + term
    return total


def times(weight, term):
    return None if term is None else weight * term


def factor_kernel(place, words, factor, rows_of, cols_of, codes, counts, *, rows, cols, gy):
    word = words[...]
    cell_bits = log2(rows * cols)
    owner = word >> (cell_bits + 2)
    cell = (word >> 2) & (rows * cols - 1)
    row = (owner >> log2(gy)) * rows + (cell >> log2(cols)) - place[0] * rows + HALO_ROWS
    col = (owner & (gy - 1)) * cols + (cell & (cols - 1)) - place[1] * cols
    inside = (row >= 0) & (row < rows + 2 * HALO_ROWS) & (col >= -HALO_COLS) & (col < cols + HALO_COLS)
    at = jnp.where(col < 0, col + cols + HALO_COLS, jnp.where(col >= cols, col + HALO_COLS, col))
    half = (cols + 2 * HALO_COLS) // 2
    tall = rows + 2 * HALO_ROWS
    upper = at >= half
    rows_of[...] = jnp.where(inside, jnp.where(upper, row + tall, row), -1)
    cols_of[...] = jnp.where(upper, at - half, at)
    codes[...] = (word & 3).astype(F32)
    counts[...] = jnp.zeros_like(counts)
    length = words.shape[1]

    @pl.loop(0, words.shape[0])
    def _(i):
        line = pl.ds(i, 1)
        row_id = lax.broadcasted_iota(jnp.int32, (2 * tall, length), 0)
        col_id = lax.broadcasted_iota(jnp.int32, (half, length), 0)
        by_row = jnp.where(row_id == rows_of[line, :], codes[line, :], 0.0).astype(BF16)
        by_col = jnp.where(col_id == cols_of[line, :], 1.0, 0.0).astype(BF16)
        counts[...] += lax.dot_general(
            by_row, by_col, (((1,), (1,)), ((), ())), preferred_element_type=F32
        )

    per_half = half // LANES
    for tile in range(2 * per_half):
        side, lane = tile // per_half, tile % per_half
        count = counts[side * tall : (side + 1) * tall, lane * LANES : (lane + 1) * LANES]
        factor[tile] = jnp.exp(count * math.log(YIELD_DROP))


def yield_factor(place, words, rows, cols, gy):
    tall, wide = rows + 2 * HALO_ROWS, cols + 2 * HALO_COLS
    return pl.pallas_call(
        functools.partial(factor_kernel, rows=rows, cols=cols, gy=gy),
        out_shape=jax.ShapeDtypeStruct((wide // LANES, tall, LANES), F32),
        in_specs=[
            pl.BlockSpec(memory_space=pltpu.SMEM),
            pl.BlockSpec(memory_space=pltpu.VMEM),
        ],
        out_specs=pl.BlockSpec(memory_space=pltpu.VMEM),
        scratch_shapes=[
            pltpu.VMEM(words.shape, jnp.int32),
            pltpu.VMEM(words.shape, jnp.int32),
            pltpu.VMEM(words.shape, F32),
            pltpu.VMEM((2 * tall, wide // 2), F32),
        ],
        compiler_params=pltpu.CompilerParams(vmem_limit_bytes=VMEM_LIMIT),
        cost_estimate=pl.CostEstimate(flops=10**9, bytes_accessed=10**6, transcendentals=0),
        name="yield_factor",
    )(place, words)


class Level:
    def __init__(self, matrix, names_at, inverse, spill):
        self.matrix, self.names_at, self.inverse, self.spill = matrix, names_at, inverse, spill
        self.count = matrix.shape[1]

    def entry(self, name, m, k):
        at = self.names_at.get(name)
        return None if at is None else self.matrix[at, m, k]

    def stress(self, m, k, modes):
        names = "123rc"
        known = {}
        result = []
        for i in range(5):
            terms = []
            for j in range(5):
                name = names[min(i, j)] + names[max(i, j)]
                if name not in known:
                    known[name] = self.entry(name, m, k)
                if known[name] is not None:
                    terms.append(known[name] * modes[j])
            result.append(plus(*terms))
        return result

    def halves(self, component, m, k):
        if component == 0:
            names = ("11", "33", "rr", "13", "1r", "3r")
        else:
            names = ("22", "33", "cc", "23", "3c", "2c")
        first, second, third, cross, by_col, by_row = [self.entry(name, m, k) for name in names]
        base = first + second + third
        by_row, by_col, cross = 2.0 * by_row, 2.0 * by_col, times(2.0, cross)
        if cross is None:
            return base - by_row, base + by_row, by_col, by_col
        return base - by_row, base + by_row, by_col - cross, by_col + cross

    def components(self):
        return (0, 1)

    def make_inverse(self, row_ok, col_ok):
        count = self.count
        for component in self.components():
            kept = {}
            for k in range(count):
                parts = [self.halves(component, m, k) for m in range(count)]
                for m in range(count):
                    above = parts[m - 1] if m else parts[count - 1]
                    lower = [above[1], above[3]]
                    if m == 0:
                        lower = [from_before(value, 0) for value in lower]
                    even, odd = parts[m][0] + lower[0], parts[m][2] + lower[1]
                    kept[m, k] = (even - odd, even + odd)
            for k in range(count):
                for m in range(count):
                    left = kept[m, k - 1][1] if k else from_before(kept[m, count - 1][1], 1)
                    diagonal = kept[m, k][0] + left
                    value = jnp.where(diagonal > 0.0, 0.5 / diagonal, 0.0)
                    if m == 0:
                        value = value * row_ok
                    if k == 0:
                        value = value * col_ok
                    self.inverse[component, m, k] = value


class FineLevel(Level):
    def stress(self, m, k, modes):
        lame, shear, mixed = self.matrix[0, m, k], self.matrix[1, m, k], self.matrix[2, m, k]
        first, second, third, bend_row, bend_col = modes
        twice, mean = shear + shear, lame * (first + second)
        return [
            mean + twice * first,
            mean + twice * second,
            shear * third,
            mixed * bend_row,
            mixed * bend_col,
        ]

    def components(self):
        return (0,)

    def make_inverse(self, row_ok, col_ok):
        count = self.count

        @pl.loop(0, count)
        def _(k):
            parts = [self.matrix[2, m, k] for m in range(count)]
            for m in range(count):
                above = parts[m - 1] if m else from_before(parts[count - 1], 0)
                self.inverse[0, m, k] = parts[m] + above

        for m in range(count):
            left = from_before(self.inverse[0, m, count - 1], 1)
            for k in range(count):
                here = self.inverse[0, m, k]
                diagonal = 4.0 * (here + left)
                left = here
                value = jnp.where(diagonal > 0.0, 0.5 / diagonal, 0.0)
                if m == 0:
                    value = value * row_ok
                if k == 0:
                    value = value * col_ok
                self.inverse[0, m, k] = value


def inverse_of(level, component, m, k):
    return level.inverse[min(component, len(level.components()) - 1), m, k]


def close_columns(level, x):
    count = level.count
    for component in (0, 1):
        for m in range(count):
            x[component, m, count] = from_after(x[component, m, 0], 1)


def start(level, x, source):
    count = level.count

    def column(k):
        for component in (0, 1):
            for m in range(count):
                x[component, m, k] = source[component, m, k] * inverse_of(level, component, m, k)

    over_columns(count, column)
    close_columns(level, x)


def over_columns(count, column):
    if count > 2:
        pl.loop(0, count)(column)
    else:
        for k in range(count):
            column(k)


def apply(level, x, source, out, residual):
    count, spill = level.count, level.spill
    spill[...] = jnp.zeros_like(spill)

    def column(k):
        sums, steps = [], []
        for m in range(count):
            here = [x[component, m, k] for component in (0, 1)]
            after = [x[component, m, k + 1] for component in (0, 1)]
            sums.append([here[c] + after[c] for c in (0, 1)])
            steps.append([after[c] - here[c] for c in (0, 1)])
        sums.append([from_after(value, 0) for value in sums[0]])
        steps.append([from_after(value, 0) for value in steps[0]])
        own, passed = [], []
        for m in range(count):
            modes = (
                sums[m + 1][0] - sums[m][0],
                steps[m][1] + steps[m + 1][1],
                (steps[m][0] + steps[m + 1][0]) + (sums[m + 1][1] - sums[m][1]),
                steps[m + 1][0] - steps[m][0],
                steps[m + 1][1] - steps[m][1],
            )
            first, second, third, bend_row, bend_col = level.stress(m, k, modes)
            own.append((first, third - bend_row, third, second - bend_col))
            passed.append((first, third + bend_row, third, second + bend_col))
        for m in range(count):
            above = passed[m - 1] if m else [from_before(value, 0) for value in passed[count - 1]]
            for component in (0, 1):
                at = 2 * component
                even = above[at] - own[m][at]
                odd = above[at + 1] + own[m][at + 1]
                left = spill[component, m]
                spill[component, m] = even + odd
                rest = source[component, m, k] - ((even - odd) + left)
                if not residual:
                    rest = x[component, m, k] + inverse_of(level, component, m, k) * rest
                out[component, m, k] = rest

    over_columns(count, column)
    for component in (0, 1):
        for m in range(count):
            left = from_before(spill[component, m], 1)
            if not residual:
                left = left * inverse_of(level, component, m, 0)
            out[component, m, 0] = out[component, m, 0] - left
    if not residual:
        close_columns(level, out)


def restrict(residual, target, count):
    half = count // 2
    for component in (0, 1):
        for k in range(half):
            lines = []
            for m in range(count):
                odd = residual[component, m, 2 * k + 1]
                if k:
                    before = residual[component, m, 2 * k - 1]
                else:
                    before = from_before(residual[component, m, count - 1], 1)
                lines.append(residual[component, m, 2 * k] + 0.5 * (odd + before))
            for m in range(half):
                before = lines[2 * m - 1] if m else from_before(lines[count - 1], 0)
                target[component, m, k] = lines[2 * m] + 0.5 * (lines[2 * m + 1] + before)


def prolong(coarse, before, x, count):
    half = count // 2
    for component in (0, 1):
        planes = {(m, k): coarse(component, m, k) for m in range(half) for k in range(half)}
        for m in range(half):
            planes[m, half] = from_after(planes[m, 0], 1)
        for k in range(half + 1):
            planes[half, k] = from_after(planes[0, k], 0)
        for m in range(half):
            for k in range(half):
                a, b, c, d = planes[m, k], planes[m + 1, k], planes[m, k + 1], planes[m + 1, k + 1]
                x[component, 2 * m, 2 * k] = before[component, 2 * m, 2 * k] + a
                x[component, 2 * m + 1, 2 * k] = before[component, 2 * m + 1, 2 * k] + 0.5 * (a + b)
                x[component, 2 * m, 2 * k + 1] = before[component, 2 * m, 2 * k + 1] + 0.5 * (a + c)
                x[component, 2 * m + 1, 2 * k + 1] = before[component, 2 * m + 1, 2 * k + 1] + 0.25 * ((a + b) + (c + d))


def haar(level, names_at, m, k):
    def signed(name, row, col):
        if name not in names_at:
            return None
        value = {
            (a, b): level.matrix[names_at[name], 2 * m + a, 2 * k + b] for a in (0, 1) for b in (0, 1)
        }
        low = value[0, 1] - value[0, 0] if col else value[0, 1] + value[0, 0]
        high = value[1, 1] - value[1, 0] if col else value[1, 1] + value[1, 0]
        return high - low if row else high + low

    return signed


def coarsen_fine(fine, coarse):
    count = coarse.count

    def column(k):
        for m in range(count):
            signed = haar(fine, {"l": 0, "s": 1}, m, k)
            lame, shear = signed("l", 0, 0), signed("s", 0, 0)
            lame_row, shear_row = signed("l", 1, 0), signed("s", 1, 0)
            lame_col, shear_col = signed("l", 0, 1), signed("s", 0, 1)
            lame_both, shear_both = signed("l", 1, 1), signed("s", 1, 1)
            values = {
                "11": 0.25 * (lame + 2.0 * shear),
                "12": 0.25 * lame,
                "33": 0.25 * shear,
                "1r": 0.125 * (lame_col + 2.0 * shear_col),
                "2r": 0.125 * lame_col,
                "3r": 0.125 * shear_row,
                "1c": 0.125 * lame_row,
                "2c": 0.125 * (lame_row + 2.0 * shear_row),
                "3c": 0.125 * shear_col,
                "rr": (lame + 3.0 * shear) * (1.0 / 12.0),
                "rc": 0.0625 * (lame_both + shear_both),
            }
            for name, value in values.items():
                coarse.matrix[FIRST_AT[name], m, k] = value

    over_columns(count, column)


def coarsen(fine, write, count):
    for k in range(count):
        for m in range(count):
            signed = haar(fine, fine.names_at, m, k)

            def total(name):
                return signed(name, 0, 0)

            def by_row(name):
                return signed(name, 1, 0)

            def by_col(name):
                return signed(name, 0, 1)

            def by_both(name):
                return signed(name, 1, 1)

            values = {}
            for name in ("11", "12", "33"):
                values[name] = times(0.25, total(name))
            for i in "123":
                one, two, three = ["".join(sorted(i + j)) for j in "123"]
                values[i + "r"] = 0.125 * plus(by_col(one), by_row(three), total(i + "r"))
                values[i + "c"] = 0.125 * plus(by_row(two), by_col(three), total(i + "c"))
            values["rr"] = 0.0625 * plus(
                total("11"),
                total("33"),
                times(2.0, by_both("13")),
                2.0 * (by_col("1r") + by_row("3r")),
                total("rr"),
            )
            values["cc"] = 0.0625 * plus(
                total("22"),
                total("33"),
                times(2.0, by_both("23")),
                2.0 * (by_row("2c") + by_col("3c")),
                total("cc"),
            )
            values["rc"] = 0.0625 * plus(
                by_both("12"),
                total("13"),
                total("23"),
                by_both("33"),
                by_col("1c"),
                by_row("3c"),
                by_row("2r"),
                by_col("3r"),
                total("rc"),
            )
            for name in FULL:
                write(FULL_AT[name], m, k, values[name])


def edge_masks(place, shape, rows, cols, first_row, grid_rows, grid_cols):
    row = lax.broadcasted_iota(jnp.int32, shape, 0) * GROUP + (place[0] * rows + first_row)
    col = lax.broadcasted_iota(jnp.int32, shape, 1) * GROUP + (place[1] * cols - HALO_COLS)
    return (
        jnp.where(row < grid_rows, 1.0, 0.0).astype(F32),
        jnp.where(col < grid_cols, 1.0, 0.0).astype(F32),
    )


def three_parts(value):
    high = value.astype(BF16)
    rest = value - high.astype(F32)
    middle = rest.astype(BF16)
    low = (rest - middle.astype(F32)).astype(BF16)
    return high, middle, low


def down_kernel(
    place, first_lame, shear_modulus, applied_load, left, right, upper, lower, factor,
    matrix0, inverse0, source0, x0, matrix1, inverse1, source1, x1, matrix2, inverse2, source2, x2, coarsest,
    tiles, stacked, spread, other0, other1, other2, spill0, spill1, spill2, matrix3,
    *, rows, cols, gx, gy,
):
    tall, wide = rows + 2 * HALO_ROWS, cols + 2 * HALO_COLS
    side = tall // GROUP
    row_ok, col_ok = edge_masks(place, (side, LANES), rows, cols, -HALO_ROWS, gx * rows, gy * cols)

    for tile in range(wide // LANES):
        at = lax.broadcasted_iota(jnp.int32, (LANES, GROUP * LANES), 0) + tile * LANES
        if tile < cols // LANES:
            at = at + HALO_COLS
        elif tile == cols // LANES:
            at = at - cols
        target = (at & (GROUP - 1)) * LANES + (at >> LEVELS)
        lane = lax.broadcasted_iota(jnp.int32, (LANES, GROUP * LANES), 1)
        spread[tile * LANES : (tile + 1) * LANES, :] = jnp.where(lane == target, 1.0, 0.0).astype(BF16)

    own = (first_lame, shear_modulus, applied_load.at[0], applied_load.at[1])
    for field in range(4):
        for tile in range(wide // LANES):
            lanes = slice(tile * LANES, (tile + 1) * LANES)
            if tile < cols // LANES:
                middle = own[field][:, lanes]
            else:
                middle = (left if tile == cols // LANES else right)[field]
            parts = [
                (slice(0, HALO_ROWS), upper[field, :, lanes]),
                (slice(HALO_ROWS, HALO_ROWS + rows), middle),
                (slice(HALO_ROWS + rows, tall), lower[field, :, lanes]),
            ]
            for span, value in parts:
                if field < 2:
                    value = value * (0.25 * factor[tile, span, :])
                tiles[tile, span, :] = value
        for m in range(GROUP):
            for tile in range(wide // LANES):
                lanes = slice(tile * LANES, (tile + 1) * LANES)
                for part, value in enumerate(three_parts(tiles[tile, pl.ds(m, side, stride=GROUP), :])):
                    stacked[part * tall + m * side : part * tall + (m + 1) * side, lanes] = value
        for pair in range(GROUP // 2):
            lanes = slice(pair * 2 * LANES, (pair + 1) * 2 * LANES)
            product = jnp.dot(stacked[...], spread[:, lanes], preferred_element_type=F32)
            product = product[:tall] + product[tall : 2 * tall] + product[2 * tall :]
            for m in range(GROUP):
                for half in (0, 1):
                    plane = product[m * side : (m + 1) * side, half * LANES : (half + 1) * LANES]
                    if field < 2:
                        matrix0[field, m, 2 * pair + half] = plane
                    else:
                        source0[field - 2, m, 2 * pair + half] = plane

    def mix(k):
        for m in range(GROUP):
            matrix0[2, m, k] = matrix0[0, m, k] * (1.0 / 3.0) + matrix0[1, m, k]

    over_columns(GROUP, mix)

    level0 = FineLevel(matrix0, {}, inverse0, spill0)
    level1 = Level(matrix1, FIRST_AT, inverse1, spill1)
    level2 = Level(matrix2, FULL_AT, inverse2, spill2)

    coarsen_fine(level0, level1)

    def write2(at, m, k, value):
        matrix2[at, m, k] = value

    coarsen(level1, write2, level2.count)

    def write3(at, m, k, value):
        matrix3[at] = value

    coarsen(level2, write3, 1)
    for level in (level0, level1, level2):
        level.make_inverse(row_ok, col_ok)

    source3 = matrix3.at[pl.ds(len(FULL), 2)]
    chain = (
        (level0, source0, x0, other0, source1),
        (level1, source1, x1, other1, source2),
        (level2, source2, x2, other2, None),
    )
    for level, source, x, other, target in chain:
        start(level, other, source)
        apply(level, other, source, x, residual=False)
        apply(level, x, source, other, residual=True)
        if target is not None:
            restrict(other, target, level.count)
        else:
            restrict_last(other, source3)
    first = HALO_ROWS // GROUP
    for at in range(len(FULL) + 2):
        coarsest[at] = matrix3[at, first : first + rows // GROUP, :]


def restrict_last(residual, target):
    class Planes:
        def __setitem__(self, where, value):
            target[where[0]] = value

    restrict(residual, Planes(), 2)


def up_kernel(
    place, coarse, coarse_before, coarse_after,
    matrix0, inverse0, source0, x0_in, matrix1, inverse1, source1, x1_in, matrix2, inverse2, source2, x2_in,
    displacement,
    x0, other0, x1, other1, x2, other2, spill0, spill1, spill2, spill3, matrix3, inverse3, source3, x3, other3,
    stacked, gathered, tiles,
    *, rows, cols, gx, gy,
):
    block = rows // GROUP
    for at in range(len(FULL) + 2):
        for piece, part in enumerate((coarse_before, coarse, coarse_after)):
            if at < len(FULL):
                matrix3[at, 0, 0, piece * block : (piece + 1) * block, :] = part[at]
            else:
                source3[at - len(FULL), 0, 0, piece * block : (piece + 1) * block, :] = part[at]
    level3 = Level(matrix3, FULL_AT, inverse3, spill3)
    level3.make_inverse(*edge_masks(place, (3 * block, LANES), rows, cols, -rows, gx * rows, gy * cols))
    start(level3, x3, source3)
    now, then = x3, other3
    for _ in range(COARSE_SWEEPS - 1):
        apply(level3, now, source3, then, residual=False)
        now, then = then, now
    offset = block - HALO_ROWS // GROUP
    side = (rows + 2 * HALO_ROWS) // GROUP
    coarse_plane = functools.partial(cut_plane, now, offset, side)

    level0 = FineLevel(matrix0, {}, inverse0, spill0)
    level1 = Level(matrix1, FIRST_AT, inverse1, spill1)
    level2 = Level(matrix2, FULL_AT, inverse2, spill2)
    for level, source, before, x, other in (
        (level2, source2, x2_in, x2, other2),
        (level1, source1, x1_in, x1, other1),
        (level0, source0, x0_in, x0, other0),
    ):
        prolong(coarse_plane, before, x, level.count)
        close_columns(level, x)
        apply(level, x, source, other, residual=False)
        apply(level, other, source, x, residual=False)
        coarse_plane = functools.partial(whole_plane, x)

    for tile in range(cols // LANES):
        at = lax.broadcasted_iota(jnp.int32, (GROUP * LANES, LANES), 1) + tile * LANES + HALO_COLS
        target = (at & (GROUP - 1)) * LANES + (at >> LEVELS)
        line = lax.broadcasted_iota(jnp.int32, (GROUP * LANES, LANES), 0)
        gathered[:, tile * LANES : (tile + 1) * LANES] = jnp.where(line == target, 1.0, 0.0).astype(BF16)
    first = HALO_ROWS // GROUP
    for component in (0, 1):
        for pair in range(GROUP // 2):
            for k in range(GROUP):
                value = jnp.concatenate(
                    [x0[component, 2 * pair + h, k, first : first + block, :] for h in (0, 1)], axis=0
                )
                for part, piece in enumerate(three_parts(value)):
                    line = part * 2 * rows + component * rows + pair * 2 * block
                    stacked[line : line + 2 * block, k * LANES : (k + 1) * LANES] = piece
    product = jnp.dot(stacked[...], gathered[...], preferred_element_type=F32)
    product = product[: 2 * rows] + product[2 * rows : 4 * rows] + product[4 * rows :]
    for component in (0, 1):
        for tile in range(cols // LANES):
            lanes = slice(tile * LANES, (tile + 1) * LANES)
            for m in range(GROUP):
                line = component * rows + m * block
                tiles[component, tile, pl.ds(m, block, stride=GROUP), :] = product[line : line + block, lanes]
            displacement[component, :, lanes] = tiles[component, tile]


def cut_plane(x, offset, side, component, m, k):
    return x[component, 0, 0, offset : offset + side, :]


def whole_plane(x, component, m, k):
    return x[component, m, k]


def body(first_lame, shear_modulus, applied_load, plastic_owner, plastic_cell, plastic_code):
    rows, cols = first_lame.shape
    gx, gy = lax.axis_size("gx"), lax.axis_size("gy")
    devices = gx * gy
    place = jnp.stack([lax.axis_index("gx"), lax.axis_index("gy")]).astype(jnp.int32)

    word = (plastic_owner[:, 0] * (rows * cols) + plastic_cell) * 4 + plastic_code
    fields = [first_lame, shear_modulus, applied_load[0], applied_load[1]]
    first_cols = jnp.stack([field[:, :HALO_COLS] for field in fields])
    last_cols = jnp.stack([field[:, -HALO_COLS:] for field in fields])
    left = passed_along(last_cols, "gy", 1)
    right = passed_along(first_cols, "gy", -1)

    words = lax.all_to_all(
        jnp.broadcast_to(word[None], (devices, word.shape[0])), ("gx", "gy"), 0, 0, tiled=True
    )
    words, left, right = lax.optimization_barrier((words, left, right))

    def whole_rows(span):
        return jnp.concatenate(
            [jnp.stack([field[span] for field in fields]), left[:, span], right[:, span]], axis=2
        )

    upper = passed_along(whole_rows(slice(rows - HALO_ROWS, rows)), "gx", 1)
    lower = passed_along(whole_rows(slice(0, HALO_ROWS)), "gx", -1)
    factor = yield_factor(place, words, rows, cols, gy)

    tall, wide = rows + 2 * HALO_ROWS, cols + 2 * HALO_COLS
    side = tall // GROUP
    vmem, smem = pl.BlockSpec(memory_space=pltpu.VMEM), pl.BlockSpec(memory_space=pltpu.SMEM)

    def planes(fields, count, extra=0, lines=side):
        return (fields, count, count + extra, lines, LANES)

    state = []
    for count, entries, inverses in ((GROUP, 3, 1), (GROUP // 2, len(FIRST), 2), (GROUP // 4, len(FULL), 2)):
        state += [planes(entries, count), planes(inverses, count), planes(2, count), planes(2, count, 1)]
    held = len(FULL) + 2
    counts = (GROUP, GROUP // 2, GROUP // 4)
    *state, coarse = pl.pallas_call(
        functools.partial(down_kernel, rows=rows, cols=cols, gx=gx, gy=gy),
        out_shape=[jax.ShapeDtypeStruct(shape, F32) for shape in state]
        + [jax.ShapeDtypeStruct((held, rows // GROUP, LANES), F32)],
        in_specs=[smem] + [vmem] * 8,
        out_specs=[vmem] * (len(state) + 1),
        scratch_shapes=[
            pltpu.VMEM((wide // LANES, tall, LANES), F32),
            pltpu.VMEM((3 * tall, wide), BF16),
            pltpu.VMEM((wide, GROUP * LANES), BF16),
        ]
        + [pltpu.VMEM(planes(2, count, 1), F32) for count in counts]
        + [pltpu.VMEM((2, count, side, LANES), F32) for count in counts]
        + [pltpu.VMEM((held, side, LANES), F32)],
        compiler_params=pltpu.CompilerParams(vmem_limit_bytes=VMEM_LIMIT),
        name="descent",
    )(place, first_lame, shear_modulus, applied_load, left, right, upper, lower, factor)

    coarse_before = passed_along(coarse, "gx", 1)
    coarse_after = passed_along(coarse, "gx", -1)
    lines = 3 * (rows // GROUP)
    return pl.pallas_call(
        functools.partial(up_kernel, rows=rows, cols=cols, gx=gx, gy=gy),
        out_shape=jax.ShapeDtypeStruct((2, rows, cols), F32),
        in_specs=[smem] + [vmem] * (3 + len(state)),
        out_specs=vmem,
        scratch_shapes=[
            shape
            for count in counts
            for shape in (pltpu.VMEM(planes(2, count, 1), F32),) * 2
        ]
        + [pltpu.VMEM((2, count, side, LANES), F32) for count in counts]
        + [
            pltpu.VMEM((2, 1, lines, LANES), F32),
            pltpu.VMEM(planes(len(FULL), 1, 0, lines), F32),
            pltpu.VMEM(planes(2, 1, 0, lines), F32),
            pltpu.VMEM(planes(2, 1, 0, lines), F32),
            pltpu.VMEM(planes(2, 1, 1, lines), F32),
            pltpu.VMEM(planes(2, 1, 1, lines), F32),
            pltpu.VMEM((6 * rows, GROUP * LANES), BF16),
            pltpu.VMEM((GROUP * LANES, cols), BF16),
            pltpu.VMEM((2, cols // LANES, rows, LANES), F32),
        ],
        compiler_params=pltpu.CompilerParams(vmem_limit_bytes=VMEM_LIMIT),
        name="ascent",
    )(place, coarse, coarse_before, coarse_after, *state)


def solution(mesh):
    return jax.shard_map(
        body,
        mesh=mesh,
        in_specs=(
            P("gx", "gy"),
            P("gx", "gy"),
            P(None, "gx", "gy"),
            P(("gx", "gy"), None),
            P(("gx", "gy")),
            P(("gx", "gy")),
        ),
        out_specs=P(None, "gx", "gy"),
        check_vma=False,
    )
```

```python
import functools
import math

import jax
import jax.numpy as jnp
import numpy as np
from jax import lax
from jax.experimental import pallas as pl
from jax.experimental.pallas import tpu as pltpu
from jax.sharding import PartitionSpec as P

LEVELS = 3
SWEEPS = 2
COARSE_SWEEPS = 6
YIELD_DROP = 0.6
GROUP = 1 << LEVELS
HALO_ROWS = 32
HALO_COLS = 128
LANES = 128
LISTS_AT_ONCE = 16
VMEM_LIMIT = 30 * 1024 * 1024
F32 = jnp.float32
BF16 = jnp.bfloat16

FIRST = ("11", "12", "33", "1r", "2r", "3r", "1c", "2c", "3c", "rr", "rc")
FULL = FIRST + ("cc",)
FIRST_AT = {name: FIRST.index(name) for name in FIRST} | {"22": 0, "cc": FIRST.index("rr")}
FULL_AT = {name: FULL.index(name) for name in FULL} | {"22": 0}


def passed_along(array, axis, by):
    devices = lax.axis_size(axis)
    pairs = [(i, i + by) for i in range(devices) if 0 <= i + by < devices]
    return lax.ppermute(array, axis, pairs)


def log2(number):
    power = number.bit_length() - 1
    assert 1 << power == number
    return power


def from_before(value, axis):
    return pltpu.roll(value, 1, axis)


def from_after(value, axis):
    return pltpu.roll(value, value.shape[axis] - 1, axis)


def plus(*terms):
    total = None
    for term in terms:
        if term is not None:
            total = term if total is None else total + term
    return total


def times(weight, term):
    return None if term is None else weight * term


def factor_kernel(place, words, factor, tall_of, lane_of, codes, counts, *, rows, cols, gy):
    word = words[...]
    cell_bits = log2(rows * cols)
    owner = word >> (cell_bits + 2)
    cell = (word >> 2) & (rows * cols - 1)
    row = (owner >> log2(gy)) * rows + (cell >> log2(cols)) - place[0] * rows + HALO_ROWS
    col = (owner & (gy - 1)) * cols + (cell & (cols - 1)) - place[1] * cols
    tall = rows + 2 * HALO_ROWS
    inside = (row >= 0) & (row < tall) & (col >= -HALO_COLS) & (col < cols + HALO_COLS)
    at = jnp.where(col < 0, col + cols + HALO_COLS, jnp.where(col >= cols, col + HALO_COLS, col))
    tall_of[...] = jnp.where(inside, row + tall * (at >> log2(2 * LANES)), -1)
    lane_of[...] = at & (2 * LANES - 1)
    codes[...] = (word & 3).astype(F32)
    counts[...] = jnp.zeros_like(counts)
    length = words.shape[1]
    group = min(LISTS_AT_ONCE, words.shape[0])

    @pl.loop(0, words.shape[0] // group)
    def _(i):
        tall_id = lax.broadcasted_iota(jnp.int32, (counts.shape[0], length), 0)
        lane_id = lax.broadcasted_iota(jnp.int32, (2 * LANES, length), 0)
        by_tall, by_lane = [], []
        for j in range(group):
            line = pl.ds(i * group + j, 1)
            by_tall.append(jnp.where(tall_id == tall_of[line, :], codes[line, :], 0.0).astype(BF16))
            by_lane.append(jnp.where(lane_id == lane_of[line, :], 1.0, 0.0).astype(BF16))
        counts[...] += lax.dot_general(
            jnp.concatenate(by_tall, axis=1),
            jnp.concatenate(by_lane, axis=1),
            (((1,), (1,)), ((), ())),
            preferred_element_type=F32,
        )

    for tile in range(counts.shape[0] // tall * 2):
        lines, lanes = tile // 2 * tall, tile % 2 * LANES
        count = counts[lines : lines + tall, lanes : lanes + LANES]
        factor[tile] = jnp.exp(count * math.log(YIELD_DROP))


def yield_factor(place, words, rows, cols, gy):
    tall, wide = rows + 2 * HALO_ROWS, cols + 2 * HALO_COLS
    return pl.pallas_call(
        functools.partial(factor_kernel, rows=rows, cols=cols, gy=gy),
        out_shape=jax.ShapeDtypeStruct((wide // LANES, tall, LANES), F32),
        in_specs=[
            pl.BlockSpec(memory_space=pltpu.SMEM),
            pl.BlockSpec(memory_space=pltpu.VMEM),
        ],
        out_specs=pl.BlockSpec(memory_space=pltpu.VMEM),
        scratch_shapes=[
            pltpu.VMEM(words.shape, jnp.int32),
            pltpu.VMEM(words.shape, jnp.int32),
            pltpu.VMEM(words.shape, F32),
            pltpu.VMEM((tall * wide // (2 * LANES), 2 * LANES), F32),
        ],
        compiler_params=pltpu.CompilerParams(vmem_limit_bytes=VMEM_LIMIT),
        cost_estimate=pl.CostEstimate(
            flops=2 * tall * wide * words.size, bytes_accessed=4 * words.size, transcendentals=tall * wide
        ),
        name="yield_factor",
    )(place, words)


def pack_kernel(
    first_lame, shear_modulus, applied_load, owner, cell, code,
    fields, first_cols, last_cols, words, lists, arrived,
    *, cells,
):
    copies = [
        pltpu.make_async_copy(source, target, arrived.at[at])
        for at, (source, target) in enumerate(
            (
                (owner, lists.at[0]),
                (cell, lists.at[1]),
                (code, lists.at[2]),
                (first_lame, fields.at[0]),
                (shear_modulus, fields.at[1]),
                (applied_load, fields.at[pl.ds(2, 2)]),
            )
        )
    ]
    for copy in copies:
        copy.start()
    for copy in copies[:3]:
        copy.wait()
    word = (lists[0] * cells + lists[1]) * 4 + lists[2]
    for device in range(words.shape[0]):
        words[device] = word
    for copy in copies[3:]:
        copy.wait()
    first_cols[...] = fields[:, :, :HALO_COLS]
    last_cols[...] = fields[:, :, fields.shape[2] - HALO_COLS :]


def pack(first_lame, shear_modulus, applied_load, owner, cell, code, devices):
    rows, cols = first_lame.shape
    edge = jax.ShapeDtypeStruct((4, rows, HALO_COLS), F32)
    length = cell.shape[0]
    arrays = [first_lame, shear_modulus, applied_load] + [part.reshape(1, -1) for part in (owner, cell, code)]
    hbm, vmem = pl.BlockSpec(memory_space=pltpu.HBM), pl.BlockSpec(memory_space=pltpu.VMEM)
    return pl.pallas_call(
        functools.partial(pack_kernel, cells=rows * cols),
        out_shape=[
            jax.ShapeDtypeStruct((4, rows, cols), F32),
            edge,
            edge,
            jax.ShapeDtypeStruct((devices, 1, length), jnp.int32),
        ],
        in_specs=[hbm] * 6,
        out_specs=[vmem] * 4,
        scratch_shapes=[pltpu.VMEM((3, 1, length), jnp.int32), pltpu.SemaphoreType.DMA((6,))],
        compiler_params=pltpu.CompilerParams(vmem_limit_bytes=8 * 1024 * 1024),
        name="pack",
    )(*[pltpu.with_memory_space_constraint(array, pltpu.HBM) for array in arrays])


def rows_kernel(fields, left, right, last_rows, first_rows):
    cols = fields.shape[2]
    for out, start in ((last_rows, fields.shape[1] - HALO_ROWS), (first_rows, 0)):
        span = slice(start, start + HALO_ROWS)
        out[:, :, :cols] = fields[:, span, :]
        out[:, :, cols : cols + HALO_COLS] = left[:, span, :]
        out[:, :, cols + HALO_COLS :] = right[:, span, :]


def pack_rows(fields, left, right):
    edge = jax.ShapeDtypeStruct((4, HALO_ROWS, fields.shape[2] + 2 * HALO_COLS), F32)
    vmem = pl.BlockSpec(memory_space=pltpu.VMEM)
    return pl.pallas_call(
        rows_kernel,
        out_shape=[edge, edge],
        in_specs=[vmem] * 3,
        out_specs=[vmem] * 2,
        compiler_params=pltpu.CompilerParams(vmem_limit_bytes=8 * 1024 * 1024),
        name="pack_rows",
    )(fields, left, right)


class Level:
    def __init__(self, matrix, names_at, inverse, spill):
        self.matrix, self.names_at, self.inverse, self.spill = matrix, names_at, inverse, spill
        self.count = matrix.shape[1]

    def entry(self, name, m, k):
        at = self.names_at.get(name)
        return None if at is None else self.matrix[at, m, k]

    def stress(self, m, k, modes):
        names = "123rc"
        known = {}
        result = []
        for i in range(5):
            terms = []
            for j in range(5):
                name = names[min(i, j)] + names[max(i, j)]
                if name not in known:
                    known[name] = self.entry(name, m, k)
                if known[name] is not None:
                    terms.append(known[name] * modes[j])
            result.append(plus(*terms))
        return result

    def halves(self, component, m, k):
        if component == 0:
            names = ("11", "33", "rr", "13", "1r", "3r")
        else:
            names = ("22", "33", "cc", "23", "3c", "2c")
        first, second, third, cross, by_col, by_row = [self.entry(name, m, k) for name in names]
        base = first + second + third
        by_row, by_col, cross = 2.0 * by_row, 2.0 * by_col, times(2.0, cross)
        if cross is None:
            return base - by_row, base + by_row, by_col, by_col
        return base - by_row, base + by_row, by_col - cross, by_col + cross

    def components(self):
        return (0, 1)

    def make_inverse(self, row_ok, col_ok):
        count = self.count
        for component in self.components():
            kept = {}
            for k in range(count):
                parts = [self.halves(component, m, k) for m in range(count)]
                for m in range(count):
                    above = parts[m - 1] if m else parts[count - 1]
                    lower = [above[1], above[3]]
                    if m == 0:
                        lower = [from_before(value, 0) for value in lower]
                    even, odd = parts[m][0] + lower[0], parts[m][2] + lower[1]
                    kept[m, k] = (even - odd, even + odd)
            for k in range(count):
                for m in range(count):
                    left = kept[m, k - 1][1] if k else from_before(kept[m, count - 1][1], 1)
                    diagonal = kept[m, k][0] + left
                    value = jnp.where(diagonal > 0.0, 0.5 / diagonal, 0.0)
                    if m == 0:
                        value = value * row_ok
                    if k == 0:
                        value = value * col_ok
                    self.inverse[component, m, k] = value


class FineLevel(Level):
    def stress(self, m, k, modes):
        lame, shear, mixed = self.matrix[0, m, k], self.matrix[1, m, k], self.matrix[2, m, k]
        first, second, third, bend_row, bend_col = modes
        twice, mean = shear + shear, lame * (first + second)
        return [
            mean + twice * first,
            mean + twice * second,
            shear * third,
            mixed * bend_row,
            mixed * bend_col,
        ]

    def components(self):
        return (0,)

    def make_inverse(self, row_ok, col_ok):
        count = self.count

        @pl.loop(0, count)
        def _(k):
            parts = [self.matrix[2, m, k] for m in range(count)]
            for m in range(count):
                above = parts[m - 1] if m else from_before(parts[count - 1], 0)
                self.inverse[0, m, k] = parts[m] + above

        for m in range(count):
            left = from_before(self.inverse[0, m, count - 1], 1)
            for k in range(count):
                here = self.inverse[0, m, k]
                diagonal = 4.0 * (here + left)
                left = here
                value = jnp.where(diagonal > 0.0, 0.5 / diagonal, 0.0)
                if m == 0:
                    value = value * row_ok
                if k == 0:
                    value = value * col_ok
                self.inverse[0, m, k] = value


def inverse_of(level, component, m, k):
    return level.inverse[min(component, len(level.components()) - 1), m, k]


def close_columns(level, x):
    count = level.count
    for component in (0, 1):
        for m in range(count):
            x[component, m, count] = from_after(x[component, m, 0], 1)


def start(level, x, source):
    count = level.count

    def column(k):
        for component in (0, 1):
            for m in range(count):
                x[component, m, k] = source[component, m, k] * inverse_of(level, component, m, k)

    over_columns(count, column)
    close_columns(level, x)


def over_columns(count, column):
    if count > 2:
        pl.loop(0, count)(column)
    else:
        for k in range(count):
            column(k)


def apply(level, x, source, out, residual):
    count, spill = level.count, level.spill
    spill[...] = jnp.zeros_like(spill)

    def column(k):
        sums, steps = [], []
        for m in range(count):
            here = [x[component, m, k] for component in (0, 1)]
            after = [x[component, m, k + 1] for component in (0, 1)]
            sums.append([here[c] + after[c] for c in (0, 1)])
            steps.append([after[c] - here[c] for c in (0, 1)])
        sums.append([from_after(value, 0) for value in sums[0]])
        steps.append([from_after(value, 0) for value in steps[0]])
        own, passed = [], []
        for m in range(count):
            modes = (
                sums[m + 1][0] - sums[m][0],
                steps[m][1] + steps[m + 1][1],
                (steps[m][0] + steps[m + 1][0]) + (sums[m + 1][1] - sums[m][1]),
                steps[m + 1][0] - steps[m][0],
                steps[m + 1][1] - steps[m][1],
            )
            first, second, third, bend_row, bend_col = level.stress(m, k, modes)
            own.append((first, third - bend_row, third, second - bend_col))
            passed.append((first, third + bend_row, third, second + bend_col))
        for m in range(count):
            above = passed[m - 1] if m else [from_before(value, 0) for value in passed[count - 1]]
            for component in (0, 1):
                at = 2 * component
                even = above[at] - own[m][at]
                odd = above[at + 1] + own[m][at + 1]
                left = spill[component, m]
                spill[component, m] = even + odd
                rest = source[component, m, k] - ((even - odd) + left)
                if not residual:
                    rest = x[component, m, k] + inverse_of(level, component, m, k) * rest
                out[component, m, k] = rest

    over_columns(count, column)
    for component in (0, 1):
        for m in range(count):
            left = from_before(spill[component, m], 1)
            if not residual:
                left = left * inverse_of(level, component, m, 0)
            out[component, m, 0] = out[component, m, 0] - left
    if not residual:
        close_columns(level, out)


def restrict(residual, target, count):
    half = count // 2
    for component in (0, 1):
        for k in range(half):
            lines = []
            for m in range(count):
                odd = residual[component, m, 2 * k + 1]
                if k:
                    before = residual[component, m, 2 * k - 1]
                else:
                    before = from_before(residual[component, m, count - 1], 1)
                lines.append(residual[component, m, 2 * k] + 0.5 * (odd + before))
            for m in range(half):
                before = lines[2 * m - 1] if m else from_before(lines[count - 1], 0)
                target[component, m, k] = lines[2 * m] + 0.5 * (lines[2 * m + 1] + before)


def prolong(coarse, before, x, count):
    half = count // 2
    for component in (0, 1):
        planes = {(m, k): coarse(component, m, k) for m in range(half) for k in range(half)}
        for m in range(half):
            planes[m, half] = from_after(planes[m, 0], 1)
        for k in range(half + 1):
            planes[half, k] = from_after(planes[0, k], 0)
        for m in range(half):
            for k in range(half):
                a, b, c, d = planes[m, k], planes[m + 1, k], planes[m, k + 1], planes[m + 1, k + 1]
                x[component, 2 * m, 2 * k] = before[component, 2 * m, 2 * k] + a
                x[component, 2 * m + 1, 2 * k] = before[component, 2 * m + 1, 2 * k] + 0.5 * (a + b)
                x[component, 2 * m, 2 * k + 1] = before[component, 2 * m, 2 * k + 1] + 0.5 * (a + c)
                x[component, 2 * m + 1, 2 * k + 1] = before[component, 2 * m + 1, 2 * k + 1] + 0.25 * ((a + b) + (c + d))


def haar(level, names_at, m, k):
    def signed(name, row, col):
        if name not in names_at:
            return None
        value = {
            (a, b): level.matrix[names_at[name], 2 * m + a, 2 * k + b] for a in (0, 1) for b in (0, 1)
        }
        low = value[0, 1] - value[0, 0] if col else value[0, 1] + value[0, 0]
        high = value[1, 1] - value[1, 0] if col else value[1, 1] + value[1, 0]
        return high - low if row else high + low

    return signed


def coarsen_fine(fine, coarse):
    count = coarse.count

    def column(k):
        for m in range(count):
            signed = haar(fine, {"l": 0, "s": 1}, m, k)
            lame, shear = signed("l", 0, 0), signed("s", 0, 0)
            lame_row, shear_row = signed("l", 1, 0), signed("s", 1, 0)
            lame_col, shear_col = signed("l", 0, 1), signed("s", 0, 1)
            lame_both, shear_both = signed("l", 1, 1), signed("s", 1, 1)
            values = {
                "11": 0.25 * (lame + 2.0 * shear),
                "12": 0.25 * lame,
                "33": 0.25 * shear,
                "1r": 0.125 * (lame_col + 2.0 * shear_col),
                "2r": 0.125 * lame_col,
                "3r": 0.125 * shear_row,
                "1c": 0.125 * lame_row,
                "2c": 0.125 * (lame_row + 2.0 * shear_row),
                "3c": 0.125 * shear_col,
                "rr": (lame + 3.0 * shear) * (1.0 / 12.0),
                "rc": 0.0625 * (lame_both + shear_both),
            }
            for name, value in values.items():
                coarse.matrix[FIRST_AT[name], m, k] = value

    over_columns(count, column)


def coarsen(fine, write, count):
    for k in range(count):
        for m in range(count):
            signed = haar(fine, fine.names_at, m, k)

            def total(name):
                return signed(name, 0, 0)

            def by_row(name):
                return signed(name, 1, 0)

            def by_col(name):
                return signed(name, 0, 1)

            def by_both(name):
                return signed(name, 1, 1)

            values = {}
            for name in ("11", "12", "33"):
                values[name] = times(0.25, total(name))
            for i in "123":
                one, two, three = ["".join(sorted(i + j)) for j in "123"]
                values[i + "r"] = 0.125 * plus(by_col(one), by_row(three), total(i + "r"))
                values[i + "c"] = 0.125 * plus(by_row(two), by_col(three), total(i + "c"))
            values["rr"] = 0.0625 * plus(
                total("11"),
                total("33"),
                times(2.0, by_both("13")),
                2.0 * (by_col("1r") + by_row("3r")),
                total("rr"),
            )
            values["cc"] = 0.0625 * plus(
                total("22"),
                total("33"),
                times(2.0, by_both("23")),
                2.0 * (by_row("2c") + by_col("3c")),
                total("cc"),
            )
            values["rc"] = 0.0625 * plus(
                by_both("12"),
                total("13"),
                total("23"),
                by_both("33"),
                by_col("1c"),
                by_row("3c"),
                by_row("2r"),
                by_col("3r"),
                total("rc"),
            )
            for name in FULL:
                write(FULL_AT[name], m, k, values[name])


def edge_masks(place, shape, rows, cols, first_row, grid_rows, grid_cols):
    row = lax.broadcasted_iota(jnp.int32, shape, 0) * GROUP + (place[0] * rows + first_row)
    col = lax.broadcasted_iota(jnp.int32, shape, 1) * GROUP + (place[1] * cols - HALO_COLS)
    return (
        jnp.where(row < grid_rows, 1.0, 0.0).astype(F32),
        jnp.where(col < grid_cols, 1.0, 0.0).astype(F32),
    )


def three_parts(value):
    high = value.astype(BF16)
    rest = value - high.astype(F32)
    middle = rest.astype(BF16)
    low = (rest - middle.astype(F32)).astype(BF16)
    return high, middle, low


def down_kernel(
    place, fields, left, right, upper, lower, factor,
    matrix0, inverse0, source0, x0, matrix1, inverse1, source1, x1, matrix2, inverse2, source2, x2, coarsest,
    tiles, stacked, spread, other0, other1, other2, spill0, spill1, spill2, matrix3,
    *, rows, cols, gx, gy,
):
    tall, wide = rows + 2 * HALO_ROWS, cols + 2 * HALO_COLS
    side = tall // GROUP
    row_ok, col_ok = edge_masks(place, (side, LANES), rows, cols, -HALO_ROWS, gx * rows, gy * cols)

    for tile in range(wide // LANES):
        at = lax.broadcasted_iota(jnp.int32, (LANES, GROUP * LANES), 0) + tile * LANES
        if tile < cols // LANES:
            at = at + HALO_COLS
        elif tile == cols // LANES:
            at = at - cols
        target = (at & (GROUP - 1)) * LANES + (at >> LEVELS)
        lane = lax.broadcasted_iota(jnp.int32, (LANES, GROUP * LANES), 1)
        spread[tile * LANES : (tile + 1) * LANES, :] = jnp.where(lane == target, 1.0, 0.0).astype(BF16)

    for field in range(4):
        for tile in range(wide // LANES):
            lanes = slice(tile * LANES, (tile + 1) * LANES)
            if tile < cols // LANES:
                middle = fields[field, :, lanes]
            else:
                middle = (left if tile == cols // LANES else right)[field]
            parts = [
                (slice(0, HALO_ROWS), upper[field, :, lanes]),
                (slice(HALO_ROWS, HALO_ROWS + rows), middle),
                (slice(HALO_ROWS + rows, tall), lower[field, :, lanes]),
            ]
            for span, value in parts:
                if field < 2:
                    value = value * (0.25 * factor[tile, span, :])
                tiles[tile, span, :] = value
        for m in range(GROUP):
            for tile in range(wide // LANES):
                lanes = slice(tile * LANES, (tile + 1) * LANES)
                for part, value in enumerate(three_parts(tiles[tile, pl.ds(m, side, stride=GROUP), :])):
                    stacked[part * tall + m * side : part * tall + (m + 1) * side, lanes] = value
        for pair in range(GROUP // 2):
            lanes = slice(pair * 2 * LANES, (pair + 1) * 2 * LANES)
            product = jnp.dot(stacked[...], spread[:, lanes], preferred_element_type=F32)
            product = product[:tall] + product[tall : 2 * tall] + product[2 * tall :]
            for m in range(GROUP):
                for half in (0, 1):
                    plane = product[m * side : (m + 1) * side, half * LANES : (half + 1) * LANES]
                    if field < 2:
                        matrix0[field, m, 2 * pair + half] = plane
                    else:
                        source0[field - 2, m, 2 * pair + half] = plane

    def mix(k):
        for m in range(GROUP):
            matrix0[2, m, k] = matrix0[0, m, k] * (1.0 / 3.0) + matrix0[1, m, k]

    over_columns(GROUP, mix)

    level0 = FineLevel(matrix0, {}, inverse0, spill0)
    level1 = Level(matrix1, FIRST_AT, inverse1, spill1)
    level2 = Level(matrix2, FULL_AT, inverse2, spill2)

    coarsen_fine(level0, level1)

    def write2(at, m, k, value):
        matrix2[at, m, k] = value

    coarsen(level1, write2, level2.count)

    def write3(at, m, k, value):
        matrix3[at] = value

    coarsen(level2, write3, 1)
    for level in (level0, level1, level2):
        level.make_inverse(row_ok, col_ok)

    source3 = matrix3.at[pl.ds(len(FULL), 2)]
    chain = (
        (level0, source0, x0, other0, source1),
        (level1, source1, x1, other1, source2),
        (level2, source2, x2, other2, None),
    )
    for level, source, x, other, target in chain:
        start(level, other, source)
        apply(level, other, source, x, residual=False)
        apply(level, x, source, other, residual=True)
        if target is not None:
            restrict(other, target, level.count)
        else:
            restrict_last(other, source3)
    first = HALO_ROWS // GROUP
    for at in range(len(FULL) + 2):
        coarsest[at] = matrix3[at, first : first + rows // GROUP, :]


def restrict_last(residual, target):
    class Planes:
        def __setitem__(self, where, value):
            target[where[0]] = value

    restrict(residual, Planes(), 2)


def up_kernel(
    place, coarse, coarse_before, coarse_after,
    matrix0, inverse0, source0, x0_in, matrix1, inverse1, source1, x1_in, matrix2, inverse2, source2, x2_in,
    displacement,
    x0, other0, x1, other1, x2, other2, spill0, spill1, spill2, spill3, matrix3, inverse3, source3, x3, other3,
    stacked, gathered, tiles,
    *, rows, cols, gx, gy,
):
    block = rows // GROUP
    for at in range(len(FULL) + 2):
        for piece, part in enumerate((coarse_before, coarse, coarse_after)):
            if at < len(FULL):
                matrix3[at, 0, 0, piece * block : (piece + 1) * block, :] = part[at]
            else:
                source3[at - len(FULL), 0, 0, piece * block : (piece + 1) * block, :] = part[at]
    level3 = Level(matrix3, FULL_AT, inverse3, spill3)
    level3.make_inverse(*edge_masks(place, (3 * block, LANES), rows, cols, -rows, gx * rows, gy * cols))
    start(level3, x3, source3)
    now, then = x3, other3
    for _ in range(COARSE_SWEEPS - 1):
        apply(level3, now, source3, then, residual=False)
        now, then = then, now
    offset = block - HALO_ROWS // GROUP
    side = (rows + 2 * HALO_ROWS) // GROUP
    coarse_plane = functools.partial(cut_plane, now, offset, side)

    level0 = FineLevel(matrix0, {}, inverse0, spill0)
    level1 = Level(matrix1, FIRST_AT, inverse1, spill1)
    level2 = Level(matrix2, FULL_AT, inverse2, spill2)
    for level, source, before, x, other in (
        (level2, source2, x2_in, x2, other2),
        (level1, source1, x1_in, x1, other1),
        (level0, source0, x0_in, x0, other0),
    ):
        prolong(coarse_plane, before, x, level.count)
        close_columns(level, x)
        apply(level, x, source, other, residual=False)
        apply(level, other, source, x, residual=False)
        coarse_plane = functools.partial(whole_plane, x)

    for tile in range(cols // LANES):
        at = lax.broadcasted_iota(jnp.int32, (GROUP * LANES, LANES), 1) + tile * LANES + HALO_COLS
        target = (at & (GROUP - 1)) * LANES + (at >> LEVELS)
        line = lax.broadcasted_iota(jnp.int32, (GROUP * LANES, LANES), 0)
        gathered[:, tile * LANES : (tile + 1) * LANES] = jnp.where(line == target, 1.0, 0.0).astype(BF16)
    first = HALO_ROWS // GROUP
    for component in (0, 1):
        for pair in range(GROUP // 2):
            for k in range(GROUP):
                value = jnp.concatenate(
                    [x0[component, 2 * pair + h, k, first : first + block, :] for h in (0, 1)], axis=0
                )
                for part, piece in enumerate(three_parts(value)):
                    line = part * 2 * rows + component * rows + pair * 2 * block
                    stacked[line : line + 2 * block, k * LANES : (k + 1) * LANES] = piece
    product = jnp.dot(stacked[...], gathered[...], preferred_element_type=F32)
    product = product[: 2 * rows] + product[2 * rows : 4 * rows] + product[4 * rows :]
    for component in (0, 1):
        for tile in range(cols // LANES):
            lanes = slice(tile * LANES, (tile + 1) * LANES)
            for m in range(GROUP):
                line = component * rows + m * block
                tiles[component, tile, pl.ds(m, block, stride=GROUP), :] = product[line : line + block, lanes]
            displacement[component, :, lanes] = tiles[component, tile]


def cut_plane(x, offset, side, component, m, k):
    return x[component, 0, 0, offset : offset + side, :]


def whole_plane(x, component, m, k):
    return x[component, m, k]


def body(first_lame, shear_modulus, applied_load, plastic_owner, plastic_cell, plastic_code):
    rows, cols = first_lame.shape
    gx, gy = lax.axis_size("gx"), lax.axis_size("gy")
    devices = gx * gy
    place = jnp.stack([lax.axis_index("gx"), lax.axis_index("gy")]).astype(jnp.int32)

    fields, first_cols, last_cols, words = pack(
        first_lame, shear_modulus, applied_load, plastic_owner, plastic_cell, plastic_code, devices
    )
    left = passed_along(last_cols, "gy", 1)
    right = passed_along(first_cols, "gy", -1)
    words = lax.all_to_all(words, ("gx", "gy"), 0, 0, tiled=True).reshape(devices, -1)

    last_rows, first_rows = pack_rows(fields, left, right)
    upper = passed_along(last_rows, "gx", 1)
    lower = passed_along(first_rows, "gx", -1)
    factor = yield_factor(place, words, rows, cols, gy)

    tall, wide = rows + 2 * HALO_ROWS, cols + 2 * HALO_COLS
    side = tall // GROUP
    vmem, smem = pl.BlockSpec(memory_space=pltpu.VMEM), pl.BlockSpec(memory_space=pltpu.SMEM)

    def planes(fields, count, extra=0, lines=side):
        return (fields, count, count + extra, lines, LANES)

    state = []
    for count, entries, inverses in ((GROUP, 3, 1), (GROUP // 2, len(FIRST), 2), (GROUP // 4, len(FULL), 2)):
        state += [planes(entries, count), planes(inverses, count), planes(2, count), planes(2, count, 1)]
    held = len(FULL) + 2
    counts = (GROUP, GROUP // 2, GROUP // 4)
    *state, coarse = pl.pallas_call(
        functools.partial(down_kernel, rows=rows, cols=cols, gx=gx, gy=gy),
        out_shape=[jax.ShapeDtypeStruct(shape, F32) for shape in state]
        + [jax.ShapeDtypeStruct((held, rows // GROUP, LANES), F32)],
        in_specs=[smem] + [vmem] * 6,
        out_specs=[vmem] * (len(state) + 1),
        scratch_shapes=[
            pltpu.VMEM((wide // LANES, tall, LANES), F32),
            pltpu.VMEM((3 * tall, wide), BF16),
            pltpu.VMEM((wide, GROUP * LANES), BF16),
        ]
        + [pltpu.VMEM(planes(2, count, 1), F32) for count in counts]
        + [pltpu.VMEM((2, count, side, LANES), F32) for count in counts]
        + [pltpu.VMEM((held, side, LANES), F32)],
        compiler_params=pltpu.CompilerParams(vmem_limit_bytes=VMEM_LIMIT),
        name="descent",
    )(place, fields, left, right, upper, lower, factor)

    coarse_before = passed_along(coarse, "gx", 1)
    coarse_after = passed_along(coarse, "gx", -1)
    lines = 3 * (rows // GROUP)
    return pl.pallas_call(
        functools.partial(up_kernel, rows=rows, cols=cols, gx=gx, gy=gy),
        out_shape=jax.ShapeDtypeStruct((2, rows, cols), F32),
        in_specs=[smem] + [vmem] * (3 + len(state)),
        out_specs=vmem,
        scratch_shapes=[
            shape
            for count in counts
            for shape in (pltpu.VMEM(planes(2, count, 1), F32),) * 2
        ]
        + [pltpu.VMEM((2, count, side, LANES), F32) for count in counts]
        + [
            pltpu.VMEM((2, 1, lines, LANES), F32),
            pltpu.VMEM(planes(len(FULL), 1, 0, lines), F32),
            pltpu.VMEM(planes(2, 1, 0, lines), F32),
            pltpu.VMEM(planes(2, 1, 0, lines), F32),
            pltpu.VMEM(planes(2, 1, 1, lines), F32),
            pltpu.VMEM(planes(2, 1, 1, lines), F32),
            pltpu.VMEM((6 * rows, GROUP * LANES), BF16),
            pltpu.VMEM((GROUP * LANES, cols), BF16),
            pltpu.VMEM((2, cols // LANES, rows, LANES), F32),
        ],
        compiler_params=pltpu.CompilerParams(vmem_limit_bytes=VMEM_LIMIT),
        name="ascent",
    )(place, coarse, coarse_before, coarse_after, *state)


def solution(mesh):
    return jax.shard_map(
        body,
        mesh=mesh,
        in_specs=(
            P("gx", "gy"),
            P("gx", "gy"),
            P(None, "gx", "gy"),
            P(("gx", "gy"), None),
            P(("gx", "gy")),
            P(("gx", "gy")),
        ),
        out_specs=P(None, "gx", "gy"),
        check_vma=False,
    )
```

```python
import functools
import math

import jax
import jax.numpy as jnp
import numpy as np
from jax import lax
from jax.experimental import pallas as pl
from jax.experimental.pallas import tpu as pltpu
from jax.sharding import PartitionSpec as P

LEVELS = 3
SWEEPS = 2
COARSE_SWEEPS = 6
YIELD_DROP = 0.6
GROUP = 1 << LEVELS
HALO_ROWS = 32
HALO_COLS = 128
LANES = 128
WIDE = 2 * LANES
SPAN = WIDE // GROUP
LISTS_AT_ONCE = 16
VMEM_LIMIT = 30 * 1024 * 1024
F32 = jnp.float32
BF16 = jnp.bfloat16

FIRST = ("11", "12", "33", "1r", "2r", "3r", "1c", "2c", "3c", "rr", "rc")
FULL = FIRST + ("cc",)
FIRST_AT = {name: FIRST.index(name) for name in FIRST} | {"22": 0, "cc": FIRST.index("rr")}
FULL_AT = {name: FULL.index(name) for name in FULL} | {"22": 0}


def passed_along(array, axis, by):
    devices = lax.axis_size(axis)
    pairs = [(i, i + by) for i in range(devices) if 0 <= i + by < devices]
    return lax.ppermute(array, axis, pairs)


def log2(number):
    power = number.bit_length() - 1
    assert 1 << power == number
    return power


def from_before(value, axis):
    return pltpu.roll(value, 1, axis)


def from_after(value, axis):
    return pltpu.roll(value, value.shape[axis] - 1, axis)


def plus(*terms):
    total = None
    for term in terms:
        if term is not None:
            total = term if total is None else total + term
    return total


def times(weight, term):
    return None if term is None else weight * term


def factor_kernel(place, words, factor, tall_of, lane_of, codes, counts, *, rows, cols, gy):
    for at in range(words.shape[0]):
        tall_of[at : at + 1, :] = words[at]
    word = tall_of[...]
    cell_bits = log2(rows * cols)
    owner = word >> (cell_bits + 2)
    cell = (word >> 2) & (rows * cols - 1)
    row = (owner >> log2(gy)) * rows + (cell >> log2(cols)) - place[0] * rows
    col = (owner & (gy - 1)) * cols + (cell & (cols - 1)) - place[1] * cols
    tall = rows + 2 * HALO_ROWS
    side = tall // GROUP
    inside = (row >= -HALO_ROWS) & (row < rows + HALO_ROWS) & (col >= -HALO_COLS) & (col < cols + HALO_COLS)
    at = jnp.where(col < 0, col + cols + HALO_COLS, jnp.where(col >= cols, col + HALO_COLS, col))
    line = (row & (GROUP - 1)) * side + ((row >> LEVELS) & (side - 1))
    tall_of[...] = jnp.where(inside, line + tall * (at >> log2(WIDE)), -1)
    lane_of[...] = (at & (GROUP - 1)) * SPAN + ((at & (WIDE - 1)) >> LEVELS)
    codes[...] = (word & 3).astype(F32)
    counts[...] = jnp.zeros_like(counts)
    length = words.shape[2]
    group = min(LISTS_AT_ONCE, words.shape[0])

    @pl.loop(0, words.shape[0] // group)
    def _(i):
        tall_id = lax.broadcasted_iota(jnp.int32, (counts.shape[0], length), 0)
        lane_id = lax.broadcasted_iota(jnp.int32, (WIDE, length), 0)
        by_tall, by_lane = [], []
        for j in range(group):
            line = pl.ds(i * group + j, 1)
            by_tall.append(jnp.where(tall_id == tall_of[line, :], codes[line, :], 0.0).astype(BF16))
            by_lane.append(jnp.where(lane_id == lane_of[line, :], 1.0, 0.0).astype(BF16))
        counts[...] += lax.dot_general(
            jnp.concatenate(by_tall, axis=1),
            jnp.concatenate(by_lane, axis=1),
            (((1,), (1,)), ((), ())),
            preferred_element_type=F32,
        )

    for m in range(GROUP):
        for k in range(GROUP):
            half, slot = k * SPAN // LANES, k * SPAN % LANES
            lanes = slice(half * LANES, (half + 1) * LANES)
            lines = range(m * side, counts.shape[0], tall)
            count = gather_lanes([counts[line : line + side, lanes] for line in lines], slot)
            factor[m, k] = jnp.exp(count * math.log(YIELD_DROP))


def yield_factor(place, words, rows, cols, gy):
    tall, wide = rows + 2 * HALO_ROWS, cols + 2 * HALO_COLS
    lists = (words.shape[0], words.shape[2])
    return pl.pallas_call(
        functools.partial(factor_kernel, rows=rows, cols=cols, gy=gy),
        out_shape=jax.ShapeDtypeStruct((GROUP, GROUP, tall // GROUP, LANES), F32),
        in_specs=[
            pl.BlockSpec(memory_space=pltpu.SMEM),
            pl.BlockSpec(memory_space=pltpu.VMEM),
        ],
        out_specs=pl.BlockSpec(memory_space=pltpu.VMEM),
        scratch_shapes=[
            pltpu.VMEM(lists, jnp.int32),
            pltpu.VMEM(lists, jnp.int32),
            pltpu.VMEM(lists, F32),
            pltpu.VMEM((tall * wide // WIDE, WIDE), F32),
        ],
        compiler_params=pltpu.CompilerParams(vmem_limit_bytes=VMEM_LIMIT),
        cost_estimate=pl.CostEstimate(
            flops=2 * tall * wide * words.size, bytes_accessed=4 * words.size, transcendentals=tall * wide
        ),
        name="yield_factor",
    )(place, words)


def pack_kernel(
    first_lame, shear_modulus, applied_load, owner, cell, code,
    fields, first_cols, last_cols, words, lists, copied, arrived,
    *, cells,
):
    copies = [
        pltpu.make_async_copy(source, target, arrived.at[at])
        for at, (source, target) in enumerate(
            (
                (owner, lists.at[0]),
                (cell, lists.at[1]),
                (code, lists.at[2]),
                (first_lame, fields.at[0]),
                (shear_modulus, fields.at[1]),
                (applied_load, fields.at[pl.ds(2, 2)]),
            )
        )
    ]
    for copy in copies:
        copy.start()
    for copy in copies[:3]:
        copy.wait()
    word = (lists[0] * cells + lists[1]) * 4 + lists[2]
    for device in range(words.shape[0]):
        copied[device] = word
    sent = pltpu.make_async_copy(copied, words, arrived.at[6])
    sent.start()
    for copy in copies[3:]:
        copy.wait()
    first_cols[...] = fields[:, :, :HALO_COLS]
    last_cols[...] = fields[:, :, fields.shape[2] - HALO_COLS :]
    sent.wait()


def pack(first_lame, shear_modulus, applied_load, owner, cell, code, devices):
    rows, cols = first_lame.shape
    edge = jax.ShapeDtypeStruct((4, rows, HALO_COLS), F32)
    length = cell.shape[0]
    arrays = [first_lame, shear_modulus, applied_load] + [part.reshape(1, -1) for part in (owner, cell, code)]
    hbm, vmem = pl.BlockSpec(memory_space=pltpu.HBM), pl.BlockSpec(memory_space=pltpu.VMEM)
    return pl.pallas_call(
        functools.partial(pack_kernel, cells=rows * cols),
        out_shape=[
            jax.ShapeDtypeStruct((4, rows, cols), F32),
            edge,
            edge,
            jax.ShapeDtypeStruct((devices, 1, length), jnp.int32),
        ],
        in_specs=[hbm] * 6,
        out_specs=[vmem] * 3 + [hbm],
        scratch_shapes=[
            pltpu.VMEM((3, 1, length), jnp.int32),
            pltpu.VMEM((devices, 1, length), jnp.int32),
            pltpu.SemaphoreType.DMA((7,)),
        ],
        compiler_params=pltpu.CompilerParams(vmem_limit_bytes=8 * 1024 * 1024),
        name="pack",
    )(*[pltpu.with_memory_space_constraint(array, pltpu.HBM) for array in arrays])


def rows_kernel(fields, left, right, last_rows, first_rows):
    cols = fields.shape[2]
    for out, start in ((last_rows, fields.shape[1] - HALO_ROWS), (first_rows, 0)):
        span = slice(start, start + HALO_ROWS)
        out[:, :, :cols] = fields[:, span, :]
        out[:, :, cols : cols + HALO_COLS] = left[:, span, :]
        out[:, :, cols + HALO_COLS :] = right[:, span, :]


def pack_rows(fields, left, right):
    edge = jax.ShapeDtypeStruct((4, HALO_ROWS, fields.shape[2] + 2 * HALO_COLS), F32)
    vmem = pl.BlockSpec(memory_space=pltpu.VMEM)
    return pl.pallas_call(
        rows_kernel,
        out_shape=[edge, edge],
        in_specs=[vmem] * 3,
        out_specs=[vmem] * 2,
        compiler_params=pltpu.CompilerParams(vmem_limit_bytes=8 * 1024 * 1024),
        name="pack_rows",
    )(fields, left, right)


class Level:
    def __init__(self, matrix, names_at, inverse, spill):
        self.matrix, self.names_at, self.inverse, self.spill = matrix, names_at, inverse, spill
        self.count = matrix.shape[1]

    def entry(self, name, m, k, high):
        at = self.names_at.get(name)
        return None if at is None else self.matrix[at, m, k, :high, :]

    def stress(self, m, k, modes):
        names = "123rc"
        known = {}
        result = []
        for i in range(5):
            terms = []
            for j in range(5):
                name = names[min(i, j)] + names[max(i, j)]
                if name not in known:
                    known[name] = self.entry(name, m, k, modes[0].shape[0])
                if known[name] is not None:
                    terms.append(known[name] * modes[j])
            result.append(plus(*terms))
        return result

    def halves(self, component, m, k):
        if component == 0:
            names = ("11", "33", "rr", "13", "1r", "3r")
        else:
            names = ("22", "33", "cc", "23", "3c", "2c")
        first, second, third, cross, by_col, by_row = [self.entry(name, m, k, self.matrix.shape[3]) for name in names]
        base = first + second + third
        by_row, by_col, cross = 2.0 * by_row, 2.0 * by_col, times(2.0, cross)
        if cross is None:
            return base - by_row, base + by_row, by_col, by_col
        return base - by_row, base + by_row, by_col - cross, by_col + cross

    def components(self):
        return (0, 1)

    def make_inverse(self, row_ok, col_ok):
        count = self.count
        for component in self.components():
            kept = {}
            for k in range(count):
                parts = [self.halves(component, m, k) for m in range(count)]
                for m in range(count):
                    above = parts[m - 1] if m else parts[count - 1]
                    lower = [above[1], above[3]]
                    if m == 0:
                        lower = [from_before(value, 0) for value in lower]
                    even, odd = parts[m][0] + lower[0], parts[m][2] + lower[1]
                    kept[m, k] = (even - odd, even + odd)
            for k in range(count):
                for m in range(count):
                    left = kept[m, k - 1][1] if k else from_before(kept[m, count - 1][1], 1)
                    diagonal = kept[m, k][0] + left
                    value = jnp.where(diagonal > 0.0, 0.5 / diagonal, 0.0)
                    if m == 0:
                        value = value * row_ok
                    if k == 0:
                        value = value * col_ok
                    self.inverse[component, m, k] = value


class FineLevel(Level):
    def stress(self, m, k, modes):
        lame, shear, mixed = [self.matrix[at, m, k, : modes[0].shape[0], :] for at in range(3)]
        first, second, third, bend_row, bend_col = modes
        twice, mean = shear + shear, lame * (first + second)
        return [
            mean + twice * first,
            mean + twice * second,
            shear * third,
            mixed * bend_row,
            mixed * bend_col,
        ]

    def components(self):
        return (0,)

    def make_inverse(self, row_ok, col_ok):
        count = self.count

        @pl.loop(0, count)
        def _(k):
            parts = [self.matrix[2, m, k] for m in range(count)]
            for m in range(count):
                above = parts[m - 1] if m else from_before(parts[count - 1], 0)
                self.inverse[0, m, k] = parts[m] + above

        for m in range(count):
            left = from_before(self.inverse[0, m, count - 1], 1)
            for k in range(count):
                here = self.inverse[0, m, k]
                diagonal = 4.0 * (here + left)
                left = here
                value = jnp.where(diagonal > 0.0, 0.5 / diagonal, 0.0)
                if m == 0:
                    value = value * row_ok
                if k == 0:
                    value = value * col_ok
                self.inverse[0, m, k] = value


def inverse_of(level, component, m, k, high):
    return level.inverse[min(component, len(level.components()) - 1), m, k, :high, :]


def close_columns(level, x):
    count = level.count
    for component in (0, 1):
        for m in range(count):
            x[component, m, count] = from_after(x[component, m, 0], 1)


def start(level, x, source):
    count = level.count

    def column(k):
        for component in (0, 1):
            for m in range(count):
                x[component, m, k] = source[component, m, k] * inverse_of(level, component, m, k, x.shape[3])

    over_columns(count, column)
    close_columns(level, x)


def over_columns(count, column):
    if count > 2:
        pl.loop(0, count)(column)
    else:
        for k in range(count):
            column(k)


def cut(value, height):
    return value if value.shape[0] == height else value[:height]


def apply(level, x, source, out, residual, tall_cells=None, tall_nodes=None):
    count, spill = level.count, level.spill
    side = x.shape[3]
    cells = [side if tall_cells is None or m in tall_cells else side // 2 for m in range(count)]
    nodes = [side if tall_nodes is None or m in tall_nodes else side // 2 for m in range(count)]
    held = [max(cells[m], cells[m - 1]) if m else side for m in range(count)]
    spill[...] = jnp.zeros_like(spill)

    def column(k):
        sums, steps = [], []
        for m in range(count):
            here = [x[component, m, k, : held[m], :] for component in (0, 1)]
            after = [x[component, m, k + 1, : held[m], :] for component in (0, 1)]
            sums.append([here[c] + after[c] for c in (0, 1)])
            steps.append([after[c] - here[c] for c in (0, 1)])
        sums.append([from_after(value, 0) for value in sums[0]])
        steps.append([from_after(value, 0) for value in steps[0]])
        own, passed = [], []
        for m in range(count):
            sum0, sum1 = [[cut(value, cells[m]) for value in sums[row]] for row in (m, m + 1)]
            step0, step1 = [[cut(value, cells[m]) for value in steps[row]] for row in (m, m + 1)]
            modes = (
                sum1[0] - sum0[0],
                step0[1] + step1[1],
                (step0[0] + step1[0]) + (sum1[1] - sum0[1]),
                step1[0] - step0[0],
                step1[1] - step0[1],
            )
            first, second, third, bend_row, bend_col = level.stress(m, k, modes)
            own.append((first, third - bend_row, third, second - bend_col))
            passed.append((first, third + bend_row, third, second + bend_col))
        for m in range(count):
            high = nodes[m]
            above = passed[m - 1] if m else [from_before(value, 0) for value in passed[count - 1]]
            for component in (0, 1):
                at = 2 * component
                even = cut(above[at], high) - cut(own[m][at], high)
                odd = cut(above[at + 1], high) + cut(own[m][at + 1], high)
                left = spill[component, m, :high, :]
                spill[component, m, :high, :] = even + odd
                rest = source[component, m, k, :high, :] - ((even - odd) + left)
                if not residual:
                    rest = x[component, m, k, :high, :] + inverse_of(level, component, m, k, high) * rest
                out[component, m, k, :high, :] = rest

    over_columns(count, column)
    for component in (0, 1):
        for m in range(count):
            high = nodes[m]
            left = from_before(spill[component, m, :high, :], 1)
            if not residual:
                left = left * inverse_of(level, component, m, 0, high)
            out[component, m, 0, :high, :] = out[component, m, 0, :high, :] - left
            if not residual:
                out[component, m, count, :high, :] = from_after(out[component, m, 0, :high, :], 1)


def restrict(residual, target, count):
    half = count // 2
    for component in (0, 1):
        for k in range(half):
            lines = []
            for m in range(count):
                odd = residual[component, m, 2 * k + 1]
                if k:
                    before = residual[component, m, 2 * k - 1]
                else:
                    before = from_before(residual[component, m, count - 1], 1)
                lines.append(residual[component, m, 2 * k] + 0.5 * (odd + before))
            for m in range(half):
                before = lines[2 * m - 1] if m else from_before(lines[count - 1], 0)
                target[component, m, k] = lines[2 * m] + 0.5 * (lines[2 * m + 1] + before)


def prolong(coarse, before, x, count):
    half = count // 2
    for component in (0, 1):
        planes = {(m, k): coarse(component, m, k) for m in range(half) for k in range(half)}
        for m in range(half):
            planes[m, half] = from_after(planes[m, 0], 1)
        for k in range(half + 1):
            planes[half, k] = from_after(planes[0, k], 0)
        for m in range(half):
            for k in range(half):
                a, b, c, d = planes[m, k], planes[m + 1, k], planes[m, k + 1], planes[m + 1, k + 1]
                x[component, 2 * m, 2 * k] = before[component, 2 * m, 2 * k] + a
                x[component, 2 * m + 1, 2 * k] = before[component, 2 * m + 1, 2 * k] + 0.5 * (a + b)
                x[component, 2 * m, 2 * k + 1] = before[component, 2 * m, 2 * k + 1] + 0.5 * (a + c)
                x[component, 2 * m + 1, 2 * k + 1] = before[component, 2 * m + 1, 2 * k + 1] + 0.25 * ((a + b) + (c + d))


def haar(level, names_at, m, k):
    def signed(name, row, col):
        if name not in names_at:
            return None
        value = {
            (a, b): level.matrix[names_at[name], 2 * m + a, 2 * k + b] for a in (0, 1) for b in (0, 1)
        }
        low = value[0, 1] - value[0, 0] if col else value[0, 1] + value[0, 0]
        high = value[1, 1] - value[1, 0] if col else value[1, 1] + value[1, 0]
        return high - low if row else high + low

    return signed


def coarsen_fine(fine, coarse):
    count = coarse.count

    def column(k):
        for m in range(count):
            signed = haar(fine, {"l": 0, "s": 1}, m, k)
            lame, shear = signed("l", 0, 0), signed("s", 0, 0)
            lame_row, shear_row = signed("l", 1, 0), signed("s", 1, 0)
            lame_col, shear_col = signed("l", 0, 1), signed("s", 0, 1)
            lame_both, shear_both = signed("l", 1, 1), signed("s", 1, 1)
            values = {
                "11": 0.25 * (lame + 2.0 * shear),
                "12": 0.25 * lame,
                "33": 0.25 * shear,
                "1r": 0.125 * (lame_col + 2.0 * shear_col),
                "2r": 0.125 * lame_col,
                "3r": 0.125 * shear_row,
                "1c": 0.125 * lame_row,
                "2c": 0.125 * (lame_row + 2.0 * shear_row),
                "3c": 0.125 * shear_col,
                "rr": (lame + 3.0 * shear) * (1.0 / 12.0),
                "rc": 0.0625 * (lame_both + shear_both),
            }
            for name, value in values.items():
                coarse.matrix[FIRST_AT[name], m, k] = value

    over_columns(count, column)


def coarsen(fine, write, count):
    for k in range(count):
        for m in range(count):
            signed = haar(fine, fine.names_at, m, k)

            def total(name):
                return signed(name, 0, 0)

            def by_row(name):
                return signed(name, 1, 0)

            def by_col(name):
                return signed(name, 0, 1)

            def by_both(name):
                return signed(name, 1, 1)

            values = {}
            for name in ("11", "12", "33"):
                values[name] = times(0.25, total(name))
            for i in "123":
                one, two, three = ["".join(sorted(i + j)) for j in "123"]
                values[i + "r"] = 0.125 * plus(by_col(one), by_row(three), total(i + "r"))
                values[i + "c"] = 0.125 * plus(by_row(two), by_col(three), total(i + "c"))
            values["rr"] = 0.0625 * plus(
                total("11"),
                total("33"),
                times(2.0, by_both("13")),
                2.0 * (by_col("1r") + by_row("3r")),
                total("rr"),
            )
            values["cc"] = 0.0625 * plus(
                total("22"),
                total("33"),
                times(2.0, by_both("23")),
                2.0 * (by_row("2c") + by_col("3c")),
                total("cc"),
            )
            values["rc"] = 0.0625 * plus(
                by_both("12"),
                total("13"),
                total("23"),
                by_both("33"),
                by_col("1c"),
                by_row("3c"),
                by_row("2r"),
                by_col("3r"),
                total("rc"),
            )
            for name in FULL:
                write(FULL_AT[name], m, k, values[name])


def edge_masks(place, shape, before, rows, cols, grid_rows, grid_cols):
    def wrapped(axis, ahead):
        at = lax.broadcasted_iota(jnp.int32, shape, axis)
        return jnp.where(at < shape[axis] - ahead, at, at - shape[axis]) * GROUP

    row = wrapped(0, before) + place[0] * rows
    col = wrapped(1, HALO_COLS // GROUP) + place[1] * cols
    return (
        jnp.where(row < grid_rows, 1.0, 0.0).astype(F32),
        jnp.where(col < grid_cols, 1.0, 0.0).astype(F32),
    )


def three_parts(value):
    high = value.astype(BF16)
    rest = value - high.astype(F32)
    middle = rest.astype(BF16)
    low = (rest - middle.astype(F32)).astype(BF16)
    return high, middle, low


def turned(value, by):
    return pltpu.roll(value, by % LANES, 1) if by % LANES else value


def gather_lanes(pieces, slot):
    lane = lax.broadcasted_iota(jnp.int32, pieces[0].shape, 1)
    halo = HALO_COLS // GROUP
    own = (len(pieces) - 1) * SPAN
    plane = jnp.where(lane >= LANES - halo, turned(pieces[-1], LANES - halo - slot), 0.0)
    plane = jnp.where(lane < own + halo, turned(pieces[-1], own - halo - slot), plane)
    for at in reversed(range(len(pieces) - 1)):
        plane = jnp.where(lane < (at + 1) * SPAN, turned(pieces[at], at * SPAN - slot), plane)
    return plane


def make_spread(spread):
    at = lax.broadcasted_iota(jnp.int32, (WIDE, WIDE), 0)
    lane = lax.broadcasted_iota(jnp.int32, (WIDE, WIDE), 1)
    spread[...] = jnp.where(lane == (at & (GROUP - 1)) * SPAN + (at >> LEVELS), 1.0, 0.0).astype(BF16)


def spread_fields(load, write, tiles, stacked, spread):
    fields, count, rows = tiles.shape[:3]
    block = rows // GROUP
    make_spread(spread)
    for field in range(fields):
        for tile in range(count):
            load(field, tile)
        for pair in range(GROUP // 2):
            for tile in range(count):
                lines = [tiles[field, tile, pl.ds(2 * pair + h, block, stride=GROUP), :] for h in (0, 1)]
                for part, split in enumerate(three_parts(jnp.concatenate(lines, axis=0))):
                    line = (field * 3 + part) * rows + pair * 2 * block
                    stacked[line : line + 2 * block, tile * LANES : (tile + 1) * LANES] = split
    for field in range(fields):
        pieces = []
        for piece in range(count * LANES // WIDE):
            left = stacked[field * 3 * rows : (field + 1) * 3 * rows, piece * WIDE : (piece + 1) * WIDE]
            product = jnp.dot(left, spread[...], preferred_element_type=F32)
            pieces.append(product[:rows] + product[rows : 2 * rows] + product[2 * rows :])
        for m in range(GROUP):
            for k in range(GROUP):
                half, slot = k * SPAN // LANES, k * SPAN % LANES
                lanes = slice(half * LANES, (half + 1) * LANES)
                lines = slice(m * block, (m + 1) * block)
                write(field, m, k, gather_lanes([piece[lines, lanes] for piece in pieces], slot))


def own_kernel(fields, left, right, planes, tiles, stacked, spread):
    own_tiles = fields.shape[2] // LANES

    def load(field, tile):
        if tile < own_tiles:
            tiles[field, tile] = fields[field, :, tile * LANES : (tile + 1) * LANES]
        else:
            tiles[field, tile] = (left if tile == own_tiles else right)[field]

    def write(field, m, k, plane):
        planes[field, m, k] = plane

    spread_fields(load, write, tiles, stacked, spread)


def spread_scratch(rows, wide):
    return [
        pltpu.VMEM((4, wide // LANES, rows, LANES), F32),
        pltpu.VMEM((12 * rows, wide), BF16),
        pltpu.VMEM((WIDE, WIDE), BF16),
    ]


def spread_own(fields, left, right):
    rows, wide = fields.shape[1], fields.shape[2] + 2 * HALO_COLS
    vmem = pl.BlockSpec(memory_space=pltpu.VMEM)
    return pl.pallas_call(
        own_kernel,
        out_shape=jax.ShapeDtypeStruct((4, GROUP, GROUP, rows // GROUP, LANES), F32),
        in_specs=[vmem] * 3,
        out_specs=vmem,
        scratch_shapes=spread_scratch(rows, wide),
        compiler_params=pltpu.CompilerParams(vmem_limit_bytes=12 * 1024 * 1024),
        cost_estimate=pl.CostEstimate(flops=24 * rows * wide * WIDE, bytes_accessed=0, transcendentals=0),
        name="spread_own",
    )(fields, left, right)


def down_kernel(
    place, own, upper, lower, factor,
    matrix0, inverse0, source0, x0, matrix1, inverse1, source1, x1, matrix2, inverse2, source2, x2, coarsest,
    tiles, stacked, spread, other0, other1, other2, spill0, spill1, spill2, matrix3,
    *, rows, cols, gx, gy,
):
    block = rows // GROUP
    side = block + 2 * HALO_ROWS // GROUP
    row_ok, col_ok = edge_masks(
        place, (side, LANES), HALO_ROWS // GROUP, rows, cols, gx * rows, gy * cols
    )

    def load(field, tile):
        lanes = slice(tile * LANES, (tile + 1) * LANES)
        tiles[field, tile, :HALO_ROWS] = lower[field, :, lanes]
        tiles[field, tile, HALO_ROWS:] = upper[field, :, lanes]

    def write(field, m, k, plane):
        if field < 2:
            matrix0[field, m, k, :block, :] = own[field, m, k] * (0.25 * factor[m, k, :block, :])
            matrix0[field, m, k, block:, :] = plane * (0.25 * factor[m, k, block:, :])
        else:
            source0[field - 2, m, k, :block, :] = own[field, m, k]
            source0[field - 2, m, k, block:, :] = plane

    spread_fields(load, write, tiles, stacked, spread)

    def mix(k):
        for m in range(GROUP):
            matrix0[2, m, k] = matrix0[0, m, k] * (1.0 / 3.0) + matrix0[1, m, k]

    over_columns(GROUP, mix)

    level0 = FineLevel(matrix0, {}, inverse0, spill0)
    level1 = Level(matrix1, FIRST_AT, inverse1, spill1)
    level2 = Level(matrix2, FULL_AT, inverse2, spill2)

    coarsen_fine(level0, level1)

    def write2(at, m, k, value):
        matrix2[at, m, k] = value

    coarsen(level1, write2, level2.count)

    def write3(at, m, k, value):
        matrix3[at] = value

    coarsen(level2, write3, 1)
    for level in (level0, level1, level2):
        level.make_inverse(row_ok, col_ok)

    source3 = matrix3.at[pl.ds(len(FULL), 2)]
    chain = (
        (level0, source0, x0, other0, source1),
        (level1, source1, x1, other1, source2),
        (level2, source2, x2, other2, None),
    )
    for level, source, x, other, target in chain:
        start(level, other, source)
        apply(level, other, source, x, residual=False)
        apply(level, x, source, other, residual=True)
        if target is not None:
            restrict(other, target, level.count)
        else:
            restrict_last(other, source3)
    for at in range(len(FULL) + 2):
        coarsest[at] = matrix3[at, :block, :]


def restrict_last(residual, target):
    class Planes:
        def __setitem__(self, where, value):
            target[where[0]] = value

    restrict(residual, Planes(), 2)


def up_kernel(
    place, coarse, coarse_before, coarse_after,
    matrix0, inverse0, source0, x0_in, matrix1, inverse1, source1, x1_in, matrix2, inverse2, source2, x2_in,
    displacement,
    x0, other0, x1, other1, x2, other2, spill0, spill1, spill2, spill3, matrix3, inverse3, source3, x3, other3,
    stacked, gathered, tiles,
    *, rows, cols, gx, gy,
):
    block = rows // GROUP
    for at in range(len(FULL) + 2):
        for piece, part in enumerate((coarse, coarse_after, coarse_before)):
            if at < len(FULL):
                matrix3[at, 0, 0, piece * block : (piece + 1) * block, :] = part[at]
            else:
                source3[at - len(FULL), 0, 0, piece * block : (piece + 1) * block, :] = part[at]
    level3 = Level(matrix3, FULL_AT, inverse3, spill3)
    level3.make_inverse(*edge_masks(place, (3 * block, LANES), block, rows, cols, gx * rows, gy * cols))
    start(level3, x3, source3)
    now, then = x3, other3
    for _ in range(COARSE_SWEEPS - 1):
        apply(level3, now, source3, then, residual=False)
        now, then = then, now
    coarse_plane = functools.partial(cut_plane, now, block)

    level0 = FineLevel(matrix0, {}, inverse0, spill0)
    level1 = Level(matrix1, FIRST_AT, inverse1, spill1)
    level2 = Level(matrix2, FULL_AT, inverse2, spill2)
    for level, source, before, x, other in (
        (level2, source2, x2_in, x2, other2),
        (level1, source1, x1_in, x1, other1),
        (level0, source0, x0_in, x0, other0),
    ):
        prolong(coarse_plane, before, x, level.count)
        close_columns(level, x)
        last = level.count - 1
        if level is level0:
            apply(level, x, source, other, False, {0, last - 1, last}, {0, last})
            apply(level, other, source, x, False, {last}, set())
        else:
            apply(level, x, source, other, residual=False)
            apply(level, other, source, x, residual=False)
        coarse_plane = functools.partial(whole_plane, x)

    at = lax.broadcasted_iota(jnp.int32, (WIDE, WIDE), 1)
    line = lax.broadcasted_iota(jnp.int32, (WIDE, WIDE), 0)
    gathered[...] = jnp.where(line == (at & (GROUP - 1)) * SPAN + (at >> LEVELS), 1.0, 0.0).astype(BF16)
    lane = lax.broadcasted_iota(jnp.int32, (2 * block, LANES), 1)
    for component in (0, 1):
        for pair in range(GROUP // 2):
            values = [
                jnp.concatenate(
                    [x0[component, 2 * pair + h, k, :block, :] for h in (0, 1)], axis=0
                )
                for k in range(GROUP)
            ]
            for piece in range(cols // WIDE):
                for half in range(WIDE // LANES):
                    slots = LANES // SPAN
                    value = None
                    for slot in reversed(range(slots)):
                        part = turned(values[half * slots + slot], (slot - piece) * SPAN)
                        value = part if value is None else jnp.where(lane < (slot + 1) * SPAN, part, value)
                    lanes = slice(piece * WIDE + half * LANES, piece * WIDE + (half + 1) * LANES)
                    for part, split in enumerate(three_parts(value)):
                        line = part * 2 * rows + component * rows + pair * 2 * block
                        stacked[line : line + 2 * block, lanes] = split
    pieces = []
    for piece in range(cols // WIDE):
        product = jnp.dot(
            stacked[:, piece * WIDE : (piece + 1) * WIDE], gathered[...], preferred_element_type=F32
        )
        pieces.append(product[: 2 * rows] + product[2 * rows : 4 * rows] + product[4 * rows :])
    for component in (0, 1):
        for tile in range(cols // LANES):
            lanes = slice(tile * LANES, (tile + 1) * LANES)
            for m in range(GROUP):
                line = component * rows + m * block
                tiles[component, tile, pl.ds(m, block, stride=GROUP), :] = pieces[tile * LANES // WIDE][
                    line : line + block, tile * LANES % WIDE : tile * LANES % WIDE + LANES
                ]
            displacement[component, :, lanes] = tiles[component, tile]


def cut_plane(x, block, component, m, k):
    line = lax.broadcasted_iota(jnp.int32, (block, LANES), 0)
    halo = jnp.where(
        line < HALO_ROWS // GROUP,
        x[component, 0, 0, block : 2 * block, :],
        x[component, 0, 0, 2 * block :, :],
    )
    return jnp.concatenate([x[component, 0, 0, :block, :], halo], axis=0)


def whole_plane(x, component, m, k):
    return x[component, m, k]


def body(first_lame, shear_modulus, applied_load, plastic_owner, plastic_cell, plastic_code):
    rows, cols = first_lame.shape
    gx, gy = lax.axis_size("gx"), lax.axis_size("gy")
    devices = gx * gy
    place = jnp.stack([lax.axis_index("gx"), lax.axis_index("gy")]).astype(jnp.int32)

    fields, first_cols, last_cols, words = pack(
        first_lame, shear_modulus, applied_load, plastic_owner, plastic_cell, plastic_code, devices
    )
    left = passed_along(last_cols, "gy", 1)
    right = passed_along(first_cols, "gy", -1)
    words = lax.all_to_all(words, ("gx", "gy"), 0, 0, tiled=True)

    last_rows, first_rows = pack_rows(fields, left, right)
    upper = passed_along(last_rows, "gx", 1)
    lower = passed_along(first_rows, "gx", -1)
    own = spread_own(fields, left, right)
    words, own = lax.optimization_barrier((words, own))
    factor = yield_factor(place, words, rows, cols, gy)

    tall, wide = rows + 2 * HALO_ROWS, cols + 2 * HALO_COLS
    side = tall // GROUP
    vmem, smem = pl.BlockSpec(memory_space=pltpu.VMEM), pl.BlockSpec(memory_space=pltpu.SMEM)

    def planes(fields, count, extra=0, lines=side):
        return (fields, count, count + extra, lines, LANES)

    state = []
    for count, entries, inverses in ((GROUP, 3, 1), (GROUP // 2, len(FIRST), 2), (GROUP // 4, len(FULL), 2)):
        state += [planes(entries, count), planes(inverses, count), planes(2, count), planes(2, count, 1)]
    held = len(FULL) + 2
    counts = (GROUP, GROUP // 2, GROUP // 4)
    *state, coarse = pl.pallas_call(
        functools.partial(down_kernel, rows=rows, cols=cols, gx=gx, gy=gy),
        out_shape=[jax.ShapeDtypeStruct(shape, F32) for shape in state]
        + [jax.ShapeDtypeStruct((held, rows // GROUP, LANES), F32)],
        in_specs=[smem] + [vmem] * 4,
        out_specs=[vmem] * (len(state) + 1),
        scratch_shapes=spread_scratch(2 * HALO_ROWS, wide)
        + [pltpu.VMEM(planes(2, count, 1), F32) for count in counts]
        + [pltpu.VMEM((2, count, side, LANES), F32) for count in counts]
        + [pltpu.VMEM((held, side, LANES), F32)],
        compiler_params=pltpu.CompilerParams(vmem_limit_bytes=VMEM_LIMIT),
        name="descent",
    )(place, own, upper, lower, factor)

    coarse_before = passed_along(coarse, "gx", 1)
    coarse_after = passed_along(coarse, "gx", -1)
    lines = 3 * (rows // GROUP)
    return pl.pallas_call(
        functools.partial(up_kernel, rows=rows, cols=cols, gx=gx, gy=gy),
        out_shape=jax.ShapeDtypeStruct((2, rows, cols), F32),
        in_specs=[smem] + [vmem] * (3 + len(state)),
        out_specs=vmem,
        scratch_shapes=[
            shape
            for count in counts
            for shape in (pltpu.VMEM(planes(2, count, 1), F32),) * 2
        ]
        + [pltpu.VMEM((2, count, side, LANES), F32) for count in counts]
        + [
            pltpu.VMEM((2, 1, lines, LANES), F32),
            pltpu.VMEM(planes(len(FULL), 1, 0, lines), F32),
            pltpu.VMEM(planes(2, 1, 0, lines), F32),
            pltpu.VMEM(planes(2, 1, 0, lines), F32),
            pltpu.VMEM(planes(2, 1, 1, lines), F32),
            pltpu.VMEM(planes(2, 1, 1, lines), F32),
            pltpu.VMEM((6 * rows, cols), BF16),
            pltpu.VMEM((WIDE, WIDE), BF16),
            pltpu.VMEM((2, cols // LANES, rows, LANES), F32),
        ],
        compiler_params=pltpu.CompilerParams(vmem_limit_bytes=VMEM_LIMIT),
        name="ascent",
    )(place, coarse, coarse_before, coarse_after, *state)


def solution(mesh):
    return jax.shard_map(
        body,
        mesh=mesh,
        in_specs=(
            P("gx", "gy"),
            P("gx", "gy"),
            P(None, "gx", "gy"),
            P(("gx", "gy"), None),
            P(("gx", "gy")),
            P(("gx", "gy")),
        ),
        out_specs=P(None, "gx", "gy"),
        check_vma=False,
    )
```

```python
import functools
import math

import jax
import jax.numpy as jnp
import numpy as np
from jax import lax
from jax.experimental import pallas as pl
from jax.experimental.pallas import tpu as pltpu
from jax.sharding import PartitionSpec as P

LEVELS = 3
SWEEPS = 2
COARSE_SWEEPS = 6
YIELD_DROP = 0.6
GROUP = 1 << LEVELS
HALO_ROWS = 32
HALO_COLS = 128
LANES = 128
WIDE = 2 * LANES
SPAN = WIDE // GROUP
LISTS_AT_ONCE = 16
VMEM_LIMIT = 30 * 1024 * 1024
F32 = jnp.float32
BF16 = jnp.bfloat16

FIRST = ("11", "12", "33", "1r", "2r", "3r", "1c", "2c", "3c", "rr", "rc")
FULL = FIRST + ("cc",)
FIRST_AT = {name: FIRST.index(name) for name in FIRST} | {"22": 0, "cc": FIRST.index("rr")}
FULL_AT = {name: FULL.index(name) for name in FULL} | {"22": 0}


def swapped(array, axis, odd_pairs):
    devices = lax.axis_size(axis)
    pairs = []
    for i in range(odd_pairs, devices - 1, 2):
        pairs += [(i, i + 1), (i + 1, i)]
    return lax.ppermute(array, axis, pairs)


def log2(number):
    power = number.bit_length() - 1
    assert 1 << power == number
    return power


def from_before(value, axis):
    return pltpu.roll(value, 1, axis)


def from_after(value, axis):
    return pltpu.roll(value, value.shape[axis] - 1, axis)


def plus(*terms):
    total = None
    for term in terms:
        if term is not None:
            total = term if total is None else total + term
    return total


def times(weight, term):
    return None if term is None else weight * term


def factor_kernel(words, factor, tall_of, lane_of, codes, counts, *, rows, cols, gy):
    for at in range(words.shape[0]):
        tall_of[at : at + 1, :] = words[at]
    word = tall_of[...]
    cell_bits = log2(rows * cols)
    owner = word >> (cell_bits + 2)
    cell = (word >> 2) & (rows * cols - 1)
    row = (owner >> log2(gy)) * rows + (cell >> log2(cols)) - lax.axis_index("gx") * rows
    col = (owner & (gy - 1)) * cols + (cell & (cols - 1)) - lax.axis_index("gy") * cols
    tall = rows + 2 * HALO_ROWS
    side = tall // GROUP
    inside = (row >= -HALO_ROWS) & (row < rows + HALO_ROWS) & (col >= -HALO_COLS) & (col < cols + HALO_COLS)
    at = jnp.where(col < 0, col + cols + HALO_COLS, jnp.where(col >= cols, col + HALO_COLS, col))
    line = (row & (GROUP - 1)) * side + ((row >> LEVELS) & (side - 1))
    tall_of[...] = jnp.where(inside, line + tall * (at >> log2(WIDE)), -1)
    lane_of[...] = (at & (GROUP - 1)) * SPAN + ((at & (WIDE - 1)) >> LEVELS)
    codes[...] = (word & 3).astype(F32)
    counts[...] = jnp.zeros_like(counts)
    length = words.shape[2]
    group = min(LISTS_AT_ONCE, words.shape[0])

    @pl.loop(0, words.shape[0] // group)
    def _(i):
        tall_id = lax.broadcasted_iota(jnp.int32, (counts.shape[0], length), 0)
        lane_id = lax.broadcasted_iota(jnp.int32, (WIDE, length), 0)
        by_tall, by_lane = [], []
        for j in range(group):
            line = pl.ds(i * group + j, 1)
            by_tall.append(jnp.where(tall_id == tall_of[line, :], codes[line, :], 0.0).astype(BF16))
            by_lane.append(jnp.where(lane_id == lane_of[line, :], 1.0, 0.0).astype(BF16))
        counts[...] += lax.dot_general(
            jnp.concatenate(by_tall, axis=1),
            jnp.concatenate(by_lane, axis=1),
            (((1,), (1,)), ((), ())),
            preferred_element_type=F32,
        )

    for m in range(GROUP):
        for k in range(GROUP):
            half, slot = k * SPAN // LANES, k * SPAN % LANES
            lanes = slice(half * LANES, (half + 1) * LANES)
            lines = range(m * side, counts.shape[0], tall)
            count = gather_lanes([counts[line : line + side, lanes] for line in lines], slot)
            factor[m, k] = jnp.exp(count * math.log(YIELD_DROP))


def yield_factor(words, rows, cols, gy):
    tall, wide = rows + 2 * HALO_ROWS, cols + 2 * HALO_COLS
    lists = (words.shape[0], words.shape[2])
    return pl.pallas_call(
        functools.partial(factor_kernel, rows=rows, cols=cols, gy=gy),
        out_shape=jax.ShapeDtypeStruct((GROUP, GROUP, tall // GROUP, LANES), F32),
        in_specs=[pl.BlockSpec(memory_space=pltpu.VMEM)],
        out_specs=pl.BlockSpec(memory_space=pltpu.VMEM),
        scratch_shapes=[
            pltpu.VMEM(lists, jnp.int32),
            pltpu.VMEM(lists, jnp.int32),
            pltpu.VMEM(lists, F32),
            pltpu.VMEM((tall * wide // WIDE, WIDE), F32),
        ],
        compiler_params=pltpu.CompilerParams(vmem_limit_bytes=VMEM_LIMIT),
        cost_estimate=pl.CostEstimate(
            flops=2 * tall * wide * words.size, bytes_accessed=4 * words.size, transcendentals=tall * wide
        ),
        name="yield_factor",
    )(words)


def pack_kernel(
    first_lame, shear_modulus, applied_load, owner, cell, code,
    fields, even_cols, odd_cols, words, lists, copied, arrived,
    *, cells,
):
    copies = [
        pltpu.make_async_copy(source, target, arrived.at[at])
        for at, (source, target) in enumerate(
            (
                (owner, lists.at[0]),
                (cell, lists.at[1]),
                (code, lists.at[2]),
                (first_lame, fields.at[0]),
                (shear_modulus, fields.at[1]),
                (applied_load, fields.at[pl.ds(2, 2)]),
            )
        )
    ]
    for copy in copies:
        copy.start()
    for copy in copies[:3]:
        copy.wait()
    word = (lists[0] * cells + lists[1]) * 4 + lists[2]
    for device in range(words.shape[0]):
        copied[device] = word
    sent = pltpu.make_async_copy(copied, words, arrived.at[6])
    sent.start()
    for copy in copies[3:]:
        copy.wait()
    last, odd = fields.shape[2] - HALO_COLS, lax.axis_index("gy") & 1
    even_cols[...] = fields[:, :, pl.ds(pl.multiple_of(last * (1 - odd), HALO_COLS), HALO_COLS)]
    odd_cols[...] = fields[:, :, pl.ds(pl.multiple_of(last * odd, HALO_COLS), HALO_COLS)]
    sent.wait()


def pack(first_lame, shear_modulus, applied_load, owner, cell, code, devices):
    rows, cols = first_lame.shape
    edge = jax.ShapeDtypeStruct((4, rows, HALO_COLS), F32)
    length = cell.shape[0]
    arrays = [first_lame, shear_modulus, applied_load] + [part.reshape(1, -1) for part in (owner, cell, code)]
    hbm, vmem = pl.BlockSpec(memory_space=pltpu.HBM), pl.BlockSpec(memory_space=pltpu.VMEM)
    return pl.pallas_call(
        functools.partial(pack_kernel, cells=rows * cols),
        out_shape=[
            jax.ShapeDtypeStruct((4, rows, cols), F32),
            edge,
            edge,
            jax.ShapeDtypeStruct((devices, 1, length), jnp.int32),
        ],
        in_specs=[hbm] * 6,
        out_specs=[vmem] * 3 + [hbm],
        scratch_shapes=[
            pltpu.VMEM((3, 1, length), jnp.int32),
            pltpu.VMEM((devices, 1, length), jnp.int32),
            pltpu.SemaphoreType.DMA((7,)),
        ],
        compiler_params=pltpu.CompilerParams(vmem_limit_bytes=8 * 1024 * 1024),
        name="pack",
    )(*[pltpu.with_memory_space_constraint(array, pltpu.HBM) for array in arrays])


def rows_kernel(fields, even_side, odd_side, even_rows, odd_rows):
    rows, cols = fields.shape[1:]
    last, odd, odd_col = rows - HALO_ROWS, lax.axis_index("gx") & 1, lax.axis_index("gy") & 1
    for out, side in ((even_rows, 1 - odd), (odd_rows, odd)):
        span = pl.ds(pl.multiple_of(last * side, HALO_ROWS), HALO_ROWS)
        out[:, :, :cols] = fields[:, span, :]
        for halo, after in ((even_side, 1 - odd_col), (odd_side, odd_col)):
            at = pl.multiple_of(cols + HALO_COLS * after, HALO_COLS)
            out[:, :, pl.ds(at, HALO_COLS)] = halo[:, span, :]


def pack_rows(fields, even_side, odd_side):
    edge = jax.ShapeDtypeStruct((4, HALO_ROWS, fields.shape[2] + 2 * HALO_COLS), F32)
    vmem = pl.BlockSpec(memory_space=pltpu.VMEM)
    return pl.pallas_call(
        rows_kernel,
        out_shape=[edge, edge],
        in_specs=[vmem] * 3,
        out_specs=[vmem] * 2,
        compiler_params=pltpu.CompilerParams(vmem_limit_bytes=8 * 1024 * 1024),
        name="pack_rows",
    )(fields, even_side, odd_side)


class Level:
    def __init__(self, matrix, names_at, inverse, spill):
        self.matrix, self.names_at, self.inverse, self.spill = matrix, names_at, inverse, spill
        self.count = matrix.shape[1]

    def entry(self, name, m, k, high):
        at = self.names_at.get(name)
        return None if at is None else self.matrix[at, m, k, :high, :]

    def stress(self, m, k, modes):
        names = "123rc"
        known = {}
        result = []
        for i in range(5):
            terms = []
            for j in range(5):
                name = names[min(i, j)] + names[max(i, j)]
                if name not in known:
                    known[name] = self.entry(name, m, k, modes[0].shape[0])
                if known[name] is not None:
                    terms.append(known[name] * modes[j])
            result.append(plus(*terms))
        return result

    def halves(self, component, m, k):
        if component == 0:
            names = ("11", "33", "rr", "13", "1r", "3r")
        else:
            names = ("22", "33", "cc", "23", "3c", "2c")
        first, second, third, cross, by_col, by_row = [self.entry(name, m, k, self.matrix.shape[3]) for name in names]
        base = first + second + third
        by_row, by_col, cross = 2.0 * by_row, 2.0 * by_col, times(2.0, cross)
        if cross is None:
            return base - by_row, base + by_row, by_col, by_col
        return base - by_row, base + by_row, by_col - cross, by_col + cross

    def components(self):
        return (0, 1)

    def make_inverse(self, row_ok, col_ok):
        count = self.count
        for component in self.components():
            kept = {}
            for k in range(count):
                parts = [self.halves(component, m, k) for m in range(count)]
                for m in range(count):
                    above = parts[m - 1] if m else parts[count - 1]
                    lower = [above[1], above[3]]
                    if m == 0:
                        lower = [from_before(value, 0) for value in lower]
                    even, odd = parts[m][0] + lower[0], parts[m][2] + lower[1]
                    kept[m, k] = (even - odd, even + odd)
            for k in range(count):
                for m in range(count):
                    left = kept[m, k - 1][1] if k else from_before(kept[m, count - 1][1], 1)
                    diagonal = kept[m, k][0] + left
                    value = jnp.where(diagonal > 0.0, 0.5 / diagonal, 0.0)
                    if m == 0:
                        value = value * row_ok
                    if k == 0:
                        value = value * col_ok
                    self.inverse[component, m, k] = value


class FineLevel(Level):
    def stress(self, m, k, modes):
        lame, shear, mixed = [self.matrix[at, m, k, : modes[0].shape[0], :] for at in range(3)]
        first, second, third, bend_row, bend_col = modes
        twice, mean = shear + shear, lame * (first + second)
        return [
            mean + twice * first,
            mean + twice * second,
            shear * third,
            mixed * bend_row,
            mixed * bend_col,
        ]

    def components(self):
        return (0,)

    def make_inverse(self, row_ok, col_ok):
        count = self.count

        @pl.loop(0, count)
        def _(k):
            parts = [self.matrix[2, m, k] for m in range(count)]
            for m in range(count):
                above = parts[m - 1] if m else from_before(parts[count - 1], 0)
                self.inverse[0, m, k] = parts[m] + above

        for m in range(count):
            left = from_before(self.inverse[0, m, count - 1], 1)
            for k in range(count):
                here = self.inverse[0, m, k]
                diagonal = 4.0 * (here + left)
                left = here
                value = jnp.where(diagonal > 0.0, 0.5 / diagonal, 0.0)
                if m == 0:
                    value = value * row_ok
                if k == 0:
                    value = value * col_ok
                self.inverse[0, m, k] = value


def inverse_of(level, component, m, k, high):
    return level.inverse[min(component, len(level.components()) - 1), m, k, :high, :]


def close_columns(level, x):
    count = level.count
    for component in (0, 1):
        for m in range(count):
            x[component, m, count] = from_after(x[component, m, 0], 1)


def start(level, x, source):
    count = level.count

    def column(k):
        for component in (0, 1):
            for m in range(count):
                x[component, m, k] = source[component, m, k] * inverse_of(level, component, m, k, x.shape[3])

    over_columns(count, column)
    close_columns(level, x)


def over_columns(count, column):
    if count > 2:
        pl.loop(0, count)(column)
    else:
        for k in range(count):
            column(k)


def cut(value, height):
    return value if value.shape[0] == height else value[:height]


def apply(level, x, source, out, residual, tall_cells=None, tall_nodes=None):
    count, spill = level.count, level.spill
    side = x.shape[3]
    cells = [side if tall_cells is None or m in tall_cells else side // 2 for m in range(count)]
    nodes = [side if tall_nodes is None or m in tall_nodes else side // 2 for m in range(count)]
    held = [max(cells[m], cells[m - 1]) if m else side for m in range(count)]
    spill[...] = jnp.zeros_like(spill)

    def column(k):
        sums, steps = [], []
        for m in range(count):
            here = [x[component, m, k, : held[m], :] for component in (0, 1)]
            after = [x[component, m, k + 1, : held[m], :] for component in (0, 1)]
            sums.append([here[c] + after[c] for c in (0, 1)])
            steps.append([after[c] - here[c] for c in (0, 1)])
        sums.append([from_after(value, 0) for value in sums[0]])
        steps.append([from_after(value, 0) for value in steps[0]])
        own, passed = [], []
        for m in range(count):
            sum0, sum1 = [[cut(value, cells[m]) for value in sums[row]] for row in (m, m + 1)]
            step0, step1 = [[cut(value, cells[m]) for value in steps[row]] for row in (m, m + 1)]
            modes = (
                sum1[0] - sum0[0],
                step0[1] + step1[1],
                (step0[0] + step1[0]) + (sum1[1] - sum0[1]),
                step1[0] - step0[0],
                step1[1] - step0[1],
            )
            first, second, third, bend_row, bend_col = level.stress(m, k, modes)
            own.append((first, third - bend_row, third, second - bend_col))
            passed.append((first, third + bend_row, third, second + bend_col))
        for m in range(count):
            high = nodes[m]
            above = passed[m - 1] if m else [from_before(value, 0) for value in passed[count - 1]]
            for component in (0, 1):
                at = 2 * component
                even = cut(above[at], high) - cut(own[m][at], high)
                odd = cut(above[at + 1], high) + cut(own[m][at + 1], high)
                left = spill[component, m, :high, :]
                spill[component, m, :high, :] = even + odd
                rest = source[component, m, k, :high, :] - ((even - odd) + left)
                if not residual:
                    rest = x[component, m, k, :high, :] + inverse_of(level, component, m, k, high) * rest
                out[component, m, k, :high, :] = rest

    over_columns(count, column)
    for component in (0, 1):
        for m in range(count):
            high = nodes[m]
            left = from_before(spill[component, m, :high, :], 1)
            if not residual:
                left = left * inverse_of(level, component, m, 0, high)
            out[component, m, 0, :high, :] = out[component, m, 0, :high, :] - left
            if not residual:
                out[component, m, count, :high, :] = from_after(out[component, m, 0, :high, :], 1)


def restrict(residual, target, count):
    half = count // 2
    for component in (0, 1):
        for k in range(half):
            lines = []
            for m in range(count):
                odd = residual[component, m, 2 * k + 1]
                if k:
                    before = residual[component, m, 2 * k - 1]
                else:
                    before = from_before(residual[component, m, count - 1], 1)
                lines.append(residual[component, m, 2 * k] + 0.5 * (odd + before))
            for m in range(half):
                before = lines[2 * m - 1] if m else from_before(lines[count - 1], 0)
                target[component, m, k] = lines[2 * m] + 0.5 * (lines[2 * m + 1] + before)


def prolong(coarse, before, x, count):
    half = count // 2
    for component in (0, 1):
        planes = {(m, k): coarse(component, m, k) for m in range(half) for k in range(half)}
        for m in range(half):
            planes[m, half] = from_after(planes[m, 0], 1)
        for k in range(half + 1):
            planes[half, k] = from_after(planes[0, k], 0)
        for m in range(half):
            for k in range(half):
                a, b, c, d = planes[m, k], planes[m + 1, k], planes[m, k + 1], planes[m + 1, k + 1]
                x[component, 2 * m, 2 * k] = before[component, 2 * m, 2 * k] + a
                x[component, 2 * m + 1, 2 * k] = before[component, 2 * m + 1, 2 * k] + 0.5 * (a + b)
                x[component, 2 * m, 2 * k + 1] = before[component, 2 * m, 2 * k + 1] + 0.5 * (a + c)
                x[component, 2 * m + 1, 2 * k + 1] = before[component, 2 * m + 1, 2 * k + 1] + 0.25 * ((a + b) + (c + d))


def haar(level, names_at, m, k):
    def signed(name, row, col):
        if name not in names_at:
            return None
        value = {
            (a, b): level.matrix[names_at[name], 2 * m + a, 2 * k + b] for a in (0, 1) for b in (0, 1)
        }
        low = value[0, 1] - value[0, 0] if col else value[0, 1] + value[0, 0]
        high = value[1, 1] - value[1, 0] if col else value[1, 1] + value[1, 0]
        return high - low if row else high + low

    return signed


def coarsen_fine(fine, coarse):
    count = coarse.count

    def column(k):
        for m in range(count):
            signed = haar(fine, {"l": 0, "s": 1}, m, k)
            lame, shear = signed("l", 0, 0), signed("s", 0, 0)
            lame_row, shear_row = signed("l", 1, 0), signed("s", 1, 0)
            lame_col, shear_col = signed("l", 0, 1), signed("s", 0, 1)
            lame_both, shear_both = signed("l", 1, 1), signed("s", 1, 1)
            values = {
                "11": 0.25 * (lame + 2.0 * shear),
                "12": 0.25 * lame,
                "33": 0.25 * shear,
                "1r": 0.125 * (lame_col + 2.0 * shear_col),
                "2r": 0.125 * lame_col,
                "3r": 0.125 * shear_row,
                "1c": 0.125 * lame_row,
                "2c": 0.125 * (lame_row + 2.0 * shear_row),
                "3c": 0.125 * shear_col,
                "rr": (lame + 3.0 * shear) * (1.0 / 12.0),
                "rc": 0.0625 * (lame_both + shear_both),
            }
            for name, value in values.items():
                coarse.matrix[FIRST_AT[name], m, k] = value

    over_columns(count, column)


def coarsen(fine, write, count):
    for k in range(count):
        for m in range(count):
            signed = haar(fine, fine.names_at, m, k)

            def total(name):
                return signed(name, 0, 0)

            def by_row(name):
                return signed(name, 1, 0)

            def by_col(name):
                return signed(name, 0, 1)

            def by_both(name):
                return signed(name, 1, 1)

            values = {}
            for name in ("11", "12", "33"):
                values[name] = times(0.25, total(name))
            for i in "123":
                one, two, three = ["".join(sorted(i + j)) for j in "123"]
                values[i + "r"] = 0.125 * plus(by_col(one), by_row(three), total(i + "r"))
                values[i + "c"] = 0.125 * plus(by_row(two), by_col(three), total(i + "c"))
            values["rr"] = 0.0625 * plus(
                total("11"),
                total("33"),
                times(2.0, by_both("13")),
                2.0 * (by_col("1r") + by_row("3r")),
                total("rr"),
            )
            values["cc"] = 0.0625 * plus(
                total("22"),
                total("33"),
                times(2.0, by_both("23")),
                2.0 * (by_row("2c") + by_col("3c")),
                total("cc"),
            )
            values["rc"] = 0.0625 * plus(
                by_both("12"),
                total("13"),
                total("23"),
                by_both("33"),
                by_col("1c"),
                by_row("3c"),
                by_row("2r"),
                by_col("3r"),
                total("rc"),
            )
            for name in FULL:
                write(FULL_AT[name], m, k, values[name])


def edge_masks(shape, before, rows, cols, grid_rows, grid_cols):
    def wrapped(axis, ahead):
        at = lax.broadcasted_iota(jnp.int32, shape, axis)
        return jnp.where(at < shape[axis] - ahead, at, at - shape[axis]) * GROUP

    row = wrapped(0, before) + lax.axis_index("gx") * rows
    col = wrapped(1, HALO_COLS // GROUP) + lax.axis_index("gy") * cols
    return (
        jnp.where(row < grid_rows, 1.0, 0.0).astype(F32),
        jnp.where(col < grid_cols, 1.0, 0.0).astype(F32),
    )


def three_parts(value):
    high = value.astype(BF16)
    rest = value - high.astype(F32)
    middle = rest.astype(BF16)
    low = (rest - middle.astype(F32)).astype(BF16)
    return high, middle, low


def turned(value, by):
    return pltpu.roll(value, by % LANES, 1) if by % LANES else value


def gather_lanes(pieces, slot):
    lane = lax.broadcasted_iota(jnp.int32, pieces[0].shape, 1)
    halo = HALO_COLS // GROUP
    own = (len(pieces) - 1) * SPAN
    plane = jnp.where(lane >= LANES - halo, turned(pieces[-1], LANES - halo - slot), 0.0)
    plane = jnp.where(lane < own + halo, turned(pieces[-1], own - halo - slot), plane)
    for at in reversed(range(len(pieces) - 1)):
        plane = jnp.where(lane < (at + 1) * SPAN, turned(pieces[at], at * SPAN - slot), plane)
    return plane


def make_spread(spread):
    at = lax.broadcasted_iota(jnp.int32, (WIDE, WIDE), 0)
    lane = lax.broadcasted_iota(jnp.int32, (WIDE, WIDE), 1)
    spread[...] = jnp.where(lane == (at & (GROUP - 1)) * SPAN + (at >> LEVELS), 1.0, 0.0).astype(BF16)


def spread_fields(load, write, tiles, stacked, spread):
    fields, count, rows = tiles.shape[:3]
    block = rows // GROUP
    make_spread(spread)
    for field in range(fields):
        for tile in range(count):
            load(field, tile)
        for pair in range(GROUP // 2):
            for tile in range(count):
                lines = [tiles[field, tile, pl.ds(2 * pair + h, block, stride=GROUP), :] for h in (0, 1)]
                for part, split in enumerate(three_parts(jnp.concatenate(lines, axis=0))):
                    line = (field * 3 + part) * rows + pair * 2 * block
                    stacked[line : line + 2 * block, tile * LANES : (tile + 1) * LANES] = split
    for field in range(fields):
        pieces = []
        for piece in range(count * LANES // WIDE):
            left = stacked[field * 3 * rows : (field + 1) * 3 * rows, piece * WIDE : (piece + 1) * WIDE]
            product = jnp.dot(left, spread[...], preferred_element_type=F32)
            pieces.append(product[:rows] + product[rows : 2 * rows] + product[2 * rows :])
        for m in range(GROUP):
            for k in range(GROUP):
                half, slot = k * SPAN // LANES, k * SPAN % LANES
                lanes = slice(half * LANES, (half + 1) * LANES)
                lines = slice(m * block, (m + 1) * block)
                write(field, m, k, gather_lanes([piece[lines, lanes] for piece in pieces], slot))


def own_kernel(fields, even_side, odd_side, planes, tiles, stacked, spread):
    own_tiles, odd = fields.shape[2] // LANES, lax.axis_index("gy") & 1

    def load(field, tile):
        if tile < own_tiles:
            tiles[field, tile] = fields[field, :, tile * LANES : (tile + 1) * LANES]
        elif tile == own_tiles:
            tiles[field, tile + 1 - odd] = even_side[field]
        else:
            tiles[field, own_tiles + odd] = odd_side[field]

    def write(field, m, k, plane):
        planes[field, m, k] = plane

    spread_fields(load, write, tiles, stacked, spread)


def spread_scratch(rows, wide):
    return [
        pltpu.VMEM((4, wide // LANES, rows, LANES), F32),
        pltpu.VMEM((12 * rows, wide), BF16),
        pltpu.VMEM((WIDE, WIDE), BF16),
    ]


def spread_own(fields, even_side, odd_side):
    rows, wide = fields.shape[1], fields.shape[2] + 2 * HALO_COLS
    vmem = pl.BlockSpec(memory_space=pltpu.VMEM)
    return pl.pallas_call(
        own_kernel,
        out_shape=jax.ShapeDtypeStruct((4, GROUP, GROUP, rows // GROUP, LANES), F32),
        in_specs=[vmem] * 3,
        out_specs=vmem,
        scratch_shapes=spread_scratch(rows, wide),
        compiler_params=pltpu.CompilerParams(vmem_limit_bytes=12 * 1024 * 1024),
        cost_estimate=pl.CostEstimate(flops=24 * rows * wide * WIDE, bytes_accessed=0, transcendentals=0),
        name="spread_own",
    )(fields, even_side, odd_side)


def down_kernel(
    own, even_rows, odd_rows, factor,
    matrix0, inverse0, source0, x0, matrix1, inverse1, source1, x1, matrix2, inverse2, source2, x2, coarsest,
    tiles, stacked, spread, other0, other1, other2, spill0, spill1, spill2, matrix3,
    *, rows, cols, gx, gy,
):
    block = rows // GROUP
    side = block + 2 * HALO_ROWS // GROUP
    row_ok, col_ok = edge_masks(
        (side, LANES), HALO_ROWS // GROUP, rows, cols, gx * rows, gy * cols
    )

    odd = lax.axis_index("gx") & 1

    def load(field, tile):
        lanes = slice(tile * LANES, (tile + 1) * LANES)
        for halo, before in ((even_rows, odd), (odd_rows, 1 - odd)):
            span = pl.ds(pl.multiple_of(HALO_ROWS * before, HALO_ROWS), HALO_ROWS)
            tiles[field, tile, span, :] = halo[field, :, lanes]

    def write(field, m, k, plane):
        if field < 2:
            matrix0[field, m, k, :block, :] = own[field, m, k] * (0.25 * factor[m, k, :block, :])
            matrix0[field, m, k, block:, :] = plane * (0.25 * factor[m, k, block:, :])
        else:
            source0[field - 2, m, k, :block, :] = own[field, m, k]
            source0[field - 2, m, k, block:, :] = plane

    spread_fields(load, write, tiles, stacked, spread)

    def mix(k):
        for m in range(GROUP):
            matrix0[2, m, k] = matrix0[0, m, k] * (1.0 / 3.0) + matrix0[1, m, k]

    over_columns(GROUP, mix)

    level0 = FineLevel(matrix0, {}, inverse0, spill0)
    level1 = Level(matrix1, FIRST_AT, inverse1, spill1)
    level2 = Level(matrix2, FULL_AT, inverse2, spill2)

    coarsen_fine(level0, level1)

    def write2(at, m, k, value):
        matrix2[at, m, k] = value

    coarsen(level1, write2, level2.count)

    def write3(at, m, k, value):
        matrix3[at] = value

    coarsen(level2, write3, 1)
    for level in (level0, level1, level2):
        level.make_inverse(row_ok, col_ok)

    source3 = matrix3.at[pl.ds(len(FULL), 2)]
    chain = (
        (level0, source0, x0, other0, source1),
        (level1, source1, x1, other1, source2),
        (level2, source2, x2, other2, None),
    )
    for level, source, x, other, target in chain:
        start(level, other, source)
        apply(level, other, source, x, residual=False)
        apply(level, x, source, other, residual=True)
        if target is not None:
            restrict(other, target, level.count)
        else:
            restrict_last(other, source3)
    for at in range(len(FULL) + 2):
        coarsest[at] = matrix3[at, :block, :]


def restrict_last(residual, target):
    class Planes:
        def __setitem__(self, where, value):
            target[where[0]] = value

    restrict(residual, Planes(), 2)


def up_kernel(
    coarse, coarse_even, coarse_odd,
    matrix0, inverse0, source0, x0_in, matrix1, inverse1, source1, x1_in, matrix2, inverse2, source2, x2_in,
    displacement,
    x0, other0, x1, other1, x2, other2, spill0, spill1, spill2, spill3, matrix3, inverse3, source3, x3, other3,
    stacked, gathered, tiles,
    *, rows, cols, gx, gy,
):
    block, odd = rows // GROUP, lax.axis_index("gx") & 1
    for at in range(len(FULL) + 2):
        for piece, part in ((0, coarse), (1 + odd, coarse_even), (2 - odd, coarse_odd)):
            lines = pl.ds(pl.multiple_of(piece * block, block), block)
            if at < len(FULL):
                matrix3[at, 0, 0, lines, :] = part[at]
            else:
                source3[at - len(FULL), 0, 0, lines, :] = part[at]
    level3 = Level(matrix3, FULL_AT, inverse3, spill3)
    level3.make_inverse(*edge_masks((3 * block, LANES), block, rows, cols, gx * rows, gy * cols))
    start(level3, x3, source3)
    now, then = x3, other3
    for _ in range(COARSE_SWEEPS - 1):
        apply(level3, now, source3, then, residual=False)
        now, then = then, now
    coarse_plane = functools.partial(cut_plane, now, block)

    level0 = FineLevel(matrix0, {}, inverse0, spill0)
    level1 = Level(matrix1, FIRST_AT, inverse1, spill1)
    level2 = Level(matrix2, FULL_AT, inverse2, spill2)
    for level, source, before, x, other in (
        (level2, source2, x2_in, x2, other2),
        (level1, source1, x1_in, x1, other1),
        (level0, source0, x0_in, x0, other0),
    ):
        prolong(coarse_plane, before, x, level.count)
        close_columns(level, x)
        last = level.count - 1
        if level is level0:
            apply(level, x, source, other, False, {0, last - 1, last}, {0, last})
            apply(level, other, source, x, False, {last}, set())
        else:
            apply(level, x, source, other, residual=False)
            apply(level, other, source, x, residual=False)
        coarse_plane = functools.partial(whole_plane, x)

    at = lax.broadcasted_iota(jnp.int32, (WIDE, WIDE), 1)
    line = lax.broadcasted_iota(jnp.int32, (WIDE, WIDE), 0)
    gathered[...] = jnp.where(line == (at & (GROUP - 1)) * SPAN + (at >> LEVELS), 1.0, 0.0).astype(BF16)
    lane = lax.broadcasted_iota(jnp.int32, (2 * block, LANES), 1)
    for component in (0, 1):
        for pair in range(GROUP // 2):
            values = [
                jnp.concatenate(
                    [x0[component, 2 * pair + h, k, :block, :] for h in (0, 1)], axis=0
                )
                for k in range(GROUP)
            ]
            for piece in range(cols // WIDE):
                for half in range(WIDE // LANES):
                    slots = LANES // SPAN
                    value = None
                    for slot in reversed(range(slots)):
                        part = turned(values[half * slots + slot], (slot - piece) * SPAN)
                        value = part if value is None else jnp.where(lane < (slot + 1) * SPAN, part, value)
                    lanes = slice(piece * WIDE + half * LANES, piece * WIDE + (half + 1) * LANES)
                    for part, split in enumerate(three_parts(value)):
                        line = part * 2 * rows + component * rows + pair * 2 * block
                        stacked[line : line + 2 * block, lanes] = split
    pieces = []
    for piece in range(cols // WIDE):
        product = jnp.dot(
            stacked[:, piece * WIDE : (piece + 1) * WIDE], gathered[...], preferred_element_type=F32
        )
        pieces.append(product[: 2 * rows] + product[2 * rows : 4 * rows] + product[4 * rows :])
    for component in (0, 1):
        for tile in range(cols // LANES):
            lanes = slice(tile * LANES, (tile + 1) * LANES)
            for m in range(GROUP):
                line = component * rows + m * block
                tiles[component, tile, pl.ds(m, block, stride=GROUP), :] = pieces[tile * LANES // WIDE][
                    line : line + block, tile * LANES % WIDE : tile * LANES % WIDE + LANES
                ]
            displacement[component, :, lanes] = tiles[component, tile]


def cut_plane(x, block, component, m, k):
    line = lax.broadcasted_iota(jnp.int32, (block, LANES), 0)
    halo = jnp.where(
        line < HALO_ROWS // GROUP,
        x[component, 0, 0, block : 2 * block, :],
        x[component, 0, 0, 2 * block :, :],
    )
    return jnp.concatenate([x[component, 0, 0, :block, :], halo], axis=0)


def whole_plane(x, component, m, k):
    return x[component, m, k]


def body(first_lame, shear_modulus, applied_load, plastic_owner, plastic_cell, plastic_code):
    rows, cols = first_lame.shape
    gx, gy = lax.axis_size("gx"), lax.axis_size("gy")
    devices = gx * gy

    fields, even_cols, odd_cols, words = pack(
        first_lame, shear_modulus, applied_load, plastic_owner, plastic_cell, plastic_code, devices
    )
    even_side, odd_side = swapped(even_cols, "gy", 0), swapped(odd_cols, "gy", 1)
    words = lax.all_to_all(words, ("gx", "gy"), 0, 0, tiled=True)

    even_rows, odd_rows = pack_rows(fields, even_side, odd_side)
    even_rows, odd_rows = swapped(even_rows, "gx", 0), swapped(odd_rows, "gx", 1)
    own = spread_own(fields, even_side, odd_side)
    words, own = lax.optimization_barrier((words, own))
    factor = yield_factor(words, rows, cols, gy)

    tall, wide = rows + 2 * HALO_ROWS, cols + 2 * HALO_COLS
    side = tall // GROUP
    vmem = pl.BlockSpec(memory_space=pltpu.VMEM)

    def planes(fields, count, extra=0, lines=side):
        return (fields, count, count + extra, lines, LANES)

    state = []
    for count, entries, inverses in ((GROUP, 3, 1), (GROUP // 2, len(FIRST), 2), (GROUP // 4, len(FULL), 2)):
        state += [planes(entries, count), planes(inverses, count), planes(2, count), planes(2, count, 1)]
    held = len(FULL) + 2
    counts = (GROUP, GROUP // 2, GROUP // 4)
    *state, coarse = pl.pallas_call(
        functools.partial(down_kernel, rows=rows, cols=cols, gx=gx, gy=gy),
        out_shape=[jax.ShapeDtypeStruct(shape, F32) for shape in state]
        + [jax.ShapeDtypeStruct((held, rows // GROUP, LANES), F32)],
        in_specs=[vmem] * 4,
        out_specs=[vmem] * (len(state) + 1),
        scratch_shapes=spread_scratch(2 * HALO_ROWS, wide)
        + [pltpu.VMEM(planes(2, count, 1), F32) for count in counts]
        + [pltpu.VMEM((2, count, side, LANES), F32) for count in counts]
        + [pltpu.VMEM((held, side, LANES), F32)],
        compiler_params=pltpu.CompilerParams(vmem_limit_bytes=VMEM_LIMIT),
        name="descent",
    )(own, even_rows, odd_rows, factor)

    coarse_even, coarse_odd = swapped(coarse, "gx", 0), swapped(coarse, "gx", 1)
    lines = 3 * (rows // GROUP)
    return pl.pallas_call(
        functools.partial(up_kernel, rows=rows, cols=cols, gx=gx, gy=gy),
        out_shape=jax.ShapeDtypeStruct((2, rows, cols), F32),
        in_specs=[vmem] * (3 + len(state)),
        out_specs=vmem,
        scratch_shapes=[
            shape
            for count in counts
            for shape in (pltpu.VMEM(planes(2, count, 1), F32),) * 2
        ]
        + [pltpu.VMEM((2, count, side, LANES), F32) for count in counts]
        + [
            pltpu.VMEM((2, 1, lines, LANES), F32),
            pltpu.VMEM(planes(len(FULL), 1, 0, lines), F32),
            pltpu.VMEM(planes(2, 1, 0, lines), F32),
            pltpu.VMEM(planes(2, 1, 0, lines), F32),
            pltpu.VMEM(planes(2, 1, 1, lines), F32),
            pltpu.VMEM(planes(2, 1, 1, lines), F32),
            pltpu.VMEM((6 * rows, cols), BF16),
            pltpu.VMEM((WIDE, WIDE), BF16),
            pltpu.VMEM((2, cols // LANES, rows, LANES), F32),
        ],
        compiler_params=pltpu.CompilerParams(vmem_limit_bytes=VMEM_LIMIT),
        name="ascent",
    )(coarse, coarse_even, coarse_odd, *state)


def solution(mesh):
    return jax.shard_map(
        body,
        mesh=mesh,
        in_specs=(
            P("gx", "gy"),
            P("gx", "gy"),
            P(None, "gx", "gy"),
            P(("gx", "gy"), None),
            P(("gx", "gy")),
            P(("gx", "gy")),
        ),
        out_specs=P(None, "gx", "gy"),
        check_vma=False,
    )
```

```python
import functools
import math

import jax
import jax.numpy as jnp
import numpy as np
from jax import lax
from jax.experimental import pallas as pl
from jax.experimental.pallas import tpu as pltpu
from jax.sharding import PartitionSpec as P

LEVELS = 3
SWEEPS = 2
COARSE_SWEEPS = 6
YIELD_DROP = 0.6
GROUP = 1 << LEVELS
HALO_ROWS = 32
HALO_COLS = 128
LANES = 128
WIDE = 2 * LANES
SPAN = WIDE // GROUP
LISTS_AT_ONCE = 16
VMEM_LIMIT = 30 * 1024 * 1024
F32 = jnp.float32
BF16 = jnp.bfloat16

FIRST = ("11", "12", "33", "1r", "2r", "3r", "1c", "2c", "3c", "rr", "rc")
FULL = FIRST + ("cc",)
FIRST_AT = {name: FIRST.index(name) for name in FIRST} | {"22": 0, "cc": FIRST.index("rr")}
FULL_AT = {name: FULL.index(name) for name in FULL} | {"22": 0}


def swapped(array, axis, odd_pairs):
    devices = lax.axis_size(axis)
    pairs = []
    for i in range(odd_pairs, devices - 1, 2):
        pairs += [(i, i + 1), (i + 1, i)]
    return lax.ppermute(array, axis, pairs)


def log2(number):
    power = number.bit_length() - 1
    assert 1 << power == number
    return power


def from_before(value, axis):
    return pltpu.roll(value, 1, axis)


def from_after(value, axis):
    return pltpu.roll(value, value.shape[axis] - 1, axis)


def plus(*terms):
    total = None
    for term in terms:
        if term is not None:
            total = term if total is None else total + term
    return total


def times(weight, term):
    return None if term is None else weight * term


def factor_kernel(words, factor, tall_of, lane_of, codes, counts, *, rows, cols, gy):
    for at in range(words.shape[0]):
        tall_of[at : at + 1, :] = words[at]
    word = tall_of[...]
    cell_bits = log2(rows * cols)
    owner = word >> (cell_bits + 2)
    cell = (word >> 2) & (rows * cols - 1)
    row = (owner >> log2(gy)) * rows + (cell >> log2(cols)) - lax.axis_index("gx") * rows
    col = (owner & (gy - 1)) * cols + (cell & (cols - 1)) - lax.axis_index("gy") * cols
    tall = rows + 2 * HALO_ROWS
    side = tall // GROUP
    inside = (row >= -HALO_ROWS) & (row < rows + HALO_ROWS) & (col >= -HALO_COLS) & (col < cols + HALO_COLS)
    at = jnp.where(col < 0, col + cols + HALO_COLS, jnp.where(col >= cols, col + HALO_COLS, col))
    line = (row & (GROUP - 1)) * side + ((row >> LEVELS) & (side - 1))
    tall_of[...] = jnp.where(inside, line + tall * (at >> log2(WIDE)), -1)
    lane_of[...] = (at & (GROUP - 1)) * SPAN + ((at & (WIDE - 1)) >> LEVELS)
    codes[...] = (word & 3).astype(F32)
    counts[...] = jnp.zeros_like(counts)
    length = words.shape[2]
    group = min(LISTS_AT_ONCE, words.shape[0])

    @pl.loop(0, words.shape[0] // group)
    def _(i):
        tall_id = lax.broadcasted_iota(jnp.int32, (counts.shape[0], length), 0)
        lane_id = lax.broadcasted_iota(jnp.int32, (WIDE, length), 0)
        by_tall, by_lane = [], []
        for j in range(group):
            line = pl.ds(i * group + j, 1)
            by_tall.append(jnp.where(tall_id == tall_of[line, :], codes[line, :], 0.0).astype(BF16))
            by_lane.append(jnp.where(lane_id == lane_of[line, :], 1.0, 0.0).astype(BF16))
        counts[...] += lax.dot_general(
            jnp.concatenate(by_tall, axis=1),
            jnp.concatenate(by_lane, axis=1),
            (((1,), (1,)), ((), ())),
            preferred_element_type=F32,
        )

    for m in range(GROUP):
        for k in range(GROUP):
            half, slot = k * SPAN // LANES, k * SPAN % LANES
            lanes = slice(half * LANES, (half + 1) * LANES)
            lines = range(m * side, counts.shape[0], tall)
            count = gather_lanes([counts[line : line + side, lanes] for line in lines], slot)
            factor[m, k] = jnp.exp(count * math.log(YIELD_DROP))


def yield_factor(words, rows, cols, gy):
    tall, wide = rows + 2 * HALO_ROWS, cols + 2 * HALO_COLS
    lists = (words.shape[0], words.shape[2])
    return pl.pallas_call(
        functools.partial(factor_kernel, rows=rows, cols=cols, gy=gy),
        out_shape=jax.ShapeDtypeStruct((GROUP, GROUP, tall // GROUP, LANES), F32),
        in_specs=[pl.BlockSpec(memory_space=pltpu.VMEM)],
        out_specs=pl.BlockSpec(memory_space=pltpu.VMEM),
        scratch_shapes=[
            pltpu.VMEM(lists, jnp.int32),
            pltpu.VMEM(lists, jnp.int32),
            pltpu.VMEM(lists, F32),
            pltpu.VMEM((tall * wide // WIDE, WIDE), F32),
        ],
        compiler_params=pltpu.CompilerParams(vmem_limit_bytes=VMEM_LIMIT),
        cost_estimate=pl.CostEstimate(
            flops=2 * tall * wide * words.size, bytes_accessed=4 * words.size, transcendentals=tall * wide
        ),
        name="yield_factor",
    )(words)


def pack_kernel(
    first_lame, shear_modulus, applied_load, owner, cell, code,
    fields, even_cols, odd_cols, words, lists, copied, arrived,
    *, cells,
):
    copies = [
        pltpu.make_async_copy(source, target, arrived.at[at])
        for at, (source, target) in enumerate(
            (
                (owner, lists.at[0]),
                (cell, lists.at[1]),
                (code, lists.at[2]),
                (first_lame, fields.at[0]),
                (shear_modulus, fields.at[1]),
                (applied_load, fields.at[pl.ds(2, 2)]),
            )
        )
    ]
    for copy in copies:
        copy.start()
    for copy in copies[:3]:
        copy.wait()
    word = (lists[0] * cells + lists[1]) * 4 + lists[2]
    for device in range(words.shape[0]):
        copied[device] = word
    sent = pltpu.make_async_copy(copied, words, arrived.at[6])
    sent.start()
    for copy in copies[3:]:
        copy.wait()
    last, odd = fields.shape[2] - HALO_COLS, lax.axis_index("gy") & 1
    even_cols[...] = fields[:, :, pl.ds(pl.multiple_of(last * (1 - odd), HALO_COLS), HALO_COLS)]
    odd_cols[...] = fields[:, :, pl.ds(pl.multiple_of(last * odd, HALO_COLS), HALO_COLS)]
    sent.wait()


def pack(first_lame, shear_modulus, applied_load, owner, cell, code, devices):
    rows, cols = first_lame.shape
    edge = jax.ShapeDtypeStruct((4, rows, HALO_COLS), F32)
    length = cell.shape[0]
    arrays = [first_lame, shear_modulus, applied_load] + [part.reshape(1, -1) for part in (owner, cell, code)]
    hbm, vmem = pl.BlockSpec(memory_space=pltpu.HBM), pl.BlockSpec(memory_space=pltpu.VMEM)
    return pl.pallas_call(
        functools.partial(pack_kernel, cells=rows * cols),
        out_shape=[
            jax.ShapeDtypeStruct((4, rows, cols), F32),
            edge,
            edge,
            jax.ShapeDtypeStruct((devices, 1, length), jnp.int32),
        ],
        in_specs=[hbm] * 6,
        out_specs=[vmem] * 3 + [hbm],
        scratch_shapes=[
            pltpu.VMEM((3, 1, length), jnp.int32),
            pltpu.VMEM((devices, 1, length), jnp.int32),
            pltpu.SemaphoreType.DMA((7,)),
        ],
        compiler_params=pltpu.CompilerParams(vmem_limit_bytes=8 * 1024 * 1024),
        name="pack",
    )(*[pltpu.with_memory_space_constraint(array, pltpu.HBM) for array in arrays])


def rows_kernel(fields, even_side, odd_side, even_rows, odd_rows):
    rows, cols = fields.shape[1:]
    last, odd, odd_col = rows - HALO_ROWS, lax.axis_index("gx") & 1, lax.axis_index("gy") & 1
    for out, side in ((even_rows, 1 - odd), (odd_rows, odd)):
        span = pl.ds(pl.multiple_of(last * side, HALO_ROWS), HALO_ROWS)
        out[:, :, :cols] = fields[:, span, :]
        for halo, after in ((even_side, 1 - odd_col), (odd_side, odd_col)):
            at = pl.multiple_of(cols + HALO_COLS * after, HALO_COLS)
            out[:, :, pl.ds(at, HALO_COLS)] = halo[:, span, :]


def pack_rows(fields, even_side, odd_side):
    edge = jax.ShapeDtypeStruct((4, HALO_ROWS, fields.shape[2] + 2 * HALO_COLS), F32)
    vmem = pl.BlockSpec(memory_space=pltpu.VMEM)
    return pl.pallas_call(
        rows_kernel,
        out_shape=[edge, edge],
        in_specs=[vmem] * 3,
        out_specs=[vmem] * 2,
        compiler_params=pltpu.CompilerParams(vmem_limit_bytes=8 * 1024 * 1024),
        name="pack_rows",
    )(fields, even_side, odd_side)


class Level:
    def __init__(self, matrix, names_at, inverse):
        self.matrix, self.names_at, self.inverse = matrix, names_at, inverse
        self.count = matrix.shape[1]

    def entry(self, name, m, k, high):
        at = self.names_at.get(name)
        return None if at is None else self.matrix[at, m, k, :high, :]

    def stress(self, m, k, modes):
        names = "123rc"
        known = {}
        result = []
        for i in range(5):
            terms = []
            for j in range(5):
                name = names[min(i, j)] + names[max(i, j)]
                if name not in known:
                    known[name] = self.entry(name, m, k, modes[0].shape[0])
                if known[name] is not None:
                    terms.append(known[name] * modes[j])
            result.append(plus(*terms))
        return result

    def halves(self, component, m, k):
        if component == 0:
            names = ("11", "33", "rr", "13", "1r", "3r")
        else:
            names = ("22", "33", "cc", "23", "3c", "2c")
        first, second, third, cross, by_col, by_row = [self.entry(name, m, k, self.matrix.shape[3]) for name in names]
        base = first + second + third
        by_row, by_col, cross = 2.0 * by_row, 2.0 * by_col, times(2.0, cross)
        if cross is None:
            return base - by_row, base + by_row, by_col, by_col
        return base - by_row, base + by_row, by_col - cross, by_col + cross

    def components(self):
        return (0, 1)

    def make_inverse(self, row_ok, col_ok):
        count = self.count
        for component in self.components():
            kept = {}
            for k in range(count):
                parts = [self.halves(component, m, k) for m in range(count)]
                for m in range(count):
                    above = parts[m - 1] if m else parts[count - 1]
                    lower = [above[1], above[3]]
                    if m == 0:
                        lower = [from_before(value, 0) for value in lower]
                    even, odd = parts[m][0] + lower[0], parts[m][2] + lower[1]
                    kept[m, k] = (even - odd, even + odd)
            for k in range(count):
                for m in range(count):
                    left = kept[m, k - 1][1] if k else from_before(kept[m, count - 1][1], 1)
                    diagonal = kept[m, k][0] + left
                    value = jnp.where(diagonal > 0.0, 0.5 / diagonal, 0.0)
                    if m == 0:
                        value = value * row_ok
                    if k == 0:
                        value = value * col_ok
                    self.inverse[component, m, k] = value


class FineLevel(Level):
    def stress(self, m, k, modes):
        lame, shear, mixed = [self.matrix[at, m, k, : modes[0].shape[0], :] for at in range(3)]
        first, second, third, bend_row, bend_col = modes
        twice, mean = shear + shear, lame * (first + second)
        return [
            mean + twice * first,
            mean + twice * second,
            shear * third,
            mixed * bend_row,
            mixed * bend_col,
        ]

    def components(self):
        return (0,)

    def make_inverse(self, row_ok, col_ok):
        count = self.count

        @pl.loop(0, count)
        def _(k):
            parts = [self.matrix[2, m, k] for m in range(count)]
            for m in range(count):
                above = parts[m - 1] if m else from_before(parts[count - 1], 0)
                self.inverse[0, m, k] = parts[m] + above

        for m in range(count):
            left = from_before(self.inverse[0, m, count - 1], 1)
            for k in range(count):
                here = self.inverse[0, m, k]
                diagonal = 4.0 * (here + left)
                left = here
                value = jnp.where(diagonal > 0.0, 0.5 / diagonal, 0.0)
                if m == 0:
                    value = value * row_ok
                if k == 0:
                    value = value * col_ok
                self.inverse[0, m, k] = value


def inverse_of(level, component, m, k, high):
    return level.inverse[min(component, len(level.components()) - 1), m, k, :high, :]


def close_columns(level, x):
    count = level.count
    for component in (0, 1):
        for m in range(count):
            x[component, m, count] = from_after(x[component, m, 0], 1)


def start(level, x, source):
    count = level.count

    def column(k):
        for component in (0, 1):
            for m in range(count):
                x[component, m, k] = source[component, m, k] * inverse_of(level, component, m, k, x.shape[3])

    over_columns(count, column)
    close_columns(level, x)


def over_columns(count, column):
    for k in range(count):
        column(k)


def cut(value, height):
    return value if value.shape[0] == height else value[:height]


def apply(level, x, source, out, residual, tall_cells=None, tall_nodes=None):
    count = level.count
    side = x.shape[3]
    cells = [side if tall_cells is None or m in tall_cells else side // 2 for m in range(count)]
    nodes = [side if tall_nodes is None or m in tall_nodes else side // 2 for m in range(count)]
    held = [max(cells[m], cells[m - 1]) if m else side for m in range(count)]
    passed_right = {}

    def column(k):
        sums, steps = [], []
        for m in range(count):
            here = [x[component, m, k, : held[m], :] for component in (0, 1)]
            after = [x[component, m, k + 1, : held[m], :] for component in (0, 1)]
            sums.append([here[c] + after[c] for c in (0, 1)])
            steps.append([after[c] - here[c] for c in (0, 1)])
        sums.append([from_after(value, 0) for value in sums[0]])
        steps.append([from_after(value, 0) for value in steps[0]])
        own, passed = [], []
        for m in range(count):
            sum0, sum1 = [[cut(value, cells[m]) for value in sums[row]] for row in (m, m + 1)]
            step0, step1 = [[cut(value, cells[m]) for value in steps[row]] for row in (m, m + 1)]
            modes = (
                sum1[0] - sum0[0],
                step0[1] + step1[1],
                (step0[0] + step1[0]) + (sum1[1] - sum0[1]),
                step1[0] - step0[0],
                step1[1] - step0[1],
            )
            first, second, third, bend_row, bend_col = level.stress(m, k, modes)
            own.append((first, third - bend_row, third, second - bend_col))
            passed.append((first, third + bend_row, third, second + bend_col))
        for m in range(count):
            high = nodes[m]
            above = passed[m - 1] if m else [from_before(value, 0) for value in passed[count - 1]]
            for component in (0, 1):
                at = 2 * component
                even = cut(above[at], high) - cut(own[m][at], high)
                odd = cut(above[at + 1], high) + cut(own[m][at + 1], high)
                force = even - odd
                if k:
                    force = force + passed_right[component, m]
                passed_right[component, m] = even + odd
                rest = source[component, m, k, :high, :] - force
                if not residual:
                    rest = x[component, m, k, :high, :] + inverse_of(level, component, m, k, high) * rest
                out[component, m, k, :high, :] = rest

    over_columns(count, column)
    for component in (0, 1):
        for m in range(count):
            high = nodes[m]
            left = from_before(passed_right[component, m], 1)
            if not residual:
                left = left * inverse_of(level, component, m, 0, high)
            out[component, m, 0, :high, :] = out[component, m, 0, :high, :] - left
            if not residual:
                out[component, m, count, :high, :] = from_after(out[component, m, 0, :high, :], 1)


def restrict(residual, target, count):
    half = count // 2
    for component in (0, 1):
        for k in range(half):
            lines = []
            for m in range(count):
                odd = residual[component, m, 2 * k + 1]
                if k:
                    before = residual[component, m, 2 * k - 1]
                else:
                    before = from_before(residual[component, m, count - 1], 1)
                lines.append(residual[component, m, 2 * k] + 0.5 * (odd + before))
            for m in range(half):
                before = lines[2 * m - 1] if m else from_before(lines[count - 1], 0)
                target[component, m, k] = lines[2 * m] + 0.5 * (lines[2 * m + 1] + before)


def prolong(coarse, before, x, count, tall=None):
    side = x.shape[3]

    def add(component, m, k, value):
        high = side if tall is None or m in tall else side // 2
        x[component, m, k, :high, :] = before[component, m, k, :high, :] + cut(value, high)

    half = count // 2
    for component in (0, 1):
        planes = {(m, k): coarse(component, m, k) for m in range(half) for k in range(half)}
        for m in range(half):
            planes[m, half] = from_after(planes[m, 0], 1)
        for k in range(half + 1):
            planes[half, k] = from_after(planes[0, k], 0)
        for m in range(half):
            for k in range(half):
                a, b, c, d = planes[m, k], planes[m + 1, k], planes[m, k + 1], planes[m + 1, k + 1]
                add(component, 2 * m, 2 * k, a)
                add(component, 2 * m + 1, 2 * k, 0.5 * (a + b))
                add(component, 2 * m, 2 * k + 1, 0.5 * (a + c))
                add(component, 2 * m + 1, 2 * k + 1, 0.25 * ((a + b) + (c + d)))


def haar(level, names_at, m, k):
    def signed(name, row, col):
        if name not in names_at:
            return None
        value = {
            (a, b): level.matrix[names_at[name], 2 * m + a, 2 * k + b] for a in (0, 1) for b in (0, 1)
        }
        low = value[0, 1] - value[0, 0] if col else value[0, 1] + value[0, 0]
        high = value[1, 1] - value[1, 0] if col else value[1, 1] + value[1, 0]
        return high - low if row else high + low

    return signed


def coarsen_fine(fine, coarse):
    count = coarse.count

    def column(k):
        for m in range(count):
            signed = haar(fine, {"l": 0, "s": 1}, m, k)
            lame, shear = signed("l", 0, 0), signed("s", 0, 0)
            lame_row, shear_row = signed("l", 1, 0), signed("s", 1, 0)
            lame_col, shear_col = signed("l", 0, 1), signed("s", 0, 1)
            lame_both, shear_both = signed("l", 1, 1), signed("s", 1, 1)
            values = {
                "11": 0.25 * (lame + 2.0 * shear),
                "12": 0.25 * lame,
                "33": 0.25 * shear,
                "1r": 0.125 * (lame_col + 2.0 * shear_col),
                "2r": 0.125 * lame_col,
                "3r": 0.125 * shear_row,
                "1c": 0.125 * lame_row,
                "2c": 0.125 * (lame_row + 2.0 * shear_row),
                "3c": 0.125 * shear_col,
                "rr": (lame + 3.0 * shear) * (1.0 / 12.0),
                "rc": 0.0625 * (lame_both + shear_both),
            }
            for name, value in values.items():
                coarse.matrix[FIRST_AT[name], m, k] = value

    over_columns(count, column)


def coarsen(fine, write, count):
    for k in range(count):
        for m in range(count):
            signed = haar(fine, fine.names_at, m, k)

            def total(name):
                return signed(name, 0, 0)

            def by_row(name):
                return signed(name, 1, 0)

            def by_col(name):
                return signed(name, 0, 1)

            def by_both(name):
                return signed(name, 1, 1)

            values = {}
            for name in ("11", "12", "33"):
                values[name] = times(0.25, total(name))
            for i in "123":
                one, two, three = ["".join(sorted(i + j)) for j in "123"]
                values[i + "r"] = 0.125 * plus(by_col(one), by_row(three), total(i + "r"))
                values[i + "c"] = 0.125 * plus(by_row(two), by_col(three), total(i + "c"))
            values["rr"] = 0.0625 * plus(
                total("11"),
                total("33"),
                times(2.0, by_both("13")),
                2.0 * (by_col("1r") + by_row("3r")),
                total("rr"),
            )
            values["cc"] = 0.0625 * plus(
                total("22"),
                total("33"),
                times(2.0, by_both("23")),
                2.0 * (by_row("2c") + by_col("3c")),
                total("cc"),
            )
            values["rc"] = 0.0625 * plus(
                by_both("12"),
                total("13"),
                total("23"),
                by_both("33"),
                by_col("1c"),
                by_row("3c"),
                by_row("2r"),
                by_col("3r"),
                total("rc"),
            )
            for name in FULL:
                write(FULL_AT[name], m, k, values[name])


def edge_masks(shape, before, rows, cols, grid_rows, grid_cols):
    def wrapped(axis, ahead):
        at = lax.broadcasted_iota(jnp.int32, shape, axis)
        return jnp.where(at < shape[axis] - ahead, at, at - shape[axis]) * GROUP

    row = wrapped(0, before) + lax.axis_index("gx") * rows
    col = wrapped(1, HALO_COLS // GROUP) + lax.axis_index("gy") * cols
    return (
        jnp.where(row < grid_rows, 1.0, 0.0).astype(F32),
        jnp.where(col < grid_cols, 1.0, 0.0).astype(F32),
    )


def two_parts(value):
    high = value.astype(BF16)
    return high, (value - high.astype(F32)).astype(BF16)


def turned(value, by):
    return pltpu.roll(value, by % LANES, 1) if by % LANES else value


def gather_lanes(pieces, slot):
    lane = lax.broadcasted_iota(jnp.int32, pieces[0].shape, 1)
    halo = HALO_COLS // GROUP
    own = (len(pieces) - 1) * SPAN
    plane = jnp.where(lane >= LANES - halo, turned(pieces[-1], LANES - halo - slot), 0.0)
    plane = jnp.where(lane < own + halo, turned(pieces[-1], own - halo - slot), plane)
    for at in reversed(range(len(pieces) - 1)):
        plane = jnp.where(lane < (at + 1) * SPAN, turned(pieces[at], at * SPAN - slot), plane)
    return plane


def make_spread(spread):
    at = lax.broadcasted_iota(jnp.int32, (WIDE, WIDE), 0)
    lane = lax.broadcasted_iota(jnp.int32, (WIDE, WIDE), 1)
    spread[...] = jnp.where(lane == (at & (GROUP - 1)) * SPAN + (at >> LEVELS), 1.0, 0.0).astype(BF16)


def spread_fields(load, write, tiles, stacked, spread):
    fields, count, rows = tiles.shape[:3]
    block = rows // GROUP
    make_spread(spread)
    for field in range(fields):
        for tile in range(count):
            load(field, tile)
        for pair in range(GROUP // 2):
            for tile in range(count):
                lines = [tiles[field, tile, pl.ds(2 * pair + h, block, stride=GROUP), :] for h in (0, 1)]
                for part, split in enumerate(two_parts(jnp.concatenate(lines, axis=0))):
                    line = (field * 2 + part) * rows + pair * 2 * block
                    stacked[line : line + 2 * block, tile * LANES : (tile + 1) * LANES] = split
    for field in range(fields):
        pieces = []
        for piece in range(count * LANES // WIDE):
            left = stacked[field * 2 * rows : (field + 1) * 2 * rows, piece * WIDE : (piece + 1) * WIDE]
            product = jnp.dot(left, spread[...], preferred_element_type=F32)
            pieces.append(product[:rows] + product[rows:])
        for m in range(GROUP):
            for k in range(GROUP):
                half, slot = k * SPAN // LANES, k * SPAN % LANES
                lanes = slice(half * LANES, (half + 1) * LANES)
                lines = slice(m * block, (m + 1) * block)
                write(field, m, k, gather_lanes([piece[lines, lanes] for piece in pieces], slot))


def own_kernel(fields, even_side, odd_side, planes, tiles, stacked, spread):
    own_tiles, odd = fields.shape[2] // LANES, lax.axis_index("gy") & 1

    def load(field, tile):
        if tile < own_tiles:
            tiles[field, tile] = fields[field, :, tile * LANES : (tile + 1) * LANES]
        elif tile == own_tiles:
            tiles[field, tile + 1 - odd] = even_side[field]
        else:
            tiles[field, own_tiles + odd] = odd_side[field]

    def write(field, m, k, plane):
        planes[field, m, k] = plane

    spread_fields(load, write, tiles, stacked, spread)


def spread_scratch(rows, wide):
    return [
        pltpu.VMEM((4, wide // LANES, rows, LANES), F32),
        pltpu.VMEM((8 * rows, wide), BF16),
        pltpu.VMEM((WIDE, WIDE), BF16),
    ]


def spread_own(fields, even_side, odd_side):
    rows, wide = fields.shape[1], fields.shape[2] + 2 * HALO_COLS
    vmem = pl.BlockSpec(memory_space=pltpu.VMEM)
    return pl.pallas_call(
        own_kernel,
        out_shape=jax.ShapeDtypeStruct((4, GROUP, GROUP, rows // GROUP, LANES), F32),
        in_specs=[vmem] * 3,
        out_specs=vmem,
        scratch_shapes=spread_scratch(rows, wide),
        compiler_params=pltpu.CompilerParams(vmem_limit_bytes=12 * 1024 * 1024),
        cost_estimate=pl.CostEstimate(flops=16 * rows * wide * WIDE, bytes_accessed=0, transcendentals=0),
        name="spread_own",
    )(fields, even_side, odd_side)


def down_kernel(
    own, even_rows, odd_rows, factor,
    matrix0, inverse0, source0, x0, matrix1, inverse1, source1, x1, matrix2, inverse2, source2, x2, coarsest,
    tiles, stacked, spread, other0, other1, other2, matrix3,
    *, rows, cols, gx, gy,
):
    block = rows // GROUP
    side = block + 2 * HALO_ROWS // GROUP
    row_ok, col_ok = edge_masks(
        (side, LANES), HALO_ROWS // GROUP, rows, cols, gx * rows, gy * cols
    )

    odd = lax.axis_index("gx") & 1

    def load(field, tile):
        lanes = slice(tile * LANES, (tile + 1) * LANES)
        for halo, before in ((even_rows, odd), (odd_rows, 1 - odd)):
            span = pl.ds(pl.multiple_of(HALO_ROWS * before, HALO_ROWS), HALO_ROWS)
            tiles[field, tile, span, :] = halo[field, :, lanes]

    def write(field, m, k, plane):
        if field < 2:
            spans = (slice(0, block), slice(block, side))
            for span, value in zip(spans, (own[field, m, k], plane)):
                value = value * (0.25 * factor[m, k, span, :])
                matrix0[field, m, k, span, :] = value
                if field == 1:
                    matrix0[2, m, k, span, :] = matrix0[0, m, k, span, :] * (1.0 / 3.0) + value
        else:
            source0[field - 2, m, k, :block, :] = own[field, m, k]
            source0[field - 2, m, k, block:, :] = plane

    spread_fields(load, write, tiles, stacked, spread)

    level0 = FineLevel(matrix0, {}, inverse0)
    level1 = Level(matrix1, FIRST_AT, inverse1)
    level2 = Level(matrix2, FULL_AT, inverse2)

    coarsen_fine(level0, level1)

    def write2(at, m, k, value):
        matrix2[at, m, k] = value

    coarsen(level1, write2, level2.count)

    def write3(at, m, k, value):
        matrix3[at] = value

    coarsen(level2, write3, 1)
    for level in (level0, level1, level2):
        level.make_inverse(row_ok, col_ok)

    source3 = matrix3.at[pl.ds(len(FULL), 2)]
    chain = (
        (level0, source0, x0, other0, source1),
        (level1, source1, x1, other1, source2),
        (level2, source2, x2, other2, None),
    )
    for level, source, x, other, target in chain:
        start(level, other, source)
        apply(level, other, source, x, residual=False)
        apply(level, x, source, other, residual=True)
        if target is not None:
            restrict(other, target, level.count)
        else:
            restrict_last(other, source3)
    for at in range(len(FULL) + 2):
        coarsest[at] = matrix3[at, :block, :]


def restrict_last(residual, target):
    class Planes:
        def __setitem__(self, where, value):
            target[where[0]] = value

    restrict(residual, Planes(), 2)


def up_kernel(
    coarse, coarse_even, coarse_odd,
    matrix0, inverse0, source0, x0_in, matrix1, inverse1, source1, x1_in, matrix2, inverse2, source2, x2_in,
    displacement,
    x0, other0, x1, other1, x2, other2, matrix3, inverse3, source3, x3,
    stacked, gathered, tiles,
    *, rows, cols, gx, gy,
):
    block, odd = rows // GROUP, lax.axis_index("gx") & 1
    for at in range(len(FULL) + 2):
        for piece, part in ((0, coarse), (1 + odd, coarse_even), (2 - odd, coarse_odd)):
            lines = pl.ds(pl.multiple_of(piece * block, block), block)
            if at < len(FULL):
                matrix3[at, 0, 0, lines, :] = part[at]
            else:
                source3[at - len(FULL), 0, 0, lines, :] = part[at]
    level3 = Level(matrix3, FULL_AT, inverse3)
    level3.make_inverse(*edge_masks((3 * block, LANES), block, rows, cols, gx * rows, gy * cols))
    relax(level3, source3, x3)
    now = x3
    coarse_plane = functools.partial(cut_plane, now, block)

    level0 = FineLevel(matrix0, {}, inverse0)
    level1 = Level(matrix1, FIRST_AT, inverse1)
    level2 = Level(matrix2, FULL_AT, inverse2)
    for level, source, before, x, other in (
        (level2, source2, x2_in, x2, other2),
        (level1, source1, x1_in, x1, other1),
        (level0, source0, x0_in, x0, other0),
    ):
        last = level.count - 1
        prolong(coarse_plane, before, x, level.count, {0, 1, last - 1, last} if level is level0 else None)
        close_columns(level, x)
        if level is level0:
            apply(level, x, source, other, False, {0, last - 1, last}, {0, last})
            apply(level, other, source, x, False, {last}, set())
        else:
            apply(level, x, source, other, residual=False)
            apply(level, other, source, x, residual=False)
        coarse_plane = functools.partial(whole_plane, x)

    at = lax.broadcasted_iota(jnp.int32, (WIDE, WIDE), 1)
    line = lax.broadcasted_iota(jnp.int32, (WIDE, WIDE), 0)
    gathered[...] = jnp.where(line == (at & (GROUP - 1)) * SPAN + (at >> LEVELS), 1.0, 0.0).astype(BF16)
    lane = lax.broadcasted_iota(jnp.int32, (2 * block, LANES), 1)
    for component in (0, 1):
        for pair in range(GROUP // 2):
            values = [
                jnp.concatenate(
                    [x0[component, 2 * pair + h, k, :block, :] for h in (0, 1)], axis=0
                )
                for k in range(GROUP)
            ]
            for piece in range(cols // WIDE):
                for half in range(WIDE // LANES):
                    slots = LANES // SPAN
                    value = None
                    for slot in reversed(range(slots)):
                        part = turned(values[half * slots + slot], (slot - piece) * SPAN)
                        value = part if value is None else jnp.where(lane < (slot + 1) * SPAN, part, value)
                    lanes = slice(piece * WIDE + half * LANES, piece * WIDE + (half + 1) * LANES)
                    for part, split in enumerate(two_parts(value)):
                        line = part * 2 * rows + component * rows + pair * 2 * block
                        stacked[line : line + 2 * block, lanes] = split
    pieces = []
    for piece in range(cols // WIDE):
        product = jnp.dot(
            stacked[:, piece * WIDE : (piece + 1) * WIDE], gathered[...], preferred_element_type=F32
        )
        pieces.append(product[: 2 * rows] + product[2 * rows :])
    for component in (0, 1):
        for tile in range(cols // LANES):
            lanes = slice(tile * LANES, (tile + 1) * LANES)
            for m in range(GROUP):
                line = component * rows + m * block
                tiles[component, tile, pl.ds(m, block, stride=GROUP), :] = pieces[tile * LANES // WIDE][
                    line : line + block, tile * LANES % WIDE : tile * LANES % WIDE + LANES
                ]
            displacement[component, :, lanes] = tiles[component, tile]


def relax(level, source, out):
    right = [source[component, 0, 0] for component in (0, 1)]
    inverse = [inverse_of(level, component, 0, 0, out.shape[3]) for component in (0, 1)]
    x = [right[c] * inverse[c] for c in (0, 1)]
    for _ in range(COARSE_SWEEPS - 1):
        after = [from_after(value, 1) for value in x]
        sums = [x[c] + after[c] for c in (0, 1)]
        steps = [after[c] - x[c] for c in (0, 1)]
        sum1, step1 = [[from_after(value, 0) for value in pair] for pair in (sums, steps)]
        modes = (
            sum1[0] - sums[0],
            steps[1] + step1[1],
            (steps[0] + step1[0]) + (sum1[1] - sums[1]),
            step1[0] - steps[0],
            step1[1] - steps[1],
        )
        first, second, third, bend_row, bend_col = level.stress(0, 0, modes)
        own = (first, third - bend_row, third, second - bend_col)
        above = [from_before(v, 0) for v in (first, third + bend_row, third, second + bend_col)]
        for c in (0, 1):
            even, odd = above[2 * c] - own[2 * c], above[2 * c + 1] + own[2 * c + 1]
            rest = right[c] - ((even - odd) + from_before(even + odd, 1))
            x[c] = x[c] + inverse[c] * rest
    for component in (0, 1):
        out[component, 0, 0] = x[component]


def cut_plane(x, block, component, m, k):
    line = lax.broadcasted_iota(jnp.int32, (block, LANES), 0)
    halo = jnp.where(
        line < HALO_ROWS // GROUP,
        x[component, 0, 0, block : 2 * block, :],
        x[component, 0, 0, 2 * block :, :],
    )
    return jnp.concatenate([x[component, 0, 0, :block, :], halo], axis=0)


def whole_plane(x, component, m, k):
    return x[component, m, k]


def body(first_lame, shear_modulus, applied_load, plastic_owner, plastic_cell, plastic_code):
    rows, cols = first_lame.shape
    gx, gy = lax.axis_size("gx"), lax.axis_size("gy")
    devices = gx * gy

    fields, even_cols, odd_cols, words = pack(
        first_lame, shear_modulus, applied_load, plastic_owner, plastic_cell, plastic_code, devices
    )
    even_side, odd_side = swapped(even_cols, "gy", 0), swapped(odd_cols, "gy", 1)
    words = lax.all_to_all(words, ("gx", "gy"), 0, 0, tiled=True)

    even_rows, odd_rows = pack_rows(fields, even_side, odd_side)
    even_rows, odd_rows = swapped(even_rows, "gx", 0), swapped(odd_rows, "gx", 1)
    own = spread_own(fields, even_side, odd_side)
    words, own = lax.optimization_barrier((words, own))
    factor = yield_factor(words, rows, cols, gy)

    tall, wide = rows + 2 * HALO_ROWS, cols + 2 * HALO_COLS
    side = tall // GROUP
    vmem = pl.BlockSpec(memory_space=pltpu.VMEM)

    def planes(fields, count, extra=0, lines=side):
        return (fields, count, count + extra, lines, LANES)

    state = []
    for count, entries, inverses in ((GROUP, 3, 1), (GROUP // 2, len(FIRST), 2), (GROUP // 4, len(FULL), 2)):
        state += [planes(entries, count), planes(inverses, count), planes(2, count), planes(2, count, 1)]
    held = len(FULL) + 2
    counts = (GROUP, GROUP // 2, GROUP // 4)
    *state, coarse = pl.pallas_call(
        functools.partial(down_kernel, rows=rows, cols=cols, gx=gx, gy=gy),
        out_shape=[jax.ShapeDtypeStruct(shape, F32) for shape in state]
        + [jax.ShapeDtypeStruct((held, rows // GROUP, LANES), F32)],
        in_specs=[vmem] * 4,
        out_specs=[vmem] * (len(state) + 1),
        scratch_shapes=spread_scratch(2 * HALO_ROWS, wide)
        + [pltpu.VMEM(planes(2, count, 1), F32) for count in counts]
        + [pltpu.VMEM((held, side, LANES), F32)],
        compiler_params=pltpu.CompilerParams(vmem_limit_bytes=VMEM_LIMIT),
        name="descent",
    )(own, even_rows, odd_rows, factor)

    coarse_even, coarse_odd = swapped(coarse, "gx", 0), swapped(coarse, "gx", 1)
    lines = 3 * (rows // GROUP)
    return pl.pallas_call(
        functools.partial(up_kernel, rows=rows, cols=cols, gx=gx, gy=gy),
        out_shape=jax.ShapeDtypeStruct((2, rows, cols), F32),
        in_specs=[vmem] * (3 + len(state)),
        out_specs=vmem,
        scratch_shapes=[
            shape
            for count in counts
            for shape in (pltpu.VMEM(planes(2, count, 1), F32),) * 2
        ]
        + [
            pltpu.VMEM(planes(len(FULL), 1, 0, lines), F32),
            pltpu.VMEM(planes(2, 1, 0, lines), F32),
            pltpu.VMEM(planes(2, 1, 0, lines), F32),
            pltpu.VMEM(planes(2, 1, 0, lines), F32),
            pltpu.VMEM((4 * rows, cols), BF16),
            pltpu.VMEM((WIDE, WIDE), BF16),
            pltpu.VMEM((2, cols // LANES, rows, LANES), F32),
        ],
        compiler_params=pltpu.CompilerParams(vmem_limit_bytes=VMEM_LIMIT),
        name="ascent",
    )(coarse, coarse_even, coarse_odd, *state)


def solution(mesh):
    return jax.shard_map(
        body,
        mesh=mesh,
        in_specs=(
            P("gx", "gy"),
            P("gx", "gy"),
            P(None, "gx", "gy"),
            P(("gx", "gy"), None),
            P(("gx", "gy")),
            P(("gx", "gy")),
        ),
        out_specs=P(None, "gx", "gy"),
        check_vma=False,
    )
```

```python
import functools
import math

import jax
import jax.numpy as jnp
import numpy as np
from jax import lax
from jax.experimental import pallas as pl
from jax.experimental.pallas import tpu as pltpu
from jax.sharding import PartitionSpec as P

LEVELS = 3
SWEEPS = 2
COARSE_SWEEPS = 6
YIELD_DROP = 0.6
GROUP = 1 << LEVELS
HALO_ROWS = 32
HALO_COLS = 128
LANES = 128
WIDE = 2 * LANES
SPAN = WIDE // GROUP
LISTS_AT_ONCE = 16
VMEM_LIMIT = 30 * 1024 * 1024
F32 = jnp.float32
BF16 = jnp.bfloat16

FIRST = ("11", "12", "33", "1r", "2r", "3r", "1c", "2c", "3c", "rr", "rc")
FULL = FIRST + ("cc",)
FIRST_AT = {name: FIRST.index(name) for name in FIRST} | {"22": 0, "cc": FIRST.index("rr")}
FULL_AT = {name: FULL.index(name) for name in FULL} | {"22": 0}


def swapped(array, axis, odd_pairs):
    devices = lax.axis_size(axis)
    pairs = []
    for i in range(odd_pairs, devices - 1, 2):
        pairs += [(i, i + 1), (i + 1, i)]
    return lax.ppermute(array, axis, pairs)


def log2(number):
    power = number.bit_length() - 1
    assert 1 << power == number
    return power


def from_before(value, axis):
    return pltpu.roll(value, 1, axis)


def from_after(value, axis):
    return pltpu.roll(value, value.shape[axis] - 1, axis)


def plus(*terms):
    total = None
    for term in terms:
        if term is not None:
            total = term if total is None else total + term
    return total


def times(weight, term):
    return None if term is None else weight * term


def factor_kernel(words, factor, tall_of, lane_of, codes, counts, *, rows, cols, gy):
    for at in range(words.shape[0]):
        tall_of[at : at + 1, :] = words[at]
    word = tall_of[...]
    cell_bits = log2(rows * cols)
    owner = word >> (cell_bits + 2)
    cell = (word >> 2) & (rows * cols - 1)
    row = (owner >> log2(gy)) * rows + (cell >> log2(cols)) - lax.axis_index("gx") * rows
    col = (owner & (gy - 1)) * cols + (cell & (cols - 1)) - lax.axis_index("gy") * cols
    tall = rows + 2 * HALO_ROWS
    side = tall // GROUP
    inside = (row >= -HALO_ROWS) & (row < rows + HALO_ROWS) & (col >= -HALO_COLS) & (col < cols + HALO_COLS)
    at = jnp.where(col < 0, col + cols + HALO_COLS, jnp.where(col >= cols, col + HALO_COLS, col))
    line = (row & (GROUP - 1)) * side + ((row >> LEVELS) & (side - 1))
    tall_of[...] = jnp.where(inside, line + tall * (at >> log2(WIDE)), -1)
    lane_of[...] = (at & (GROUP - 1)) * SPAN + ((at & (WIDE - 1)) >> LEVELS)
    codes[...] = (word & 3).astype(F32)
    counts[...] = jnp.zeros_like(counts)
    length = words.shape[2]
    group = min(LISTS_AT_ONCE, words.shape[0])

    @pl.loop(0, words.shape[0] // group)
    def _(i):
        tall_id = lax.broadcasted_iota(jnp.int32, (counts.shape[0], length), 0)
        lane_id = lax.broadcasted_iota(jnp.int32, (WIDE, length), 0)
        by_tall, by_lane = [], []
        for j in range(group):
            line = pl.ds(i * group + j, 1)
            by_tall.append(jnp.where(tall_id == tall_of[line, :], codes[line, :], 0.0).astype(BF16))
            by_lane.append(jnp.where(lane_id == lane_of[line, :], 1.0, 0.0).astype(BF16))
        counts[...] += lax.dot_general(
            jnp.concatenate(by_tall, axis=1),
            jnp.concatenate(by_lane, axis=1),
            (((1,), (1,)), ((), ())),
            preferred_element_type=F32,
        )

    for m in range(GROUP):
        for k in range(GROUP):
            half, slot = k * SPAN // LANES, k * SPAN % LANES
            lanes = slice(half * LANES, (half + 1) * LANES)
            lines = range(m * side, counts.shape[0], tall)
            count = gather_lanes([counts[line : line + side, lanes] for line in lines], slot)
            factor[m, k] = jnp.exp(count * math.log(YIELD_DROP))


def yield_factor(words, rows, cols, gy):
    tall, wide = rows + 2 * HALO_ROWS, cols + 2 * HALO_COLS
    lists = (words.shape[0], words.shape[2])
    return pl.pallas_call(
        functools.partial(factor_kernel, rows=rows, cols=cols, gy=gy),
        out_shape=jax.ShapeDtypeStruct((GROUP, GROUP, tall // GROUP, LANES), F32),
        in_specs=[pl.BlockSpec(memory_space=pltpu.VMEM)],
        out_specs=pl.BlockSpec(memory_space=pltpu.VMEM),
        scratch_shapes=[
            pltpu.VMEM(lists, jnp.int32),
            pltpu.VMEM(lists, jnp.int32),
            pltpu.VMEM(lists, F32),
            pltpu.VMEM((tall * wide // WIDE, WIDE), F32),
        ],
        compiler_params=pltpu.CompilerParams(vmem_limit_bytes=VMEM_LIMIT),
        cost_estimate=pl.CostEstimate(
            flops=2 * tall * wide * words.size, bytes_accessed=4 * words.size, transcendentals=tall * wide
        ),
        name="yield_factor",
    )(words)


def pack_kernel(
    first_lame, shear_modulus, applied_load, owner, cell, code,
    fields, even_cols, odd_cols, words, lists, copied, arrived,
    *, cells,
):
    copies = [
        pltpu.make_async_copy(source, target, arrived.at[at])
        for at, (source, target) in enumerate(
            (
                (owner, lists.at[0]),
                (cell, lists.at[1]),
                (code, lists.at[2]),
                (first_lame, fields.at[0]),
                (shear_modulus, fields.at[1]),
                (applied_load, fields.at[pl.ds(2, 2)]),
            )
        )
    ]
    for copy in copies:
        copy.start()
    for copy in copies[:3]:
        copy.wait()
    word = (lists[0] * cells + lists[1]) * 4 + lists[2]
    for device in range(words.shape[0]):
        copied[device] = word
    sent = pltpu.make_async_copy(copied, words, arrived.at[6])
    sent.start()
    for copy in copies[3:]:
        copy.wait()
    last, odd = fields.shape[2] - HALO_COLS, lax.axis_index("gy") & 1
    even_cols[...] = fields[:, :, pl.ds(pl.multiple_of(last * (1 - odd), HALO_COLS), HALO_COLS)]
    odd_cols[...] = fields[:, :, pl.ds(pl.multiple_of(last * odd, HALO_COLS), HALO_COLS)]
    sent.wait()


def pack(first_lame, shear_modulus, applied_load, owner, cell, code, devices):
    rows, cols = first_lame.shape
    edge = jax.ShapeDtypeStruct((4, rows, HALO_COLS), F32)
    length = cell.shape[0]
    arrays = [first_lame, shear_modulus, applied_load] + [part.reshape(1, -1) for part in (owner, cell, code)]
    hbm, vmem = pl.BlockSpec(memory_space=pltpu.HBM), pl.BlockSpec(memory_space=pltpu.VMEM)
    return pl.pallas_call(
        functools.partial(pack_kernel, cells=rows * cols),
        out_shape=[
            jax.ShapeDtypeStruct((4, rows, cols), F32),
            edge,
            edge,
            jax.ShapeDtypeStruct((devices, 1, length), jnp.int32),
        ],
        in_specs=[hbm] * 6,
        out_specs=[vmem] * 3 + [hbm],
        scratch_shapes=[
            pltpu.VMEM((3, 1, length), jnp.int32),
            pltpu.VMEM((devices, 1, length), jnp.int32),
            pltpu.SemaphoreType.DMA((7,)),
        ],
        compiler_params=pltpu.CompilerParams(vmem_limit_bytes=8 * 1024 * 1024),
        name="pack",
    )(*[pltpu.with_memory_space_constraint(array, pltpu.HBM) for array in arrays])


def rows_kernel(fields, even_side, odd_side, even_rows, odd_rows):
    rows, cols = fields.shape[1:]
    last, odd, odd_col = rows - HALO_ROWS, lax.axis_index("gx") & 1, lax.axis_index("gy") & 1
    for out, side in ((even_rows, 1 - odd), (odd_rows, odd)):
        span = pl.ds(pl.multiple_of(last * side, HALO_ROWS), HALO_ROWS)
        out[:, :, :cols] = fields[:, span, :]
        for halo, after in ((even_side, 1 - odd_col), (odd_side, odd_col)):
            at = pl.multiple_of(cols + HALO_COLS * after, HALO_COLS)
            out[:, :, pl.ds(at, HALO_COLS)] = halo[:, span, :]


def pack_rows(fields, even_side, odd_side):
    edge = jax.ShapeDtypeStruct((4, HALO_ROWS, fields.shape[2] + 2 * HALO_COLS), F32)
    vmem = pl.BlockSpec(memory_space=pltpu.VMEM)
    return pl.pallas_call(
        rows_kernel,
        out_shape=[edge, edge],
        in_specs=[vmem] * 3,
        out_specs=[vmem] * 2,
        compiler_params=pltpu.CompilerParams(vmem_limit_bytes=8 * 1024 * 1024),
        name="pack_rows",
    )(fields, even_side, odd_side)


class Level:
    def __init__(self, matrix, names_at, inverse):
        self.matrix, self.names_at, self.inverse = matrix, names_at, inverse
        self.count = matrix.shape[1]

    def entry(self, name, m, k, high):
        at = self.names_at.get(name)
        return None if at is None else self.matrix[at, m, k, :high, :]

    def stress(self, m, k, modes):
        names = "123rc"
        known = {}
        result = []
        for i in range(5):
            terms = []
            for j in range(5):
                name = names[min(i, j)] + names[max(i, j)]
                if name not in known:
                    known[name] = self.entry(name, m, k, modes[0].shape[0])
                if known[name] is not None:
                    terms.append(known[name] * modes[j])
            result.append(plus(*terms))
        return result

    def halves(self, component, m, k):
        if component == 0:
            names = ("11", "33", "rr", "13", "1r", "3r")
        else:
            names = ("22", "33", "cc", "23", "3c", "2c")
        first, second, third, cross, by_col, by_row = [self.entry(name, m, k, self.matrix.shape[3]) for name in names]
        base = first + second + third
        by_row, by_col, cross = 2.0 * by_row, 2.0 * by_col, times(2.0, cross)
        if cross is None:
            return base - by_row, base + by_row, by_col, by_col
        return base - by_row, base + by_row, by_col - cross, by_col + cross

    def components(self):
        return (0, 1)

    def make_inverse(self, row_ok, col_ok):
        count = self.count
        for component in self.components():
            kept = {}
            for k in range(count):
                parts = [self.halves(component, m, k) for m in range(count)]
                for m in range(count):
                    above = parts[m - 1] if m else parts[count - 1]
                    lower = [above[1], above[3]]
                    if m == 0:
                        lower = [from_before(value, 0) for value in lower]
                    even, odd = parts[m][0] + lower[0], parts[m][2] + lower[1]
                    kept[m, k] = (even - odd, even + odd)
            for k in range(count):
                for m in range(count):
                    left = kept[m, k - 1][1] if k else from_before(kept[m, count - 1][1], 1)
                    diagonal = kept[m, k][0] + left
                    value = jnp.where(diagonal > 0.0, 0.5 / diagonal, 0.0)
                    if m == 0:
                        value = value * row_ok
                    if k == 0:
                        value = value * col_ok
                    self.inverse[component, m, k] = value


class FineLevel(Level):
    def stress(self, m, k, modes):
        lame, shear, mixed = [self.matrix[at, m, k, : modes[0].shape[0], :] for at in range(3)]
        first, second, third, bend_row, bend_col = modes
        twice, mean = shear + shear, lame * (first + second)
        return [
            mean + twice * first,
            mean + twice * second,
            shear * third,
            mixed * bend_row,
            mixed * bend_col,
        ]

    def components(self):
        return (0,)

    def make_inverse(self, row_ok, col_ok):
        count = self.count

        def pair_sums(k):
            parts = [self.matrix[2, m, k] for m in range(count)]
            return [parts[m] + (parts[m - 1] if m else from_before(parts[count - 1], 0)) for m in range(count)]

        left = [from_before(value, 1) for value in pair_sums(count - 1)]
        for k in range(count):
            here = pair_sums(k)
            for m in range(count):
                diagonal = 4.0 * (here[m] + left[m])
                value = jnp.where(diagonal > 0.0, 0.5 / diagonal, 0.0)
                if m == 0:
                    value = value * row_ok
                if k == 0:
                    value = value * col_ok
                self.inverse[0, m, k] = value
            left = here


def inverse_of(level, component, m, k, high):
    return level.inverse[min(component, len(level.components()) - 1), m, k, :high, :]


def close_columns(level, x):
    count = level.count
    for component in (0, 1):
        for m in range(count):
            x[component, m, count] = from_after(x[component, m, 0], 1)


def start(level, x, source):
    count = level.count

    def column(k):
        for component in (0, 1):
            for m in range(count):
                x[component, m, k] = source[component, m, k] * inverse_of(level, component, m, k, x.shape[3])

    over_columns(count, column)
    close_columns(level, x)


def over_columns(count, column):
    for k in range(count):
        column(k)


def cut(value, height):
    return value if value.shape[0] == height else value[:height]


def apply(level, x, source, out, residual, tall_cells=None, tall_nodes=None):
    count = level.count
    side = x.shape[3]
    cells = [side if tall_cells is None or m in tall_cells else side // 2 for m in range(count)]
    nodes = [side if tall_nodes is None or m in tall_nodes else side // 2 for m in range(count)]
    held = [max(cells[m], cells[m - 1]) if m else side for m in range(count)]
    passed_right = {}

    def column(k):
        sums, steps = [], []
        for m in range(count):
            here = [x[component, m, k, : held[m], :] for component in (0, 1)]
            after = [x[component, m, k + 1, : held[m], :] for component in (0, 1)]
            sums.append([here[c] + after[c] for c in (0, 1)])
            steps.append([after[c] - here[c] for c in (0, 1)])
        sums.append([from_after(value, 0) for value in sums[0]])
        steps.append([from_after(value, 0) for value in steps[0]])
        own, passed = [], []
        for m in range(count):
            sum0, sum1 = [[cut(value, cells[m]) for value in sums[row]] for row in (m, m + 1)]
            step0, step1 = [[cut(value, cells[m]) for value in steps[row]] for row in (m, m + 1)]
            modes = (
                sum1[0] - sum0[0],
                step0[1] + step1[1],
                (step0[0] + step1[0]) + (sum1[1] - sum0[1]),
                step1[0] - step0[0],
                step1[1] - step0[1],
            )
            first, second, third, bend_row, bend_col = level.stress(m, k, modes)
            own.append((first, third - bend_row, third, second - bend_col))
            passed.append((first, third + bend_row, third, second + bend_col))
        for m in range(count):
            high = nodes[m]
            above = passed[m - 1] if m else [from_before(value, 0) for value in passed[count - 1]]
            for component in (0, 1):
                at = 2 * component
                even = cut(above[at], high) - cut(own[m][at], high)
                odd = cut(above[at + 1], high) + cut(own[m][at + 1], high)
                force = even - odd
                if k:
                    force = force + passed_right[component, m]
                passed_right[component, m] = even + odd
                rest = source[component, m, k, :high, :] - force
                if not residual:
                    rest = x[component, m, k, :high, :] + inverse_of(level, component, m, k, high) * rest
                out[component, m, k, :high, :] = rest

    over_columns(count, column)
    for component in (0, 1):
        for m in range(count):
            high = nodes[m]
            left = from_before(passed_right[component, m], 1)
            if not residual:
                left = left * inverse_of(level, component, m, 0, high)
            out[component, m, 0, :high, :] = out[component, m, 0, :high, :] - left
            if not residual:
                out[component, m, count, :high, :] = from_after(out[component, m, 0, :high, :], 1)


def restrict(residual, target, count):
    half = count // 2
    for component in (0, 1):
        for k in range(half):
            lines = []
            for m in range(count):
                odd = residual[component, m, 2 * k + 1]
                if k:
                    before = residual[component, m, 2 * k - 1]
                else:
                    before = from_before(residual[component, m, count - 1], 1)
                lines.append(residual[component, m, 2 * k] + 0.5 * (odd + before))
            for m in range(half):
                before = lines[2 * m - 1] if m else from_before(lines[count - 1], 0)
                target[component, m, k] = lines[2 * m] + 0.5 * (lines[2 * m + 1] + before)


def prolong(coarse, before, x, count, tall=None):
    side = x.shape[3]

    def add(component, m, k, value):
        high = side if tall is None or m in tall else side // 2
        x[component, m, k, :high, :] = before[component, m, k, :high, :] + cut(value, high)

    half = count // 2
    for component in (0, 1):
        planes = {(m, k): coarse(component, m, k) for m in range(half) for k in range(half)}
        for m in range(half):
            planes[m, half] = from_after(planes[m, 0], 1)
        for k in range(half + 1):
            planes[half, k] = from_after(planes[0, k], 0)
        for m in range(half):
            for k in range(half):
                a, b, c, d = planes[m, k], planes[m + 1, k], planes[m, k + 1], planes[m + 1, k + 1]
                add(component, 2 * m, 2 * k, a)
                add(component, 2 * m + 1, 2 * k, 0.5 * (a + b))
                add(component, 2 * m, 2 * k + 1, 0.5 * (a + c))
                add(component, 2 * m + 1, 2 * k + 1, 0.25 * ((a + b) + (c + d)))


def haar(level, names_at, m, k):
    def signed(name, row, col):
        if name not in names_at:
            return None
        value = {
            (a, b): level.matrix[names_at[name], 2 * m + a, 2 * k + b] for a in (0, 1) for b in (0, 1)
        }
        low = value[0, 1] - value[0, 0] if col else value[0, 1] + value[0, 0]
        high = value[1, 1] - value[1, 0] if col else value[1, 1] + value[1, 0]
        return high - low if row else high + low

    return signed


def coarsen_fine(fine, coarse):
    count = coarse.count

    def column(k):
        for m in range(count):
            signed = haar(fine, {"l": 0, "s": 1}, m, k)
            lame, shear = signed("l", 0, 0), signed("s", 0, 0)
            lame_row, shear_row = signed("l", 1, 0), signed("s", 1, 0)
            lame_col, shear_col = signed("l", 0, 1), signed("s", 0, 1)
            lame_both, shear_both = signed("l", 1, 1), signed("s", 1, 1)
            values = {
                "11": 0.25 * (lame + 2.0 * shear),
                "12": 0.25 * lame,
                "33": 0.25 * shear,
                "1r": 0.125 * (lame_col + 2.0 * shear_col),
                "2r": 0.125 * lame_col,
                "3r": 0.125 * shear_row,
                "1c": 0.125 * lame_row,
                "2c": 0.125 * (lame_row + 2.0 * shear_row),
                "3c": 0.125 * shear_col,
                "rr": (lame + 3.0 * shear) * (1.0 / 12.0),
                "rc": 0.0625 * (lame_both + shear_both),
            }
            for name, value in values.items():
                coarse.matrix[FIRST_AT[name], m, k] = value

    over_columns(count, column)


def coarsen(fine, write, count):
    for k in range(count):
        for m in range(count):
            signed = haar(fine, fine.names_at, m, k)

            def total(name):
                return signed(name, 0, 0)

            def by_row(name):
                return signed(name, 1, 0)

            def by_col(name):
                return signed(name, 0, 1)

            def by_both(name):
                return signed(name, 1, 1)

            values = {}
            for name in ("11", "12", "33"):
                values[name] = times(0.25, total(name))
            for i in "123":
                one, two, three = ["".join(sorted(i + j)) for j in "123"]
                values[i + "r"] = 0.125 * plus(by_col(one), by_row(three), total(i + "r"))
                values[i + "c"] = 0.125 * plus(by_row(two), by_col(three), total(i + "c"))
            values["rr"] = 0.0625 * plus(
                total("11"),
                total("33"),
                times(2.0, by_both("13")),
                2.0 * (by_col("1r") + by_row("3r")),
                total("rr"),
            )
            values["cc"] = 0.0625 * plus(
                total("22"),
                total("33"),
                times(2.0, by_both("23")),
                2.0 * (by_row("2c") + by_col("3c")),
                total("cc"),
            )
            values["rc"] = 0.0625 * plus(
                by_both("12"),
                total("13"),
                total("23"),
                by_both("33"),
                by_col("1c"),
                by_row("3c"),
                by_row("2r"),
                by_col("3r"),
                total("rc"),
            )
            for name in FULL:
                write(FULL_AT[name], m, k, values[name])


def edge_masks(shape, before, rows, cols, grid_rows, grid_cols):
    def wrapped(axis, ahead):
        at = lax.broadcasted_iota(jnp.int32, shape, axis)
        return jnp.where(at < shape[axis] - ahead, at, at - shape[axis]) * GROUP

    row = wrapped(0, before) + lax.axis_index("gx") * rows
    col = wrapped(1, HALO_COLS // GROUP) + lax.axis_index("gy") * cols
    return (
        jnp.where(row < grid_rows, 1.0, 0.0).astype(F32),
        jnp.where(col < grid_cols, 1.0, 0.0).astype(F32),
    )


def two_parts(value):
    high = value.astype(BF16)
    return high, (value - high.astype(F32)).astype(BF16)


def turned(value, by):
    return pltpu.roll(value, by % LANES, 1) if by % LANES else value


def gather_lanes(pieces, slot):
    lane = lax.broadcasted_iota(jnp.int32, pieces[0].shape, 1)
    halo = HALO_COLS // GROUP
    own = (len(pieces) - 1) * SPAN
    plane = jnp.where(lane >= LANES - halo, turned(pieces[-1], LANES - halo - slot), 0.0)
    plane = jnp.where(lane < own + halo, turned(pieces[-1], own - halo - slot), plane)
    for at in reversed(range(len(pieces) - 1)):
        plane = jnp.where(lane < (at + 1) * SPAN, turned(pieces[at], at * SPAN - slot), plane)
    return plane


def make_spread(spread):
    at = lax.broadcasted_iota(jnp.int32, (WIDE, WIDE), 0)
    lane = lax.broadcasted_iota(jnp.int32, (WIDE, WIDE), 1)
    spread[...] = jnp.where(lane == (at & (GROUP - 1)) * SPAN + (at >> LEVELS), 1.0, 0.0).astype(BF16)


def spread_fields(load, write, tiles, stacked, spread):
    fields, count, rows = tiles.shape[:3]
    block = rows // GROUP
    make_spread(spread)
    for field in range(fields):
        for tile in range(count):
            load(field, tile)
        for pair in range(GROUP // 2):
            for tile in range(count):
                lines = [tiles[field, tile, pl.ds(2 * pair + h, block, stride=GROUP), :] for h in (0, 1)]
                for part, split in enumerate(two_parts(jnp.concatenate(lines, axis=0))):
                    line = (field * 2 + part) * rows + pair * 2 * block
                    stacked[line : line + 2 * block, tile * LANES : (tile + 1) * LANES] = split
    for field in range(fields):
        pieces = []
        for piece in range(count * LANES // WIDE):
            left = stacked[field * 2 * rows : (field + 1) * 2 * rows, piece * WIDE : (piece + 1) * WIDE]
            product = jnp.dot(left, spread[...], preferred_element_type=F32)
            pieces.append(product[:rows] + product[rows:])
        for m in range(GROUP):
            for k in range(GROUP):
                half, slot = k * SPAN // LANES, k * SPAN % LANES
                lanes = slice(half * LANES, (half + 1) * LANES)
                lines = slice(m * block, (m + 1) * block)
                write(field, m, k, gather_lanes([piece[lines, lanes] for piece in pieces], slot))


def own_kernel(fields, even_side, odd_side, planes, tiles, stacked, spread):
    own_tiles, odd = fields.shape[2] // LANES, lax.axis_index("gy") & 1

    def load(field, tile):
        if tile < own_tiles:
            tiles[field, tile] = fields[field, :, tile * LANES : (tile + 1) * LANES]
        elif tile == own_tiles:
            tiles[field, tile + 1 - odd] = even_side[field]
        else:
            tiles[field, own_tiles + odd] = odd_side[field]

    def write(field, m, k, plane):
        planes[field, m, k] = plane

    spread_fields(load, write, tiles, stacked, spread)


def spread_scratch(rows, wide):
    return [
        pltpu.VMEM((4, wide // LANES, rows, LANES), F32),
        pltpu.VMEM((8 * rows, wide), BF16),
        pltpu.VMEM((WIDE, WIDE), BF16),
    ]


def spread_own(fields, even_side, odd_side):
    rows, wide = fields.shape[1], fields.shape[2] + 2 * HALO_COLS
    vmem = pl.BlockSpec(memory_space=pltpu.VMEM)
    return pl.pallas_call(
        own_kernel,
        out_shape=jax.ShapeDtypeStruct((4, GROUP, GROUP, rows // GROUP, LANES), F32),
        in_specs=[vmem] * 3,
        out_specs=vmem,
        scratch_shapes=spread_scratch(rows, wide),
        compiler_params=pltpu.CompilerParams(vmem_limit_bytes=12 * 1024 * 1024),
        cost_estimate=pl.CostEstimate(flops=16 * rows * wide * WIDE, bytes_accessed=0, transcendentals=0),
        name="spread_own",
    )(fields, even_side, odd_side)


def down_kernel(
    own, even_rows, odd_rows, factor,
    matrix0, inverse0, source0, x0, matrix1, inverse1, source1, x1, matrix2, inverse2, source2, x2, coarsest,
    tiles, stacked, spread, other0, other1, other2, matrix3,
    *, rows, cols, gx, gy,
):
    block = rows // GROUP
    side = block + 2 * HALO_ROWS // GROUP
    row_ok, col_ok = edge_masks(
        (side, LANES), HALO_ROWS // GROUP, rows, cols, gx * rows, gy * cols
    )

    odd = lax.axis_index("gx") & 1

    def load(field, tile):
        lanes = slice(tile * LANES, (tile + 1) * LANES)
        for halo, before in ((even_rows, odd), (odd_rows, 1 - odd)):
            span = pl.ds(pl.multiple_of(HALO_ROWS * before, HALO_ROWS), HALO_ROWS)
            tiles[field, tile, span, :] = halo[field, :, lanes]

    def write(field, m, k, plane):
        if field < 2:
            spans = (slice(0, block), slice(block, side))
            for span, value in zip(spans, (own[field, m, k], plane)):
                value = value * (0.25 * factor[m, k, span, :])
                matrix0[field, m, k, span, :] = value
                if field == 1:
                    matrix0[2, m, k, span, :] = matrix0[0, m, k, span, :] * (1.0 / 3.0) + value
        else:
            source0[field - 2, m, k, :block, :] = own[field, m, k]
            source0[field - 2, m, k, block:, :] = plane

    spread_fields(load, write, tiles, stacked, spread)

    level0 = FineLevel(matrix0, {}, inverse0)
    level1 = Level(matrix1, FIRST_AT, inverse1)
    level2 = Level(matrix2, FULL_AT, inverse2)

    coarsen_fine(level0, level1)

    def write2(at, m, k, value):
        matrix2[at, m, k] = value

    coarsen(level1, write2, level2.count)

    def write3(at, m, k, value):
        matrix3[at] = value

    coarsen(level2, write3, 1)
    for level in (level0, level1, level2):
        level.make_inverse(row_ok, col_ok)

    source3 = matrix3.at[pl.ds(len(FULL), 2)]
    chain = (
        (level0, source0, x0, other0, source1),
        (level1, source1, x1, other1, source2),
        (level2, source2, x2, other2, None),
    )
    for level, source, x, other, target in chain:
        start(level, other, source)
        apply(level, other, source, x, residual=False)
        apply(level, x, source, other, residual=True)
        if target is not None:
            restrict(other, target, level.count)
        else:
            restrict_last(other, source3)
    for at in range(len(FULL) + 2):
        coarsest[at] = matrix3[at, :block, :]


def restrict_last(residual, target):
    class Planes:
        def __setitem__(self, where, value):
            target[where[0]] = value

    restrict(residual, Planes(), 2)


def up_kernel(
    coarse, coarse_even, coarse_odd,
    matrix0, inverse0, source0, x0_in, matrix1, inverse1, source1, x1_in, matrix2, inverse2, source2, x2_in,
    displacement,
    x0, other0, x1, other1, x2, other2, matrix3, inverse3, source3, x3,
    stacked, gathered, tiles,
    *, rows, cols, gx, gy,
):
    block, odd = rows // GROUP, lax.axis_index("gx") & 1
    for at in range(len(FULL) + 2):
        for piece, part in ((0, coarse), (1 + odd, coarse_even), (2 - odd, coarse_odd)):
            lines = pl.ds(pl.multiple_of(piece * block, block), block)
            if at < len(FULL):
                matrix3[at, 0, 0, lines, :] = part[at]
            else:
                source3[at - len(FULL), 0, 0, lines, :] = part[at]
    level3 = Level(matrix3, FULL_AT, inverse3)
    level3.make_inverse(*edge_masks((3 * block, LANES), block, rows, cols, gx * rows, gy * cols))
    relax(level3, source3, x3)
    now = x3
    coarse_plane = functools.partial(cut_plane, now, block)

    level0 = FineLevel(matrix0, {}, inverse0)
    level1 = Level(matrix1, FIRST_AT, inverse1)
    level2 = Level(matrix2, FULL_AT, inverse2)
    for level, source, before, x, other in (
        (level2, source2, x2_in, x2, other2),
        (level1, source1, x1_in, x1, other1),
        (level0, source0, x0_in, x0, other0),
    ):
        last = level.count - 1
        prolong(coarse_plane, before, x, level.count, {0, 1, last - 1, last} if level is level0 else None)
        close_columns(level, x)
        if level is level0:
            apply(level, x, source, other, False, {0, last - 1, last}, {0, last})
            apply(level, other, source, x, False, {last}, set())
        else:
            apply(level, x, source, other, residual=False)
            apply(level, other, source, x, residual=False)
        coarse_plane = functools.partial(whole_plane, x)

    at = lax.broadcasted_iota(jnp.int32, (WIDE, WIDE), 1)
    line = lax.broadcasted_iota(jnp.int32, (WIDE, WIDE), 0)
    gathered[...] = jnp.where(line == (at & (GROUP - 1)) * SPAN + (at >> LEVELS), 1.0, 0.0).astype(BF16)
    lane = lax.broadcasted_iota(jnp.int32, (2 * block, LANES), 1)
    for component in (0, 1):
        for pair in range(GROUP // 2):
            values = [
                jnp.concatenate(
                    [x0[component, 2 * pair + h, k, :block, :] for h in (0, 1)], axis=0
                )
                for k in range(GROUP)
            ]
            for piece in range(cols // WIDE):
                for half in range(WIDE // LANES):
                    slots = LANES // SPAN
                    value = None
                    for slot in reversed(range(slots)):
                        part = turned(values[half * slots + slot], (slot - piece) * SPAN)
                        value = part if value is None else jnp.where(lane < (slot + 1) * SPAN, part, value)
                    lanes = slice(piece * WIDE + half * LANES, piece * WIDE + (half + 1) * LANES)
                    for part, split in enumerate(two_parts(value)):
                        line = part * 2 * rows + component * rows + pair * 2 * block
                        stacked[line : line + 2 * block, lanes] = split
    pieces = []
    for piece in range(cols // WIDE):
        product = jnp.dot(
            stacked[:, piece * WIDE : (piece + 1) * WIDE], gathered[...], preferred_element_type=F32
        )
        pieces.append(product[: 2 * rows] + product[2 * rows :])
    for component in (0, 1):
        for tile in range(cols // LANES):
            lanes = slice(tile * LANES, (tile + 1) * LANES)
            for m in range(GROUP):
                line = component * rows + m * block
                tiles[component, tile, pl.ds(m, block, stride=GROUP), :] = pieces[tile * LANES // WIDE][
                    line : line + block, tile * LANES % WIDE : tile * LANES % WIDE + LANES
                ]
            displacement[component, :, lanes] = tiles[component, tile]


def relax(level, source, out):
    right = [source[component, 0, 0] for component in (0, 1)]
    inverse = [inverse_of(level, component, 0, 0, out.shape[3]) for component in (0, 1)]
    x = [right[c] * inverse[c] for c in (0, 1)]
    for _ in range(COARSE_SWEEPS - 1):
        after = [from_after(value, 1) for value in x]
        sums = [x[c] + after[c] for c in (0, 1)]
        steps = [after[c] - x[c] for c in (0, 1)]
        sum1, step1 = [[from_after(value, 0) for value in pair] for pair in (sums, steps)]
        modes = (
            sum1[0] - sums[0],
            steps[1] + step1[1],
            (steps[0] + step1[0]) + (sum1[1] - sums[1]),
            step1[0] - steps[0],
            step1[1] - steps[1],
        )
        first, second, third, bend_row, bend_col = level.stress(0, 0, modes)
        own = (first, third - bend_row, third, second - bend_col)
        above = [from_before(v, 0) for v in (first, third + bend_row, third, second + bend_col)]
        for c in (0, 1):
            even, odd = above[2 * c] - own[2 * c], above[2 * c + 1] + own[2 * c + 1]
            rest = right[c] - ((even - odd) + from_before(even + odd, 1))
            x[c] = x[c] + inverse[c] * rest
    for component in (0, 1):
        out[component, 0, 0] = x[component]


def cut_plane(x, block, component, m, k):
    line = lax.broadcasted_iota(jnp.int32, (block, LANES), 0)
    halo = jnp.where(
        line < HALO_ROWS // GROUP,
        x[component, 0, 0, block : 2 * block, :],
        x[component, 0, 0, 2 * block :, :],
    )
    return jnp.concatenate([x[component, 0, 0, :block, :], halo], axis=0)


def whole_plane(x, component, m, k):
    return x[component, m, k]


def body(first_lame, shear_modulus, applied_load, plastic_owner, plastic_cell, plastic_code):
    rows, cols = first_lame.shape
    gx, gy = lax.axis_size("gx"), lax.axis_size("gy")
    devices = gx * gy

    fields, even_cols, odd_cols, words = pack(
        first_lame, shear_modulus, applied_load, plastic_owner, plastic_cell, plastic_code, devices
    )
    even_side, odd_side = swapped(even_cols, "gy", 0), swapped(odd_cols, "gy", 1)
    words = lax.all_to_all(words, ("gx", "gy"), 0, 0, tiled=True)

    even_rows, odd_rows = pack_rows(fields, even_side, odd_side)
    even_rows, odd_rows = swapped(even_rows, "gx", 0), swapped(odd_rows, "gx", 1)
    own = spread_own(fields, even_side, odd_side)
    words, own = lax.optimization_barrier((words, own))
    factor = yield_factor(words, rows, cols, gy)

    tall, wide = rows + 2 * HALO_ROWS, cols + 2 * HALO_COLS
    side = tall // GROUP
    vmem = pl.BlockSpec(memory_space=pltpu.VMEM)

    def planes(fields, count, extra=0, lines=side):
        return (fields, count, count + extra, lines, LANES)

    state = []
    for count, entries, inverses in ((GROUP, 3, 1), (GROUP // 2, len(FIRST), 2), (GROUP // 4, len(FULL), 2)):
        state += [planes(entries, count), planes(inverses, count), planes(2, count), planes(2, count, 1)]
    held = len(FULL) + 2
    counts = (GROUP, GROUP // 2, GROUP // 4)
    *state, coarse = pl.pallas_call(
        functools.partial(down_kernel, rows=rows, cols=cols, gx=gx, gy=gy),
        out_shape=[jax.ShapeDtypeStruct(shape, F32) for shape in state]
        + [jax.ShapeDtypeStruct((held, rows // GROUP, LANES), F32)],
        in_specs=[vmem] * 4,
        out_specs=[vmem] * (len(state) + 1),
        scratch_shapes=spread_scratch(2 * HALO_ROWS, wide)
        + [pltpu.VMEM(planes(2, count, 1), F32) for count in counts]
        + [pltpu.VMEM((held, side, LANES), F32)],
        compiler_params=pltpu.CompilerParams(vmem_limit_bytes=VMEM_LIMIT),
        name="descent",
    )(own, even_rows, odd_rows, factor)

    coarse_even, coarse_odd = swapped(coarse, "gx", 0), swapped(coarse, "gx", 1)
    lines = 3 * (rows // GROUP)
    return pl.pallas_call(
        functools.partial(up_kernel, rows=rows, cols=cols, gx=gx, gy=gy),
        out_shape=jax.ShapeDtypeStruct((2, rows, cols), F32),
        in_specs=[vmem] * (3 + len(state)),
        out_specs=vmem,
        scratch_shapes=[
            shape
            for count in counts
            for shape in (pltpu.VMEM(planes(2, count, 1), F32),) * 2
        ]
        + [
            pltpu.VMEM(planes(len(FULL), 1, 0, lines), F32),
            pltpu.VMEM(planes(2, 1, 0, lines), F32),
            pltpu.VMEM(planes(2, 1, 0, lines), F32),
            pltpu.VMEM(planes(2, 1, 0, lines), F32),
            pltpu.VMEM((4 * rows, cols), BF16),
            pltpu.VMEM((WIDE, WIDE), BF16),
            pltpu.VMEM((2, cols // LANES, rows, LANES), F32),
        ],
        compiler_params=pltpu.CompilerParams(vmem_limit_bytes=VMEM_LIMIT),
        name="ascent",
    )(coarse, coarse_even, coarse_odd, *state)


def solution(mesh):
    return jax.shard_map(
        body,
        mesh=mesh,
        in_specs=(
            P("gx", "gy"),
            P("gx", "gy"),
            P(None, "gx", "gy"),
            P(("gx", "gy"), None),
            P(("gx", "gy")),
            P(("gx", "gy")),
        ),
        out_specs=P(None, "gx", "gy"),
        check_vma=False,
    )
```

```python
import functools
import math

import jax
import jax.numpy as jnp
import numpy as np
from jax import lax
from jax.experimental import pallas as pl
from jax.experimental.pallas import tpu as pltpu
from jax.sharding import PartitionSpec as P

LEVELS = 3
SWEEPS = 2
COARSE_SWEEPS = 6
YIELD_DROP = 0.6
GROUP = 1 << LEVELS
HALO_ROWS = 32
HALO_COLS = 128
LANES = 128
WIDE = 2 * LANES
SPAN = WIDE // GROUP
LISTS_AT_ONCE = 16
VMEM_LIMIT = 30 * 1024 * 1024
F32 = jnp.float32
BF16 = jnp.bfloat16

FIRST = ("11", "12", "33", "1r", "2r", "3r", "1c", "2c", "3c", "rr", "rc")
FULL = FIRST + ("cc",)
FIRST_AT = {name: FIRST.index(name) for name in FIRST} | {"22": 0, "cc": FIRST.index("rr")}
FULL_AT = {name: FULL.index(name) for name in FULL} | {"22": 0}


def swapped(array, axis, odd_pairs):
    devices = lax.axis_size(axis)
    pairs = []
    for i in range(odd_pairs, devices - 1, 2):
        pairs += [(i, i + 1), (i + 1, i)]
    return lax.ppermute(array, axis, pairs)


def log2(number):
    power = number.bit_length() - 1
    assert 1 << power == number
    return power


def from_before(value, axis):
    return pltpu.roll(value, 1, axis)


def from_after(value, axis):
    return pltpu.roll(value, value.shape[axis] - 1, axis)


def plus(*terms):
    total = None
    for term in terms:
        if term is not None:
            total = term if total is None else total + term
    return total


def times(weight, term):
    return None if term is None else weight * term


def factor_kernel(words, factor, tall_of, lane_of, codes, counts, *, rows, cols, gy):
    for at in range(words.shape[0]):
        tall_of[at : at + 1, :] = words[at]
    word = tall_of[...]
    cell_bits = log2(rows * cols)
    owner = word >> (cell_bits + 2)
    cell = (word >> 2) & (rows * cols - 1)
    row = (owner >> log2(gy)) * rows + (cell >> log2(cols)) - lax.axis_index("gx") * rows
    col = (owner & (gy - 1)) * cols + (cell & (cols - 1)) - lax.axis_index("gy") * cols
    tall = rows + 2 * HALO_ROWS
    side = tall // GROUP
    inside = (row >= -HALO_ROWS) & (row < rows + HALO_ROWS) & (col >= -HALO_COLS) & (col < cols + HALO_COLS)
    at = jnp.where(col < 0, col + cols + HALO_COLS, jnp.where(col >= cols, col + HALO_COLS, col))
    line = (row & (GROUP - 1)) * side + ((row >> LEVELS) & (side - 1))
    tall_of[...] = jnp.where(inside, line + tall * (at >> log2(WIDE)), -1)
    lane_of[...] = (at & (GROUP - 1)) * SPAN + ((at & (WIDE - 1)) >> LEVELS)
    codes[...] = (word & 3).astype(F32)
    counts[...] = jnp.zeros_like(counts)
    length = words.shape[2]
    group = min(LISTS_AT_ONCE, words.shape[0])

    @pl.loop(0, words.shape[0] // group)
    def _(i):
        tall_id = lax.broadcasted_iota(jnp.int32, (counts.shape[0], length), 0)
        lane_id = lax.broadcasted_iota(jnp.int32, (WIDE, length), 0)
        by_tall, by_lane = [], []
        for j in range(group):
            line = pl.ds(i * group + j, 1)
            by_tall.append(jnp.where(tall_id == tall_of[line, :], codes[line, :], 0.0).astype(BF16))
            by_lane.append(jnp.where(lane_id == lane_of[line, :], 1.0, 0.0).astype(BF16))
        counts[...] += lax.dot_general(
            jnp.concatenate(by_tall, axis=1),
            jnp.concatenate(by_lane, axis=1),
            (((1,), (1,)), ((), ())),
            preferred_element_type=F32,
        )

    for m in range(GROUP):
        for k in range(GROUP):
            half, slot = k * SPAN // LANES, k * SPAN % LANES
            lanes = slice(half * LANES, (half + 1) * LANES)
            lines = range(m * side, counts.shape[0], tall)
            count = gather_lanes([counts[line : line + side, lanes] for line in lines], slot)
            factor[m, k] = jnp.exp(count * math.log(YIELD_DROP))


def yield_factor(words, rows, cols, gy):
    tall, wide = rows + 2 * HALO_ROWS, cols + 2 * HALO_COLS
    lists = (words.shape[0], words.shape[2])
    return pl.pallas_call(
        functools.partial(factor_kernel, rows=rows, cols=cols, gy=gy),
        out_shape=jax.ShapeDtypeStruct((GROUP, GROUP, tall // GROUP, LANES), F32),
        in_specs=[pl.BlockSpec(memory_space=pltpu.VMEM)],
        out_specs=pl.BlockSpec(memory_space=pltpu.VMEM),
        scratch_shapes=[
            pltpu.VMEM(lists, jnp.int32),
            pltpu.VMEM(lists, jnp.int32),
            pltpu.VMEM(lists, F32),
            pltpu.VMEM((tall * wide // WIDE, WIDE), F32),
        ],
        compiler_params=pltpu.CompilerParams(vmem_limit_bytes=VMEM_LIMIT),
        cost_estimate=pl.CostEstimate(
            flops=2 * tall * wide * words.size, bytes_accessed=4 * words.size, transcendentals=tall * wide
        ),
        name="yield_factor",
    )(words)


def pack_kernel(
    first_lame, shear_modulus, applied_load, owner, cell, code,
    fields, even_cols, odd_cols, words, lists, copied, arrived,
    *, cells,
):
    copies = [
        pltpu.make_async_copy(source, target, arrived.at[at])
        for at, (source, target) in enumerate(
            (
                (owner, lists.at[0]),
                (cell, lists.at[1]),
                (code, lists.at[2]),
                (first_lame, fields.at[0]),
                (shear_modulus, fields.at[1]),
                (applied_load, fields.at[pl.ds(2, 2)]),
            )
        )
    ]
    for copy in copies:
        copy.start()
    for copy in copies[:3]:
        copy.wait()
    word = (lists[0] * cells + lists[1]) * 4 + lists[2]
    for device in range(words.shape[0]):
        copied[device] = word
    sent = pltpu.make_async_copy(copied, words, arrived.at[6])
    sent.start()
    for copy in copies[3:]:
        copy.wait()
    last, odd = fields.shape[2] - HALO_COLS, lax.axis_index("gy") & 1
    even_cols[...] = fields[:, :, pl.ds(pl.multiple_of(last * (1 - odd), HALO_COLS), HALO_COLS)]
    odd_cols[...] = fields[:, :, pl.ds(pl.multiple_of(last * odd, HALO_COLS), HALO_COLS)]
    sent.wait()


def pack(first_lame, shear_modulus, applied_load, owner, cell, code, devices):
    rows, cols = first_lame.shape
    edge = jax.ShapeDtypeStruct((4, rows, HALO_COLS), F32)
    length = cell.shape[0]
    arrays = [first_lame, shear_modulus, applied_load] + [part.reshape(1, -1) for part in (owner, cell, code)]
    hbm, vmem = pl.BlockSpec(memory_space=pltpu.HBM), pl.BlockSpec(memory_space=pltpu.VMEM)
    return pl.pallas_call(
        functools.partial(pack_kernel, cells=rows * cols),
        out_shape=[
            jax.ShapeDtypeStruct((4, rows, cols), F32),
            edge,
            edge,
            jax.ShapeDtypeStruct((devices, 1, length), jnp.int32),
        ],
        in_specs=[hbm] * 6,
        out_specs=[vmem] * 3 + [hbm],
        scratch_shapes=[
            pltpu.VMEM((3, 1, length), jnp.int32),
            pltpu.VMEM((devices, 1, length), jnp.int32),
            pltpu.SemaphoreType.DMA((7,)),
        ],
        compiler_params=pltpu.CompilerParams(vmem_limit_bytes=8 * 1024 * 1024),
        name="pack",
    )(*[pltpu.with_memory_space_constraint(array, pltpu.HBM) for array in arrays])


def rows_kernel(fields, even_side, odd_side, even_rows, odd_rows):
    rows, cols = fields.shape[1:]
    last, odd, odd_col = rows - HALO_ROWS, lax.axis_index("gx") & 1, lax.axis_index("gy") & 1
    for out, side in ((even_rows, 1 - odd), (odd_rows, odd)):
        span = pl.ds(pl.multiple_of(last * side, HALO_ROWS), HALO_ROWS)
        out[:, :, :cols] = fields[:, span, :]
        for halo, after in ((even_side, 1 - odd_col), (odd_side, odd_col)):
            at = pl.multiple_of(cols + HALO_COLS * after, HALO_COLS)
            out[:, :, pl.ds(at, HALO_COLS)] = halo[:, span, :]


def pack_rows(fields, even_side, odd_side):
    edge = jax.ShapeDtypeStruct((4, HALO_ROWS, fields.shape[2] + 2 * HALO_COLS), F32)
    vmem = pl.BlockSpec(memory_space=pltpu.VMEM)
    return pl.pallas_call(
        rows_kernel,
        out_shape=[edge, edge],
        in_specs=[vmem] * 3,
        out_specs=[vmem] * 2,
        compiler_params=pltpu.CompilerParams(vmem_limit_bytes=8 * 1024 * 1024),
        name="pack_rows",
    )(fields, even_side, odd_side)


class Level:
    def __init__(self, matrix, names_at, inverse):
        self.matrix, self.names_at, self.inverse = matrix, names_at, inverse
        self.count = matrix.shape[1]

    def entry(self, name, m, k, high):
        at = self.names_at.get(name)
        return None if at is None else self.matrix[at, m, k, :high, :]

    def stress(self, m, k, modes):
        names = "123rc"
        known = {}
        result = []
        for i in range(5):
            terms = []
            for j in range(5):
                name = names[min(i, j)] + names[max(i, j)]
                if name not in known:
                    known[name] = self.entry(name, m, k, modes[0].shape[0])
                if known[name] is not None:
                    terms.append(known[name] * modes[j])
            result.append(plus(*terms))
        return result

    def halves(self, component, m, k):
        if component == 0:
            names = ("11", "33", "rr", "13", "1r", "3r")
        else:
            names = ("22", "33", "cc", "23", "3c", "2c")
        first, second, third, cross, by_col, by_row = [self.entry(name, m, k, self.matrix.shape[3]) for name in names]
        base = first + second + third
        by_row, by_col, cross = 2.0 * by_row, 2.0 * by_col, times(2.0, cross)
        if cross is None:
            return base - by_row, base + by_row, by_col, by_col
        return base - by_row, base + by_row, by_col - cross, by_col + cross

    def components(self):
        return (0, 1)

    def make_inverse(self, row_ok, col_ok):
        count = self.count
        for component in self.components():
            kept = {}
            for k in range(count):
                parts = [self.halves(component, m, k) for m in range(count)]
                for m in range(count):
                    above = parts[m - 1] if m else parts[count - 1]
                    lower = [above[1], above[3]]
                    if m == 0:
                        lower = [from_before(value, 0) for value in lower]
                    even, odd = parts[m][0] + lower[0], parts[m][2] + lower[1]
                    kept[m, k] = (even - odd, even + odd)
            for k in range(count):
                for m in range(count):
                    left = kept[m, k - 1][1] if k else from_before(kept[m, count - 1][1], 1)
                    diagonal = kept[m, k][0] + left
                    value = jnp.where(diagonal > 0.0, 0.5 / diagonal, 0.0)
                    if m == 0:
                        value = value * row_ok
                    if k == 0:
                        value = value * col_ok
                    self.inverse[component, m, k] = value


class FineLevel(Level):
    def stress(self, m, k, modes):
        lame, shear, mixed = [self.matrix[at, m, k, : modes[0].shape[0], :] for at in range(3)]
        first, second, third, bend_row, bend_col = modes
        twice, mean = shear + shear, lame * (first + second)
        return [
            mean + twice * first,
            mean + twice * second,
            shear * third,
            mixed * bend_row,
            mixed * bend_col,
        ]

    def components(self):
        return (0,)

    def make_inverse(self, row_ok, col_ok, source, x):
        count = self.count

        def pair_sums(k):
            parts = [self.matrix[2, m, k] for m in range(count)]
            return [parts[m] + (parts[m - 1] if m else from_before(parts[count - 1], 0)) for m in range(count)]

        left = [from_before(value, 1) for value in pair_sums(count - 1)]
        for k in range(count):
            here = pair_sums(k)
            for m in range(count):
                diagonal = 4.0 * (here[m] + left[m])
                value = jnp.where(diagonal > 0.0, 0.5 / diagonal, 0.0)
                if m == 0:
                    value = value * row_ok
                if k == 0:
                    value = value * col_ok
                self.inverse[0, m, k] = value
                for component in (0, 1):
                    x[component, m, k] = source[component, m, k] * value
            left = here
        close_columns(self, x)


def inverse_of(level, component, m, k, high):
    return level.inverse[min(component, len(level.components()) - 1), m, k, :high, :]


def close_columns(level, x):
    count = level.count
    for component in (0, 1):
        for m in range(count):
            x[component, m, count] = from_after(x[component, m, 0], 1)


def start(level, x, source):
    count = level.count

    def column(k):
        for component in (0, 1):
            for m in range(count):
                x[component, m, k] = source[component, m, k] * inverse_of(level, component, m, k, x.shape[3])

    over_columns(count, column)
    close_columns(level, x)


def over_columns(count, column):
    for k in range(count):
        column(k)


def cut(value, height):
    return value if value.shape[0] == height else value[:height]


def apply(level, x, source, out, residual, tall_cells=None, tall_nodes=None):
    count = level.count
    side = x.shape[3]
    cells = [side if tall_cells is None or m in tall_cells else side // 2 for m in range(count)]
    nodes = [side if tall_nodes is None or m in tall_nodes else side // 2 for m in range(count)]
    held = [max(cells[m], cells[m - 1]) if m else side for m in range(count)]
    passed_right = {}

    def column(k):
        sums, steps = [], []
        for m in range(count):
            here = [x[component, m, k, : held[m], :] for component in (0, 1)]
            after = [x[component, m, k + 1, : held[m], :] for component in (0, 1)]
            sums.append([here[c] + after[c] for c in (0, 1)])
            steps.append([after[c] - here[c] for c in (0, 1)])
        sums.append([from_after(value, 0) for value in sums[0]])
        steps.append([from_after(value, 0) for value in steps[0]])
        own, passed = [], []
        for m in range(count):
            sum0, sum1 = [[cut(value, cells[m]) for value in sums[row]] for row in (m, m + 1)]
            step0, step1 = [[cut(value, cells[m]) for value in steps[row]] for row in (m, m + 1)]
            modes = (
                sum1[0] - sum0[0],
                step0[1] + step1[1],
                (step0[0] + step1[0]) + (sum1[1] - sum0[1]),
                step1[0] - step0[0],
                step1[1] - step0[1],
            )
            first, second, third, bend_row, bend_col = level.stress(m, k, modes)
            own.append((first, third - bend_row, third, second - bend_col))
            passed.append((first, third + bend_row, third, second + bend_col))
        for m in range(count):
            high = nodes[m]
            above = passed[m - 1] if m else [from_before(value, 0) for value in passed[count - 1]]
            for component in (0, 1):
                at = 2 * component
                even = cut(above[at], high) - cut(own[m][at], high)
                odd = cut(above[at + 1], high) + cut(own[m][at + 1], high)
                force = even - odd
                if k:
                    force = force + passed_right[component, m]
                passed_right[component, m] = even + odd
                rest = source[component, m, k, :high, :] - force
                if not residual:
                    rest = x[component, m, k, :high, :] + inverse_of(level, component, m, k, high) * rest
                out[component, m, k, :high, :] = rest

    over_columns(count, column)
    for component in (0, 1):
        for m in range(count):
            high = nodes[m]
            left = from_before(passed_right[component, m], 1)
            if not residual:
                left = left * inverse_of(level, component, m, 0, high)
            out[component, m, 0, :high, :] = out[component, m, 0, :high, :] - left
            if not residual:
                out[component, m, count, :high, :] = from_after(out[component, m, 0, :high, :], 1)


def restrict(residual, target, count):
    half = count // 2
    for component in (0, 1):
        for k in range(half):
            lines = []
            for m in range(count):
                odd = residual[component, m, 2 * k + 1]
                if k:
                    before = residual[component, m, 2 * k - 1]
                else:
                    before = from_before(residual[component, m, count - 1], 1)
                lines.append(residual[component, m, 2 * k] + 0.5 * (odd + before))
            for m in range(half):
                before = lines[2 * m - 1] if m else from_before(lines[count - 1], 0)
                target[component, m, k] = lines[2 * m] + 0.5 * (lines[2 * m + 1] + before)


def prolong(coarse, before, x, count, tall=None):
    side = x.shape[3]

    def add(component, m, k, value):
        high = side if tall is None or m in tall else side // 2
        x[component, m, k, :high, :] = before[component, m, k, :high, :] + cut(value, high)

    half = count // 2
    for component in (0, 1):
        planes = {(m, k): coarse(component, m, k) for m in range(half) for k in range(half)}
        for m in range(half):
            planes[m, half] = from_after(planes[m, 0], 1)
        for k in range(half + 1):
            planes[half, k] = from_after(planes[0, k], 0)
        for m in range(half):
            for k in range(half):
                a, b, c, d = planes[m, k], planes[m + 1, k], planes[m, k + 1], planes[m + 1, k + 1]
                add(component, 2 * m, 2 * k, a)
                add(component, 2 * m + 1, 2 * k, 0.5 * (a + b))
                add(component, 2 * m, 2 * k + 1, 0.5 * (a + c))
                add(component, 2 * m + 1, 2 * k + 1, 0.25 * ((a + b) + (c + d)))


def haar(level, names_at, m, k):
    def signed(name, row, col):
        if name not in names_at:
            return None
        value = {
            (a, b): level.matrix[names_at[name], 2 * m + a, 2 * k + b] for a in (0, 1) for b in (0, 1)
        }
        low = value[0, 1] - value[0, 0] if col else value[0, 1] + value[0, 0]
        high = value[1, 1] - value[1, 0] if col else value[1, 1] + value[1, 0]
        return high - low if row else high + low

    return signed


def coarsen_fine(fine, coarse):
    count = coarse.count

    def column(k):
        for m in range(count):
            signed = haar(fine, {"l": 0, "s": 1}, m, k)
            lame, shear = signed("l", 0, 0), signed("s", 0, 0)
            lame_row, shear_row = signed("l", 1, 0), signed("s", 1, 0)
            lame_col, shear_col = signed("l", 0, 1), signed("s", 0, 1)
            lame_both, shear_both = signed("l", 1, 1), signed("s", 1, 1)
            values = {
                "11": 0.25 * (lame + 2.0 * shear),
                "12": 0.25 * lame,
                "33": 0.25 * shear,
                "1r": 0.125 * (lame_col + 2.0 * shear_col),
                "2r": 0.125 * lame_col,
                "3r": 0.125 * shear_row,
                "1c": 0.125 * lame_row,
                "2c": 0.125 * (lame_row + 2.0 * shear_row),
                "3c": 0.125 * shear_col,
                "rr": (lame + 3.0 * shear) * (1.0 / 12.0),
                "rc": 0.0625 * (lame_both + shear_both),
            }
            for name, value in values.items():
                coarse.matrix[FIRST_AT[name], m, k] = value

    over_columns(count, column)


def coarsen(fine, write, count):
    for k in range(count):
        for m in range(count):
            signed = haar(fine, fine.names_at, m, k)

            def total(name):
                return signed(name, 0, 0)

            def by_row(name):
                return signed(name, 1, 0)

            def by_col(name):
                return signed(name, 0, 1)

            def by_both(name):
                return signed(name, 1, 1)

            values = {}
            for name in ("11", "12", "33"):
                values[name] = times(0.25, total(name))
            for i in "123":
                one, two, three = ["".join(sorted(i + j)) for j in "123"]
                values[i + "r"] = 0.125 * plus(by_col(one), by_row(three), total(i + "r"))
                values[i + "c"] = 0.125 * plus(by_row(two), by_col(three), total(i + "c"))
            values["rr"] = 0.0625 * plus(
                total("11"),
                total("33"),
                times(2.0, by_both("13")),
                2.0 * (by_col("1r") + by_row("3r")),
                total("rr"),
            )
            values["cc"] = 0.0625 * plus(
                total("22"),
                total("33"),
                times(2.0, by_both("23")),
                2.0 * (by_row("2c") + by_col("3c")),
                total("cc"),
            )
            values["rc"] = 0.0625 * plus(
                by_both("12"),
                total("13"),
                total("23"),
                by_both("33"),
                by_col("1c"),
                by_row("3c"),
                by_row("2r"),
                by_col("3r"),
                total("rc"),
            )
            for name in FULL:
                write(FULL_AT[name], m, k, values[name])


def edge_masks(shape, before, rows, cols, grid_rows, grid_cols):
    def wrapped(axis, ahead):
        at = lax.broadcasted_iota(jnp.int32, shape, axis)
        return jnp.where(at < shape[axis] - ahead, at, at - shape[axis]) * GROUP

    row = wrapped(0, before) + lax.axis_index("gx") * rows
    col = wrapped(1, HALO_COLS // GROUP) + lax.axis_index("gy") * cols
    return (
        jnp.where(row < grid_rows, 1.0, 0.0).astype(F32),
        jnp.where(col < grid_cols, 1.0, 0.0).astype(F32),
    )


def two_parts(value):
    high = value.astype(BF16)
    return high, (value - high.astype(F32)).astype(BF16)


def turned(value, by):
    return pltpu.roll(value, by % LANES, 1) if by % LANES else value


def gather_lanes(pieces, slot):
    lane = lax.broadcasted_iota(jnp.int32, pieces[0].shape, 1)
    halo = HALO_COLS // GROUP
    own = (len(pieces) - 1) * SPAN
    plane = jnp.where(lane >= LANES - halo, turned(pieces[-1], LANES - halo - slot), 0.0)
    plane = jnp.where(lane < own + halo, turned(pieces[-1], own - halo - slot), plane)
    for at in reversed(range(len(pieces) - 1)):
        plane = jnp.where(lane < (at + 1) * SPAN, turned(pieces[at], at * SPAN - slot), plane)
    return plane


def make_spread(spread):
    at = lax.broadcasted_iota(jnp.int32, (WIDE, WIDE), 0)
    lane = lax.broadcasted_iota(jnp.int32, (WIDE, WIDE), 1)
    spread[...] = jnp.where(lane == (at & (GROUP - 1)) * SPAN + (at >> LEVELS), 1.0, 0.0).astype(BF16)


def spread_fields(load, write, tiles, stacked, spread):
    fields, count, rows = tiles.shape[:3]
    block = rows // GROUP
    make_spread(spread)
    for field in range(fields):
        for tile in range(count):
            load(field, tile)
        for pair in range(GROUP // 2):
            for tile in range(count):
                lines = [tiles[field, tile, pl.ds(2 * pair + h, block, stride=GROUP), :] for h in (0, 1)]
                for part, split in enumerate(two_parts(jnp.concatenate(lines, axis=0))):
                    line = (field * 2 + part) * rows + pair * 2 * block
                    stacked[line : line + 2 * block, tile * LANES : (tile + 1) * LANES] = split
    for field in range(fields):
        pieces = []
        for piece in range(count * LANES // WIDE):
            left = stacked[field * 2 * rows : (field + 1) * 2 * rows, piece * WIDE : (piece + 1) * WIDE]
            product = jnp.dot(left, spread[...], preferred_element_type=F32)
            pieces.append(product[:rows] + product[rows:])
        for m in range(GROUP):
            for k in range(GROUP):
                half, slot = k * SPAN // LANES, k * SPAN % LANES
                lanes = slice(half * LANES, (half + 1) * LANES)
                lines = slice(m * block, (m + 1) * block)
                write(field, m, k, gather_lanes([piece[lines, lanes] for piece in pieces], slot))


def own_kernel(fields, even_side, odd_side, planes, tiles, stacked, spread):
    own_tiles, odd = fields.shape[2] // LANES, lax.axis_index("gy") & 1

    def load(field, tile):
        if tile < own_tiles:
            tiles[field, tile] = fields[field, :, tile * LANES : (tile + 1) * LANES]
        elif tile == own_tiles:
            tiles[field, tile + 1 - odd] = even_side[field]
        else:
            tiles[field, own_tiles + odd] = odd_side[field]

    def write(field, m, k, plane):
        planes[field, m, k] = plane

    spread_fields(load, write, tiles, stacked, spread)


def spread_scratch(rows, wide):
    return [
        pltpu.VMEM((4, wide // LANES, rows, LANES), F32),
        pltpu.VMEM((8 * rows, wide), BF16),
        pltpu.VMEM((WIDE, WIDE), BF16),
    ]


def spread_own(fields, even_side, odd_side):
    rows, wide = fields.shape[1], fields.shape[2] + 2 * HALO_COLS
    vmem = pl.BlockSpec(memory_space=pltpu.VMEM)
    return pl.pallas_call(
        own_kernel,
        out_shape=jax.ShapeDtypeStruct((4, GROUP, GROUP, rows // GROUP, LANES), F32),
        in_specs=[vmem] * 3,
        out_specs=vmem,
        scratch_shapes=spread_scratch(rows, wide),
        compiler_params=pltpu.CompilerParams(vmem_limit_bytes=12 * 1024 * 1024),
        cost_estimate=pl.CostEstimate(flops=16 * rows * wide * WIDE, bytes_accessed=0, transcendentals=0),
        name="spread_own",
    )(fields, even_side, odd_side)


def down_kernel(
    own, even_rows, odd_rows, factor,
    matrix0, inverse0, source0, x0, matrix1, inverse1, source1, x1, matrix2, inverse2, source2, x2, coarsest,
    tiles, stacked, spread, other0, other1, other2, matrix3,
    *, rows, cols, gx, gy,
):
    block = rows // GROUP
    side = block + 2 * HALO_ROWS // GROUP
    row_ok, col_ok = edge_masks(
        (side, LANES), HALO_ROWS // GROUP, rows, cols, gx * rows, gy * cols
    )

    odd = lax.axis_index("gx") & 1

    def load(field, tile):
        lanes = slice(tile * LANES, (tile + 1) * LANES)
        for halo, before in ((even_rows, odd), (odd_rows, 1 - odd)):
            span = pl.ds(pl.multiple_of(HALO_ROWS * before, HALO_ROWS), HALO_ROWS)
            tiles[field, tile, span, :] = halo[field, :, lanes]

    def write(field, m, k, plane):
        if field < 2:
            spans = (slice(0, block), slice(block, side))
            for span, value in zip(spans, (own[field, m, k], plane)):
                value = value * (0.25 * factor[m, k, span, :])
                matrix0[field, m, k, span, :] = value
                if field == 1:
                    matrix0[2, m, k, span, :] = matrix0[0, m, k, span, :] * (1.0 / 3.0) + value
        else:
            source0[field - 2, m, k, :block, :] = own[field, m, k]
            source0[field - 2, m, k, block:, :] = plane

    spread_fields(load, write, tiles, stacked, spread)

    level0 = FineLevel(matrix0, {}, inverse0)
    level1 = Level(matrix1, FIRST_AT, inverse1)
    level2 = Level(matrix2, FULL_AT, inverse2)

    coarsen_fine(level0, level1)

    def write2(at, m, k, value):
        matrix2[at, m, k] = value

    coarsen(level1, write2, level2.count)

    def write3(at, m, k, value):
        matrix3[at] = value

    coarsen(level2, write3, 1)
    level0.make_inverse(row_ok, col_ok, source0, other0)
    for level in (level1, level2):
        level.make_inverse(row_ok, col_ok)

    source3 = matrix3.at[pl.ds(len(FULL), 2)]
    chain = (
        (level0, source0, x0, other0, source1),
        (level1, source1, x1, other1, source2),
        (level2, source2, x2, other2, None),
    )
    for level, source, x, other, target in chain:
        if level is not level0:
            start(level, other, source)
        apply(level, other, source, x, residual=False)
        apply(level, x, source, other, residual=True)
        if target is not None:
            restrict(other, target, level.count)
        else:
            restrict_last(other, source3)
    for at in range(len(FULL) + 2):
        coarsest[at] = matrix3[at, :block, :]


def restrict_last(residual, target):
    class Planes:
        def __setitem__(self, where, value):
            target[where[0]] = value

    restrict(residual, Planes(), 2)


def up_kernel(
    coarse, coarse_even, coarse_odd,
    matrix0, inverse0, source0, x0_in, matrix1, inverse1, source1, x1_in, matrix2, inverse2, source2, x2_in,
    displacement,
    x0, other0, x1, other1, x2, other2, matrix3, inverse3, source3, x3,
    stacked, gathered, tiles,
    *, rows, cols, gx, gy,
):
    block, odd = rows // GROUP, lax.axis_index("gx") & 1
    for at in range(len(FULL) + 2):
        for piece, part in ((0, coarse), (1 + odd, coarse_even), (2 - odd, coarse_odd)):
            lines = pl.ds(pl.multiple_of(piece * block, block), block)
            if at < len(FULL):
                matrix3[at, 0, 0, lines, :] = part[at]
            else:
                source3[at - len(FULL), 0, 0, lines, :] = part[at]
    level3 = Level(matrix3, FULL_AT, inverse3)
    level3.make_inverse(*edge_masks((3 * block, LANES), block, rows, cols, gx * rows, gy * cols))
    relax(level3, source3, x3)
    now = x3
    coarse_plane = functools.partial(cut_plane, now, block)

    level0 = FineLevel(matrix0, {}, inverse0)
    level1 = Level(matrix1, FIRST_AT, inverse1)
    level2 = Level(matrix2, FULL_AT, inverse2)
    for level, source, before, x, other in (
        (level2, source2, x2_in, x2, other2),
        (level1, source1, x1_in, x1, other1),
        (level0, source0, x0_in, x0, other0),
    ):
        last = level.count - 1
        prolong(coarse_plane, before, x, level.count, {0, 1, last - 1, last} if level is level0 else None)
        close_columns(level, x)
        if level is level0:
            apply(level, x, source, other, False, {0, last - 1, last}, {0, last})
            apply(level, other, source, x, False, {last}, set())
        else:
            apply(level, x, source, other, residual=False)
            apply(level, other, source, x, residual=False)
        coarse_plane = functools.partial(whole_plane, x)

    at = lax.broadcasted_iota(jnp.int32, (WIDE, WIDE), 1)
    line = lax.broadcasted_iota(jnp.int32, (WIDE, WIDE), 0)
    gathered[...] = jnp.where(line == (at & (GROUP - 1)) * SPAN + (at >> LEVELS), 1.0, 0.0).astype(BF16)
    lane = lax.broadcasted_iota(jnp.int32, (2 * block, LANES), 1)
    for component in (0, 1):
        for pair in range(GROUP // 2):
            values = [
                jnp.concatenate(
                    [x0[component, 2 * pair + h, k, :block, :] for h in (0, 1)], axis=0
                )
                for k in range(GROUP)
            ]
            for piece in range(cols // WIDE):
                for half in range(WIDE // LANES):
                    slots = LANES // SPAN
                    value = None
                    for slot in reversed(range(slots)):
                        part = turned(values[half * slots + slot], (slot - piece) * SPAN)
                        value = part if value is None else jnp.where(lane < (slot + 1) * SPAN, part, value)
                    lanes = slice(piece * WIDE + half * LANES, piece * WIDE + (half + 1) * LANES)
                    for part, split in enumerate(two_parts(value)):
                        line = part * 2 * rows + component * rows + pair * 2 * block
                        stacked[line : line + 2 * block, lanes] = split
    pieces = []
    for piece in range(cols // WIDE):
        product = jnp.dot(
            stacked[:, piece * WIDE : (piece + 1) * WIDE], gathered[...], preferred_element_type=F32
        )
        pieces.append(product[: 2 * rows] + product[2 * rows :])
    for component in (0, 1):
        for tile in range(cols // LANES):
            lanes = slice(tile * LANES, (tile + 1) * LANES)
            for m in range(GROUP):
                line = component * rows + m * block
                tiles[component, tile, pl.ds(m, block, stride=GROUP), :] = pieces[tile * LANES // WIDE][
                    line : line + block, tile * LANES % WIDE : tile * LANES % WIDE + LANES
                ]
            displacement[component, :, lanes] = tiles[component, tile]


def relax(level, source, out):
    right = [source[component, 0, 0] for component in (0, 1)]
    inverse = [inverse_of(level, component, 0, 0, out.shape[3]) for component in (0, 1)]
    x = [right[c] * inverse[c] for c in (0, 1)]
    for _ in range(COARSE_SWEEPS - 1):
        after = [from_after(value, 1) for value in x]
        sums = [x[c] + after[c] for c in (0, 1)]
        steps = [after[c] - x[c] for c in (0, 1)]
        sum1, step1 = [[from_after(value, 0) for value in pair] for pair in (sums, steps)]
        modes = (
            sum1[0] - sums[0],
            steps[1] + step1[1],
            (steps[0] + step1[0]) + (sum1[1] - sums[1]),
            step1[0] - steps[0],
            step1[1] - steps[1],
        )
        first, second, third, bend_row, bend_col = level.stress(0, 0, modes)
        own = (first, third - bend_row, third, second - bend_col)
        above = [from_before(v, 0) for v in (first, third + bend_row, third, second + bend_col)]
        for c in (0, 1):
            even, odd = above[2 * c] - own[2 * c], above[2 * c + 1] + own[2 * c + 1]
            rest = right[c] - ((even - odd) + from_before(even + odd, 1))
            x[c] = x[c] + inverse[c] * rest
    for component in (0, 1):
        out[component, 0, 0] = x[component]


def cut_plane(x, block, component, m, k):
    line = lax.broadcasted_iota(jnp.int32, (block, LANES), 0)
    halo = jnp.where(
        line < HALO_ROWS // GROUP,
        x[component, 0, 0, block : 2 * block, :],
        x[component, 0, 0, 2 * block :, :],
    )
    return jnp.concatenate([x[component, 0, 0, :block, :], halo], axis=0)


def whole_plane(x, component, m, k):
    return x[component, m, k]


def body(first_lame, shear_modulus, applied_load, plastic_owner, plastic_cell, plastic_code):
    rows, cols = first_lame.shape
    gx, gy = lax.axis_size("gx"), lax.axis_size("gy")
    devices = gx * gy

    fields, even_cols, odd_cols, words = pack(
        first_lame, shear_modulus, applied_load, plastic_owner, plastic_cell, plastic_code, devices
    )
    even_side, odd_side = swapped(even_cols, "gy", 0), swapped(odd_cols, "gy", 1)
    words = lax.all_to_all(words, ("gx", "gy"), 0, 0, tiled=True)

    even_rows, odd_rows = pack_rows(fields, even_side, odd_side)
    even_rows, odd_rows = swapped(even_rows, "gx", 0), swapped(odd_rows, "gx", 1)
    own = spread_own(fields, even_side, odd_side)
    words, own = lax.optimization_barrier((words, own))
    factor = yield_factor(words, rows, cols, gy)

    tall, wide = rows + 2 * HALO_ROWS, cols + 2 * HALO_COLS
    side = tall // GROUP
    vmem = pl.BlockSpec(memory_space=pltpu.VMEM)

    def planes(fields, count, extra=0, lines=side):
        return (fields, count, count + extra, lines, LANES)

    state = []
    for count, entries, inverses in ((GROUP, 3, 1), (GROUP // 2, len(FIRST), 2), (GROUP // 4, len(FULL), 2)):
        state += [planes(entries, count), planes(inverses, count), planes(2, count), planes(2, count, 1)]
    held = len(FULL) + 2
    counts = (GROUP, GROUP // 2, GROUP // 4)
    *state, coarse = pl.pallas_call(
        functools.partial(down_kernel, rows=rows, cols=cols, gx=gx, gy=gy),
        out_shape=[jax.ShapeDtypeStruct(shape, F32) for shape in state]
        + [jax.ShapeDtypeStruct((held, rows // GROUP, LANES), F32)],
        in_specs=[vmem] * 4,
        out_specs=[vmem] * (len(state) + 1),
        scratch_shapes=spread_scratch(2 * HALO_ROWS, wide)
        + [pltpu.VMEM(planes(2, count, 1), F32) for count in counts]
        + [pltpu.VMEM((held, side, LANES), F32)],
        compiler_params=pltpu.CompilerParams(vmem_limit_bytes=VMEM_LIMIT),
        name="descent",
    )(own, even_rows, odd_rows, factor)

    coarse_even, coarse_odd = swapped(coarse, "gx", 0), swapped(coarse, "gx", 1)
    lines = 3 * (rows // GROUP)
    return pl.pallas_call(
        functools.partial(up_kernel, rows=rows, cols=cols, gx=gx, gy=gy),
        out_shape=jax.ShapeDtypeStruct((2, rows, cols), F32),
        in_specs=[vmem] * (3 + len(state)),
        out_specs=vmem,
        scratch_shapes=[
            shape
            for count in counts
            for shape in (pltpu.VMEM(planes(2, count, 1), F32),) * 2
        ]
        + [
            pltpu.VMEM(planes(len(FULL), 1, 0, lines), F32),
            pltpu.VMEM(planes(2, 1, 0, lines), F32),
            pltpu.VMEM(planes(2, 1, 0, lines), F32),
            pltpu.VMEM(planes(2, 1, 0, lines), F32),
            pltpu.VMEM((4 * rows, cols), BF16),
            pltpu.VMEM((WIDE, WIDE), BF16),
            pltpu.VMEM((2, cols // LANES, rows, LANES), F32),
        ],
        compiler_params=pltpu.CompilerParams(vmem_limit_bytes=VMEM_LIMIT),
        name="ascent",
    )(coarse, coarse_even, coarse_odd, *state)


def solution(mesh):
    return jax.shard_map(
        body,
        mesh=mesh,
        in_specs=(
            P("gx", "gy"),
            P("gx", "gy"),
            P(None, "gx", "gy"),
            P(("gx", "gy"), None),
            P(("gx", "gy")),
            P(("gx", "gy")),
        ),
        out_specs=P(None, "gx", "gy"),
        check_vma=False,
    )
```
